32 devices in a mesh: narrow: 4 (over y, core), wide: 8 (over z, x).
Axes of the slice: x: 2, y: 2, z: 4, core: 2. Of those that a mesh axis runs over, the one named last changes fastest.
Arguments:
- tokens: bfloat16 [4, 4, 1024, 384], P('narrow', None, 'wide'), may hold values from -6 to 6
- cotangent: bfloat16 [4, 4, 1024, 384], P('narrow', None, 'wide'), may hold values from -6 to 6
- emb_table: bfloat16 [4, 384], replicated, may hold values from -5 to 5
- ada_weight: bfloat16 [1, 384, 2304], replicated, may hold values from -0.3125 to 0.3125
- ada_bias: bfloat16 [1, 2304], replicated, may hold values from -3 to 3
- qkv_weight: bfloat16 [1, 384, 1152], replicated, may hold values from -0.3125 to 0.3125
- out_weight: bfloat16 [1, 384, 384], replicated, may hold values from -6 to 6
- out_bias: bfloat16 [1, 384], replicated, may hold values from -3 to 3
- up_weight: bfloat16 [1, 384, 1536], replicated, may hold values from -0.3125 to 0.3125
- up_bias: bfloat16 [1, 1536], replicated, may hold values from -3 to 3
- down_weight: bfloat16 [1, 1536, 384], replicated, may hold values from -0.15625 to 0.15625
- down_bias: bfloat16 [1, 384], replicated, may hold values from -3 to 3
- lead_class: int32 [4, 4], replicated, may hold values from 0 to 3
- group_count: int32 [4], replicated, may hold values from 3 to 4, as said below
Outputs:
- output: float32 [4, 4, 1024, 384], P('narrow', None, 'wide')
- grad_tokens: float32 [4, 4, 1024, 384], P('narrow', None, 'wide')
- grad_table: float32 [4, 384], replicated
- grad_ada_weight: float32 [1, 384, 2304], replicated
- grad_ada_bias: float32 [1, 2304], replicated
- grad_qkv_weight: float32 [1, 384, 1152], replicated
- grad_out_weight: float32 [1, 384, 384], replicated
- grad_out_bias: float32 [1, 384], replicated
- grad_up_weight: float32 [1, 384, 1536], replicated
- grad_up_bias: float32 [1, 1536], replicated
- grad_down_weight: float32 [1, 1536, 384], replicated
- grad_down_bias: float32 [1, 384], replicated
The draws below stay inside these ranges and needn't reach their ends.
Inputs may be any that keep to these rules, and one draw needn't show every extreme that they name: `group_count`: half of the groups hold 4 live items and the others 4 - 1; a group's live items fill its first slots.
All inputs are finite; a program needn't handle non-finite values.
Results may differ from the reference program's by a relative error of at most 0.028.
Values may be sent and summed in bfloat16 or wider, within the bound.
A program may use at most 320 MiB of HBM per device.

```python
from functools import partial
import jax
import jax.numpy as jnp
from jax import lax

D = 384
HEADS = 6
HEAD_DIM = 64
FF = 1536
MOD = 2304
CLASSES = 4
SLOTS = 4
LAYERS = 1
PATCHES = 1024
GROUPS = 4


def draw_group_count(key, part):
    key = jax.random.fold_in(key, 11)
    order = jax.random.permutation(key, GROUPS)
    return (SLOTS - order % 2).astype(jnp.int32)


def place_ends(values, own_key, least, high):
    longest = values.shape.index(max(values.shape))
    spots = []
    for shift in (0, 1):
        where = [jax.random.randint(jax.random.fold_in(own_key, axis), (), 0, length) for axis, length in enumerate(values.shape)]
        where[longest] = (where[longest] + shift) % values.shape[longest]
        spots.append(tuple(where))
    return values.at[spots[0]].set(least).at[spots[1]].set(high)


def levels(key, shape, cuts, low, top_value):
    def one(axis_at, blocks):
        steps = jax.random.uniform(jax.random.fold_in(jax.random.fold_in(key, 6), axis_at), (blocks,), jnp.float32, low / len(cuts), top_value / len(cuts))
        return jnp.repeat(jnp.exp(steps), shape[axis_at] // blocks).reshape((-1,) + (1,) * (len(shape) - axis_at - 1))

    gain = one(*cuts[0])
    for cut in cuts[1:]:
        gain = gain * one(*cut)
    return gain


def scatter_about(own_key, dims, width, bound, shards=(), kind=jnp.bfloat16):
    result = width * jax.random.normal(own_key, dims, jnp.float32)
    if shards:
        result = result * levels(own_key, dims, shards, -0.22, 0.18)
    return jnp.clip(result, -bound, bound).astype(kind)


def setup_inputs(seed: int = 0) -> dict:
    keys = jax.random.split(jax.random.key(seed), 15)
    return {
        "tokens": scatter_about(keys[0], (GROUPS, SLOTS, PATCHES, D), 1.0, 6.0, ((0, 4), (2, 8))),
        "cotangent": scatter_about(keys[1], (GROUPS, SLOTS, PATCHES, D), 1.0, 6.0, ((0, 4), (2, 8))),
        "emb_table": scatter_about(keys[2], (CLASSES, D), 1.0, 5.0),
        "ada_weight": scatter_about(keys[3], (LAYERS, D, MOD), D ** -0.5, 0.3125),
        "ada_bias": scatter_about(keys[4], (LAYERS, MOD), 0.5, 3.0),
        "qkv_weight": scatter_about(keys[5], (LAYERS, D, 3 * D), D ** -0.5, 0.3125),
        "out_weight": scatter_about(keys[6], (LAYERS, D, D), 1.0, 6.0),
        "out_bias": scatter_about(keys[7], (LAYERS, D), 0.5, 3.0),
        "up_weight": scatter_about(keys[8], (LAYERS, D, FF), D ** -0.5, 0.3125),
        "up_bias": scatter_about(keys[9], (LAYERS, FF), 0.5, 3.0),
        "down_weight": scatter_about(keys[10], (LAYERS, FF, D), FF ** -0.5, 0.15625),
        "down_bias": scatter_about(keys[11], (LAYERS, D), 0.5, 3.0),
        "lead_class": place_ends(jax.random.randint(keys[12], (GROUPS, SLOTS), 0, CLASSES), jax.random.fold_in(keys[12], 1), 0, CLASSES - 1).astype(jnp.int32),
        "group_count": draw_group_count(jax.random.fold_in(keys[14], 71), 0),
    }


epsilon = 1e-06
highest = lax.Precision.HIGHEST

@jax.custom_vjp
def low(v):
    return lax.optimization_barrier(v.astype(jnp.bfloat16)).astype(jnp.float32)

@jax.custom_vjp
def low_back(v):
    return v

def low_keep(v):
    return (low(v), None)

def low_pass(kept, grad):
    return (grad,)

def back_keep(v):
    return (v, None)

def back_low(kept, grad):
    return (low(grad),)
low.defvjp(low_keep, low_pass)
low_back.defvjp(back_keep, back_low)

def layer_norm(values):
    average = lax.optimization_barrier(jnp.mean(values, axis=-1, keepdims=True))
    centred = values - average
    variance = lax.optimization_barrier(jnp.mean(centred * centred, axis=-1, keepdims=True))
    return centred * lax.rsqrt(variance + epsilon)

def gelu_exact(values):
    return 0.5 * values * (1.0 + jax.scipy.special.erf(values * 0.7071067811865476))

def attend_block(query_block, item_keys, item_values):
    scores = low_back(jnp.einsum('phe,nhe->hpn', query_block, item_keys, precision=highest) * HEAD_DIM ** (-0.5))
    highest_score = lax.optimization_barrier(jnp.max(scores, axis=-1, keepdims=True))
    raised = jnp.exp(scores - highest_score)
    weights = raised / lax.optimization_barrier(jnp.sum(raised, axis=-1, keepdims=True))
    return jnp.einsum('hpn,nhe->phe', low(weights), item_values, precision=highest)

def item_layers(item_tokens, item_mod, qkv_weight, out_weight, out_bias, up_weight, up_bias, down_weight, down_bias):
    hidden = item_tokens
    rows = hidden.shape[0]
    block_rows = min(512, rows)
    for layer in range(LAYERS):
        pieces = item_mod[layer].reshape(6, D)
        modulated = layer_norm(hidden) * (1.0 + pieces[1]) + pieces[0]
        projected = jnp.dot(low(modulated), qkv_weight[layer], precision=highest)
        queries = low(low_back(projected[:, :D])).reshape(rows, HEADS, HEAD_DIM)
        item_keys = low(low_back(projected[:, D:2 * D])).reshape(rows, HEADS, HEAD_DIM)
        item_values = low(low_back(projected[:, 2 * D:])).reshape(rows, HEADS, HEAD_DIM)
        blocks = queries.reshape(rows // block_rows, block_rows, HEADS, HEAD_DIM)
        attended = lax.map(jax.checkpoint(partial(attend_block, item_keys=item_keys, item_values=item_values)), blocks)
        attended = low(low_back(attended.reshape(rows, D)))
        branch = low_back(jnp.dot(attended, out_weight[layer], precision=highest) + out_bias[layer])
        middle = hidden + pieces[2] * branch
        modulated = layer_norm(middle) * (1.0 + pieces[4]) + pieces[3]
        upward = low_back(jnp.dot(low(modulated), up_weight[layer], precision=highest) + up_bias[layer])
        feed = low_back(jnp.dot(low(gelu_exact(upward)), down_weight[layer], precision=highest) + down_bias[layer])
        hidden = middle + pieces[5] * feed
    return hidden

def forward(tokens, emb_table, ada_weight, ada_bias, qkv_weight, out_weight, out_bias, up_weight, up_bias, down_weight, down_bias, lead_class, group_count):
    embedded = emb_table[lead_class]
    activated = embedded * jax.nn.sigmoid(embedded)
    modulation = jnp.einsum('gsd,lde->gsle', activated, ada_weight, precision=highest) + ada_bias[None, None]
    flat_tokens = tokens.reshape(GROUPS * SLOTS, PATCHES, D)
    flat_mod = modulation.reshape(GROUPS * SLOTS, LAYERS, 6 * D)

    def item_step(carry, item):
        return (carry, item_layers(item[0], item[1], qkv_weight, out_weight, out_bias, up_weight, up_bias, down_weight, down_bias))
    unused, outputs = lax.scan(item_step, None, (flat_tokens, flat_mod))
    live = (jnp.arange(SLOTS, dtype=jnp.int32)[None, :] < group_count[:, None]).astype(jnp.float32)
    return outputs.reshape(GROUPS, SLOTS, PATCHES, D) * live[:, :, None, None]

def reference(tokens, cotangent, emb_table, ada_weight, ada_bias, qkv_weight, out_weight, out_bias, up_weight, up_bias, down_weight, down_bias, lead_class, group_count):

    def wrapped(tokens_in, table_in, ada_w, ada_b, qkv_w, out_w, out_b, up_w, up_b, down_w, down_b):
        return forward(tokens_in, table_in, ada_w, ada_b, qkv_w, out_w, out_b, up_w, up_b, down_w, down_b, lead_class, group_count)
    floats = tuple((array.astype(jnp.float32) for array in (tokens, emb_table, ada_weight, ada_bias, qkv_weight, out_weight, out_bias, up_weight, up_bias, down_weight, down_bias)))
    output, pullback = jax.vjp(wrapped, *floats)
    grads = pullback(cotangent.astype(jnp.float32))
    return (output, grads[0], grads[1], grads[2], grads[3], grads[4], grads[5], grads[6], grads[7], grads[8], grads[9], grads[10])
```

```python
import functools
from types import SimpleNamespace

import jax
import jax.numpy as jnp
from jax import lax
from jax.experimental import pallas as pl
from jax.experimental.pallas import tpu as pltpu
from jax.sharding import PartitionSpec as P

MESH = pl.DeviceIdType.MESH
f32, bf16 = jnp.float32, jnp.bfloat16
EPS = 1e-06
ROOT_HALF = 0.7071067811865476
INV_ROOT_2PI = 0.3989422804014327
HEAD_DIM = 64


def dot_nn(a, b):
    return lax.dot_general(a, b, (((1,), (0,)), ((), ())), preferred_element_type=f32)


def dot_nt(a, b):
    return lax.dot_general(a, b, (((1,), (1,)), ((), ())), preferred_element_type=f32)


def dot_tn(a, b):
    return lax.dot_general(a, b, (((0,), (0,)), ((), ())), preferred_element_type=f32)


def norm_rows(x):
    centred = x - jnp.mean(x, axis=-1, keepdims=True)
    inverse = lax.rsqrt(jnp.mean(centred * centred, axis=-1, keepdims=True) + EPS)
    return centred * inverse, inverse


def norm_rows_back(x, n, inverse):
    first = jnp.mean(x, axis=-1, keepdims=True)
    second = jnp.mean(x * n, axis=-1, keepdims=True)
    return inverse * (x - first - n * second)


def col_sum(x):
    return jnp.sum(x, axis=0, keepdims=True)


class Place:
    def __init__(self):
        narrow, wide = lax.axis_index("narrow"), lax.axis_index("wide")
        self.y, self.c = narrow // 2, narrow % 2
        self.z, self.x = wide // 2, wide % 2
        self.wide = wide
        self.low = wide % 4
        self.half = wide // 4
        self.rows_half = 1 - self.c
        self.plane = 2 * self.y + self.x

    def low_xor(self, i):
        a = self.low
        if i & 1:
            a = a + 1 - 2 * (a % 2)
        if i & 2:
            a = a + 2 - 4 * (a // 2)
        return a

    def home(self, i):
        slot = self.low_xor(i)
        return slot, (2 * self.y + 1 - self.half, 4 * self.c + slot)

    def source(self, i):
        strip = self.low_xor(i)
        return strip, (2 * self.y + self.half, 4 * self.rows_half + strip)

    def core(self):
        return (2 * self.y + 1 - self.c, self.wide)

    def in_plane(self, k):
        x = 1 - self.x if k & 1 else self.x
        y = 1 - self.y if k & 2 else self.y
        return 2 * y + x, (2 * y + self.c, 2 * self.z + x)

    def along_z(self, k):
        z = self.z
        if k & 1:
            z = z + 1 - 2 * (z % 2)
        if k & 2:
            z = z + 2 - 4 * (z // 2)
        return z, (2 * self.y + self.c, 2 * z + self.x)


class Wire:
    def __init__(self, send_sems, recv_sems):
        self.send_sems, self.recv_sems = send_sems, recv_sems
        self.count = 0
        self.sent = []

    def copy(self, src, dst, device):
        index = self.count
        self.count += 1
        made = pltpu.make_async_remote_copy(
            src_ref=src,
            dst_ref=dst,
            send_sem=self.send_sems.at[index],
            recv_sem=self.recv_sems.at[index],
            device_id=device,
            device_id_type=MESH,
        )
        made.start()
        self.sent.append(made)
        return made

    def finish(self):
        for made in self.sent:
            made.wait_send()


def main_kernel(sizes, names, *refs):
    r = SimpleNamespace(**dict(zip(names, refs, strict=True)))
    R, D, FF = sizes
    M, N = 4 * R, 8 * R
    MB = M // 2
    pairs = D // 128
    here = Place()
    wire = Wire(r.send_sems, r.recv_sems)
    local_sems = r.local_sems
    local_count = [0]

    def local(src, dst):
        made = pltpu.make_async_copy(src, dst, local_sems.at[local_count[0]])
        local_count[0] += 1
        made.start()
        return made

    load_ada = local(r.ada_weight.at[0], r.ada_weight_v)
    load_qkv = local(r.qkv_weight.at[0], r.qkv_weight_v)
    load_rest = [
        local(r.out_weight.at[0], r.out_weight_v),
        local(r.up_weight.at[0], r.up_weight_v),
        local(r.down_weight.at[0], r.down_weight_v),
    ]

    barrier = pltpu.get_barrier_semaphore()
    partners = [here.core()]
    partners += [here.home(i)[1] for i in range(4)] + [here.source(i)[1] for i in range(4)]
    partners += [here.in_plane(k)[1] for k in (1, 2, 3)] + [here.along_z(k)[1] for k in (1, 2, 3)]
    for device in partners:
        pl.semaphore_signal(barrier, inc=1, device_id=device, device_id_type=MESH)
    pl.semaphore_wait(barrier, len(partners))

    def send_home(whole, landing):
        place = pl.ds(pl.multiple_of(here.low * R, R), R)
        made = []
        for i in range(4):
            slot, device = here.home(i)
            made.append(wire.copy(whole.at[0, slot], landing.at[place, :], device))
        return made

    tokens_in = send_home(r.tokens, r.tokens_v)
    cotangent_in = send_home(r.cotangent, r.cotangent_v)

    group, slot = 2 * here.y + here.half, here.low
    item_class = r.lead_class[group, slot]
    live = (slot < r.group_count[group]).astype(f32)
    table = r.emb_table[...].astype(f32)
    class_col = lax.broadcasted_iota(jnp.int32, (table.shape[0], 1), 0)
    onehot = (class_col == item_class).astype(f32)
    embed = jnp.sum(onehot * table, axis=0, keepdims=True)
    silu = embed * (1.0 / (1.0 + jnp.exp(-embed)))
    high = silu.astype(bf16).astype(f32)
    middle_part = (silu - high).astype(bf16).astype(f32)
    low_part = silu - high - middle_part
    row = lax.broadcasted_iota(jnp.int32, (16, D), 0)
    parts = jnp.where(row == 0, high, jnp.where(row == 1, middle_part, jnp.where(row == 2, low_part, 0.0)))
    load_ada.wait()
    mods = r.mods
    for k in range(6):
        cols = pl.ds(k * D, D)
        mods[k : k + 1, :] = col_sum(
            dot_nn(parts.astype(bf16), r.ada_weight_v[:, cols])
        ) + r.ada_bias[:, cols].astype(f32)

    def mod(k):
        return mods[k : k + 1, :]

    acc = r.acc
    acc[...] = jnp.zeros_like(acc)

    load_qkv.wait()
    lane = lax.broadcasted_iota(jnp.int32, (R, 128), 1)
    left = lane < HEAD_DIM
    kv, qst = r.kv, r.qst
    kv_copies = []
    own = pl.multiple_of(here.rows_half * M, M)
    for i in range(4):
        strip, _ = here.source(i)
        tokens_in[i].wait_recv()
        at = pl.multiple_of(strip * R, R)
        rows = pl.ds(at, R)
        normed, inverse = norm_rows(r.tokens_v[rows, :].astype(f32))
        r.normed[rows, :] = normed
        r.inverse[rows, :] = inverse
        modulated = (normed * (1.0 + mod(1)) + mod(0)).astype(bf16)
        r.modulated[rows, :] = modulated
        projected = dot_nn(modulated, r.qkv_weight_v[...])
        kv_rows = pl.ds(pl.multiple_of(own + at, R), R)
        kv[kv_rows, :] = projected[:, D:].astype(bf16)
        kv_copies.append(wire.copy(kv.at[kv_rows, :], kv.at[kv_rows, :], here.core()))
        for p in range(pairs):
            q = projected[:, p * 128 : (p + 1) * 128].astype(bf16) * HEAD_DIM ** (-0.5)
            zero = jnp.zeros_like(q)
            qst[p, pl.ds(at, R), :] = jnp.where(left, q, zero)
            qst[p, pl.ds(pl.multiple_of(M + at, R), R), :] = jnp.where(left, zero, q)
    for made in kv_copies:
        made.wait_recv()

    kvt, es, ots = r.kvt, r.es, r.ots
    for b in range(2 * pairs):
        kvt[b * 128 : (b + 1) * 128, :] = kv[:, b * 128 : (b + 1) * 128].T
    QB = M // 2

    def forward_block(j, carry):
        p, qb = j // 4, j % 4
        cols = pl.ds(pl.multiple_of(p * 128, 128), 128)
        queries = pl.ds(pl.multiple_of(qb * QB, QB), QB)
        scores = dot_nt(kv[:, cols], qst[p, queries, :])
        top = jnp.max(scores, axis=0, keepdims=True)
        raised = jnp.exp(scores - top)
        inv = 1.0 / col_sum(raised)
        raised = raised.astype(bf16)
        es[p, :, queries] = raised
        r.inv_sum[j] = inv
        head = pl.multiple_of(p * 128 + (qb // 2) * HEAD_DIM, HEAD_DIM)
        mixed = dot_nn(kvt[pl.ds(pl.multiple_of(D + head, HEAD_DIM), HEAD_DIM), :], raised) * inv
        ots[pl.ds(head, HEAD_DIM), pl.ds(pl.multiple_of((qb % 2) * QB, QB), QB)] = mixed
        return carry

    lax.fori_loop(0, 4 * pairs, forward_block, 0)
    att = r.att
    for p in range(pairs):
        att[:, p * 128 : (p + 1) * 128] = ots[p * 128 : (p + 1) * 128, :].T.astype(bf16)

    for made in load_rest:
        made.wait()
    for made in cotangent_in:
        made.wait_recv()
    outw, upw, downw = r.out_weight_v, r.up_weight_v, r.down_weight_v
    chunks = FF // D

    def feed_block(t, carry):
        rows = pl.ds(pl.multiple_of(t * MB, MB), MB)
        branch = dot_nn(att[rows, :], outw[...]) + r.out_bias[...].astype(f32)
        middle = r.tokens_v[rows, :].astype(f32) + mod(2) * branch
        n, inverse = norm_rows(middle)
        modulated = (n * (1.0 + mod(4)) + mod(3)).astype(bf16)
        r.modulated_m[rows, :] = modulated

        def up_chunk(ck, inner):
            cols = pl.ds(pl.multiple_of(ck * D, D), D)
            u = dot_nn(modulated, upw[:, cols]) + r.up_bias[:, cols].astype(f32)
            phi = 0.5 * (1.0 + lax.erf(u * ROOT_HALF))
            r.activated[rows, cols] = (u * phi).astype(bf16)
            r.slope[:, cols] = phi + u * (INV_ROOT_2PI * jnp.exp(-0.5 * u * u))
            return inner

        lax.fori_loop(0, chunks, up_chunk, 0)
        feed = dot_nn(r.activated[rows, :], downw[...]) + r.down_bias[...].astype(f32)
        r.out_stage[rows, :] = ((middle + mod(5) * feed) * live).astype(bf16)
        grad = r.cotangent_v[rows, :].astype(f32) * live
        grad_feed = (grad * mod(5)).astype(bf16)
        r.grad_feed[rows, :] = grad_feed
        acc[5:6, :] += col_sum(grad * feed)
        acc[8:9, :] += col_sum(grad_feed.astype(f32))

        def down_chunk(ck, inner):
            cols = pl.ds(pl.multiple_of(ck * D, D), D)
            grad_up = (dot_nt(grad_feed, downw[cols, :]) * r.slope[:, cols]).astype(bf16)
            r.grad_up[rows, cols] = grad_up
            acc[pl.ds(9 + ck, 1), :] += col_sum(grad_up.astype(f32))
            return inner

        lax.fori_loop(0, chunks, down_chunk, 0)
        back = dot_nt(r.grad_up[rows, :], upw[...])
        acc[3:4, :] += col_sum(back)
        acc[4:5, :] += col_sum(back * n)
        grad_middle = grad + norm_rows_back(back * (1.0 + mod(4)), n, inverse)
        r.grad_middle[rows, :] = grad_middle
        acc[2:3, :] += col_sum(grad_middle * branch)
        grad_branch = (grad_middle * mod(2)).astype(bf16)
        r.grad_branch[rows, :] = grad_branch
        acc[13:14, :] += col_sum(grad_branch.astype(f32))
        r.grad_att[rows, :] = dot_nt(grad_branch, outw[...]).astype(bf16)
        return carry

    lax.fori_loop(0, 2, feed_block, 0)

    def send_back(stage, landing):
        made = []
        for i in range(4):
            strip, device = here.source(i)
            rows = pl.ds(pl.multiple_of(strip * R, R), R)
            made.append(wire.copy(stage.at[rows, :], landing.at[here.low], device))
        return made

    out_copies = send_back(r.out_stage, r.out_o)

    part, total = r.part, r.total
    piece_rows = 4 * D
    core_rows, plane_rows, z_rows = piece_rows // 2, piece_rows // 8, piece_rows // 32
    by_core, by_plane, by_z, by_z_back, by_plane_back, by_core_back = {}, {}, {}, {}, {}, {}

    def piece_core(i):
        base = i * piece_rows
        src = part.at[pl.ds(pl.multiple_of(base + core_rows * (1 - here.c), core_rows), core_rows), :]
        by_core[i] = [wire.copy(src, r.land_core.at[i], here.core())]

    def own_core(i):
        return pl.multiple_of(i * piece_rows + core_rows * here.c, core_rows)

    def piece_plane(i):
        for made in by_core[i]:
            made.wait_recv()

        def add(q, carry):
            rows = pl.ds(pl.multiple_of(q * plane_rows, plane_rows), plane_rows)
            mine = pl.ds(pl.multiple_of(own_core(i) + q * plane_rows, plane_rows), plane_rows)
            r.sum_core[i, rows, :] = (
                part[mine, :].astype(f32) + r.land_core[i, rows, :].astype(f32)
            ).astype(bf16)
            return carry

        lax.fori_loop(0, 4, add, 0)
        by_plane[i] = []
        for k in (3, 1, 2):
            q, device = here.in_plane(k)
            rows = pl.ds(pl.multiple_of(q * plane_rows, plane_rows), plane_rows)
            by_plane[i].append(
                wire.copy(r.sum_core.at[i, rows, :], r.land_plane.at[i, k - 1], device)
            )

    def piece_z(i):
        for made in by_plane[i]:
            made.wait_recv()
        rows = pl.ds(pl.multiple_of(here.plane * plane_rows, plane_rows), plane_rows)
        summed = r.sum_core[i, rows, :].astype(f32)
        for k in range(3):
            summed = summed + r.land_plane[i, k].astype(f32)
        r.sum_plane[i] = summed.astype(bf16)
        by_z[i] = []
        for k in (3, 2, 1):
            z, device = here.along_z(k)
            rows = pl.ds(pl.multiple_of(z * z_rows, z_rows), z_rows)
            by_z[i].append(
                wire.copy(r.sum_plane.at[i, rows, :], r.land_z.at[i, k - 1], device)
            )

    def own_plane(i):
        return pl.multiple_of(own_core(i) + here.plane * plane_rows, plane_rows)

    def piece_z_back(i):
        for made in by_z[i]:
            made.wait_recv()
        rows = pl.ds(pl.multiple_of(here.z * z_rows, z_rows), z_rows)
        summed = r.sum_plane[i, rows, :].astype(f32)
        for k in range(3):
            summed = summed + r.land_z[i, k].astype(f32)
        mine = pl.ds(pl.multiple_of(own_plane(i) + here.z * z_rows, z_rows), z_rows)
        total[mine, :] = summed.astype(bf16)
        by_z_back[i] = [
            wire.copy(total.at[mine, :], total.at[mine, :], here.along_z(k)[1]) for k in (3, 2, 1)
        ]

    def piece_plane_back(i):
        for made in by_z_back[i]:
            made.wait_recv()
        mine = pl.ds(own_plane(i), plane_rows)
        by_plane_back[i] = [
            wire.copy(total.at[mine, :], total.at[mine, :], here.in_plane(k)[1]) for k in (3, 1, 2)
        ]

    def piece_core_back(i):
        for made in by_plane_back[i]:
            made.wait_recv()
        mine = pl.ds(own_core(i), core_rows)
        by_core_back[i] = [wire.copy(total.at[mine, :], total.at[mine, :], here.core())]

    stored = []

    def piece_store(i):
        for made in by_core_back[i]:
            made.wait_recv()
        rows = pl.ds(i * piece_rows, piece_rows)
        stored.append(local(total.at[rows, :], r.grads_o.at[rows, :]))

    def down_grad(ck, carry):
        cols = pl.ds(pl.multiple_of(ck * D, D), D)
        part[cols, :] = dot_tn(r.activated[:, cols], r.grad_feed[...]).astype(bf16)
        return carry

    lax.fori_loop(0, chunks, down_grad, 0)
    piece_core(0)

    def up_grad(ck, carry):
        cols = pl.ds(pl.multiple_of(ck * D, D), D)
        rows = pl.ds(pl.multiple_of(FF + ck * D, D), D)
        part[rows, :] = dot_tn(r.modulated_m[...], r.grad_up[:, cols]).astype(bf16)
        return carry

    lax.fori_loop(0, chunks, up_grad, 0)
    piece_core(1)
    piece_plane(0)
    part[2 * FF : 2 * FF + D, :] = dot_tn(att[...], r.grad_branch[...]).astype(bf16)

    gat, qgt = r.gat, r.qgt
    for p in range(pairs):
        gat[p * 128 : (p + 1) * 128, :] = r.grad_att[:, p * 128 : (p + 1) * 128].T.astype(f32)
    zero_half = jnp.zeros((HEAD_DIM, QB), bf16)
    gst, gstt, deltas, dss = r.gst, r.gstt, r.deltas, r.dss
    dkv = r.dkv
    dkv_copies = []
    other = pl.multiple_of((1 - here.rows_half) * M, M)
    for p in range(pairs):
        for qb in range(4):
            half = qb // 2
            head = p * 128 + half * HEAD_DIM
            queries = slice((qb % 2) * QB, (qb % 2) * QB + QB)
            inv = r.inv_sum[4 * p + qb]
            scaled = gat[head : head + HEAD_DIM, queries] * inv
            deltas[qb] = col_sum(scaled * ots[head : head + HEAD_DIM, queries])
            scaled = scaled.astype(bf16)
            filled = [scaled, zero_half] if half == 0 else [zero_half, scaled]
            gstt[:, qb * QB : (qb + 1) * QB] = jnp.concatenate(filled, axis=0)
        gst[...] = gstt[...].T

        def backward_block(qb, carry, p=p):
            queries = pl.ds(pl.multiple_of(qb * QB, QB), QB)
            slope = dot_nn(kv[:, D + p * 128 : D + (p + 1) * 128], gstt[:, queries])
            grad_scores = (es[p, :, queries].astype(f32) * (slope - deltas[qb])).astype(bf16)
            dss[:, queries] = grad_scores
            head = pl.multiple_of(p * 128 + (qb // 2) * HEAD_DIM, HEAD_DIM)
            grad_q = dot_nn(kvt[pl.ds(head, HEAD_DIM), :], grad_scores) * HEAD_DIM ** (-0.5)
            qgt[pl.ds(head, HEAD_DIM), pl.ds(pl.multiple_of((qb % 2) * QB, QB), QB)] = grad_q
            return carry

        lax.fori_loop(0, 4, backward_block, 0)
        dkv[p, :, 0:128] = dot_nn(dss[...], qst[p]).astype(bf16)
        dkv[p, :, 128:256] = dot_nn(es[p], gst[...]).astype(bf16)
        dkv_copies.append(wire.copy(dkv.at[p, pl.ds(other, M), :], r.land_dkv.at[p], here.core()))
        if p == 0:
            piece_plane(1)
            piece_z(0)
        if p == 1:
            piece_z(1)
            piece_z_back(0)
    gp = r.grad_projected
    for p in range(pairs):
        cols = slice(p * 128, (p + 1) * 128)
        gp[:, cols] = qgt[cols, :].T.astype(bf16)
        dkv_copies[p].wait_recv()
        summed = dkv[p, pl.ds(own, M), :].astype(f32) + r.land_dkv[p].astype(f32)
        gp[:, D + p * 128 : D + (p + 1) * 128] = summed[:, :128].astype(bf16)
        gp[:, 2 * D + p * 128 : 2 * D + (p + 1) * 128] = summed[:, 128:].astype(bf16)

    for b in range(3):
        cols = slice(b * D, (b + 1) * D)
        rows = slice(2 * FF + (b + 1) * D, 2 * FF + (b + 2) * D)
        part[rows, :] = dot_tn(r.modulated[...], gp[:, cols]).astype(bf16)
    piece_core(2)

    def token_block(t, carry):
        rows = pl.ds(pl.multiple_of(t * MB, MB), MB)
        back = dot_nt(gp[rows, :], r.qkv_weight_v[...])
        n = r.normed[rows, :]
        acc[0:1, :] += col_sum(back)
        acc[1:2, :] += col_sum(back * n)
        grad = r.grad_middle[rows, :] + norm_rows_back(
            back * (1.0 + mod(1)), n, r.inverse[rows, :]
        )
        r.gtok_stage[rows, :] = grad.astype(bf16)
        return carry

    lax.fori_loop(0, 2, token_block, 0)
    piece_plane(2)
    gtok_copies = send_back(r.gtok_stage, r.gtok_o)

    small = r.small
    for k in range(6):
        small[4 * k : 4 * k + 4, :] = onehot * acc[k : k + 1, :]
    small[24:32, :] = acc[8:16, :]
    rows_here = pl.ds(pl.multiple_of(16 * here.c, 16), 16)
    rows_there = pl.ds(pl.multiple_of(16 * (1 - here.c), 16), 16)
    flight = wire.copy(small.at[rows_there, :], r.land_small.at[0], here.core())
    flight.wait_recv()
    r.small_a[...] = small[rows_here, :] + r.land_small[0]
    flight = [
        wire.copy(r.small_a, r.land_small.at[k], here.in_plane(k)[1]) for k in (3, 1, 2)
    ]
    piece_z_back(1)
    for made in flight:
        made.wait_recv()
    r.small_b[...] = (
        r.small_a[...] + r.land_small[1] + r.land_small[2] + r.land_small[3]
    )
    flight = [
        wire.copy(r.small_b, r.land_small.at[3 + k], here.along_z(k)[1]) for k in (3, 2, 1)
    ]
    piece_plane_back(0)
    piece_z(2)
    piece_plane_back(1)
    for made in flight:
        made.wait_recv()
    small_sum = r.small_sum
    small_sum[rows_here, :] = (
        r.small_b[...] + r.land_small[4] + r.land_small[5] + r.land_small[6]
    )
    flight = wire.copy(small_sum.at[rows_here, :], small_sum.at[rows_here, :], here.core())
    piece_core_back(0)
    piece_z_back(2)
    piece_core_back(1)
    flight.wait_recv()
    stored.append(local(small_sum, r.small_o))
    piece_store(0)
    piece_plane_back(2)
    piece_store(1)
    piece_core_back(2)
    piece_store(2)
    for made in out_copies + gtok_copies:
        made.wait_recv()
    wire.finish()
    for made in stored:
        made.wait()


def last_kernel(sizes, names, *refs):
    r = SimpleNamespace(**dict(zip(names, refs, strict=True)))
    D, FF = sizes
    sems = r.sems
    count = [0]

    def local(src, dst):
        made = pltpu.make_async_copy(src, dst, sems.at[count[0]])
        count[0] += 1
        made.start()
        return made

    small_in = local(r.small_i, r.small_i_v)
    ada_in = local(r.ada_weight, r.ada_weight_v)
    out_in = local(r.out_i, r.out_i_v)
    gtok_in = local(r.gtok_i, r.gtok_i_v)
    grads_in = []
    for b in range(3):
        rows = pl.ds(b * 4 * D, 4 * D)
        grads_in.append(local(r.grads_i.at[rows, :], r.grads_v.at[rows, :]))
    outs = []
    small_in.wait()
    small = r.small_i_v
    table = r.emb_table[...].astype(f32)
    sigmoid = 1.0 / (1.0 + jnp.exp(-table))
    silu = table * sigmoid

    def split(v):
        high = v.astype(bf16).astype(f32)
        return high, v - high

    silu_high, silu_low = split(silu)
    zero = jnp.zeros_like(silu)
    left = jnp.concatenate([silu_high, silu_low, silu_high, zero], axis=0).astype(bf16)
    grad_silu = jnp.zeros_like(table)
    ada_in.wait()
    for k in range(6):
        cols = slice(k * D, (k + 1) * D)
        block = small[4 * k : 4 * k + 4, :]
        high, low = split(block)
        right = jnp.concatenate([high, high, low, zero], axis=0).astype(bf16)
        r.gada_v[:, cols] = dot_tn(left, right)
        r.gada_b[:, cols] = col_sum(block)
        both = jnp.concatenate([high, low, zero, zero], axis=0).astype(bf16)
        found = dot_nt(both, r.ada_weight_v[0, :, cols])
        grad_silu = grad_silu + found[0:4, :] + found[4:8, :]
    outs.append(local(r.gada_v, r.gada.at[0]))
    r.table_o[...] = grad_silu * (sigmoid + table * sigmoid * (1.0 - sigmoid))
    r.down_b[...] = small[24:25, :]
    for k in range(FF // D):
        r.up_b[:, k * D : (k + 1) * D] = small[25 + k : 26 + k, :]
    r.out_b[...] = small[29:30, :]
    for arrived, given, wide_v, result in (
        (out_in, r.out_i_v, r.out_v, r.out),
        (gtok_in, r.gtok_i_v, r.gtok_v, r.gtok),
    ):
        arrived.wait()
        for s in range(4):
            wide_v[s] = given[s].astype(f32)
        outs.append(local(wide_v, result.at[0]))
    grads = r.grads_v
    grads_in[0].wait()
    for k in range(FF // D):
        r.gdown_v[k * D : (k + 1) * D, :] = grads[k * D : (k + 1) * D, :].astype(f32)
    outs.append(local(r.gdown_v, r.gdown.at[0]))
    grads_in[1].wait()
    for k in range(FF // D):
        r.gup_v[:, k * D : (k + 1) * D] = grads[FF + k * D : FF + (k + 1) * D, :].astype(f32)
    outs.append(local(r.gup_v, r.gup.at[0]))
    grads_in[2].wait()
    r.gout_v[...] = grads[2 * FF : 2 * FF + D, :].astype(f32)
    outs.append(local(r.gout_v, r.gout.at[0]))
    for k in range(3):
        rows = slice(2 * FF + (k + 1) * D, 2 * FF + (k + 2) * D)
        r.gqkv_v[:, k * D : (k + 1) * D] = grads[rows, :].astype(f32)
    outs.append(local(r.gqkv_v, r.gqkv.at[0]))
    for made in outs:
        made.wait()


def fast_body(*args):
    tokens, emb_table, ada_weight, up_weight = args[0], args[2], args[3], args[8]
    R, D = tokens.shape[2:]
    FF = up_weight.shape[2]
    M, N = 4 * R, 8 * R
    pairs = D // 128
    total_rows = 2 * FF + 4 * D
    vmem = pl.BlockSpec(memory_space=pltpu.VMEM)
    smem = pl.BlockSpec(memory_space=pltpu.SMEM)
    anywhere = pl.BlockSpec(memory_space=pl.ANY)
    arguments = dict(
        tokens=anywhere,
        cotangent=anywhere,
        emb_table=vmem,
        ada_weight=anywhere,
        ada_bias=vmem,
        qkv_weight=anywhere,
        out_weight=anywhere,
        out_bias=vmem,
        up_weight=anywhere,
        up_bias=vmem,
        down_weight=anywhere,
        down_bias=vmem,
        lead_class=smem,
        group_count=smem,
    )
    piece = 4 * D
    scratch = dict(
        ada_weight_v=pltpu.VMEM((D, 6 * D), bf16),
        qkv_weight_v=pltpu.VMEM((D, 3 * D), bf16),
        out_weight_v=pltpu.VMEM((D, D), bf16),
        up_weight_v=pltpu.VMEM((D, FF), bf16),
        down_weight_v=pltpu.VMEM((FF, D), bf16),
        tokens_v=pltpu.VMEM((M, D), bf16),
        cotangent_v=pltpu.VMEM((M, D), bf16),
        mods=pltpu.VMEM((8, D), f32),
        acc=pltpu.VMEM((16, D), f32),
        normed=pltpu.VMEM((M, D), f32),
        inverse=pltpu.VMEM((M, 1), f32),
        modulated=pltpu.VMEM((M, D), bf16),
        kv=pltpu.VMEM((N, 2 * D), bf16),
        kvt=pltpu.VMEM((2 * D, N), bf16),
        qst=pltpu.VMEM((pairs, 2 * M, 128), bf16),
        es=pltpu.VMEM((pairs, N, 2 * M), bf16),
        inv_sum=pltpu.VMEM((4 * pairs, 1, M // 2), f32),
        ots=pltpu.VMEM((D, M), f32),
        att=pltpu.VMEM((M, D), bf16),
        modulated_m=pltpu.VMEM((M, D), bf16),
        activated=pltpu.VMEM((M, FF), bf16),
        slope=pltpu.VMEM((M // 2, FF), f32),
        out_stage=pltpu.VMEM((M, D), bf16),
        grad_feed=pltpu.VMEM((M, D), bf16),
        grad_up=pltpu.VMEM((M, FF), bf16),
        grad_middle=pltpu.VMEM((M, D), f32),
        grad_branch=pltpu.VMEM((M, D), bf16),
        grad_att=pltpu.VMEM((M, D), bf16),
        gat=pltpu.VMEM((D, M), f32),
        qgt=pltpu.VMEM((D, M), f32),
        gst=pltpu.VMEM((2 * M, 128), bf16),
        gstt=pltpu.VMEM((128, 2 * M), bf16),
        deltas=pltpu.VMEM((4, 1, M // 2), f32),
        dss=pltpu.VMEM((N, 2 * M), bf16),
        dkv=pltpu.VMEM((pairs, N, 256), bf16),
        land_dkv=pltpu.VMEM((pairs, M, 256), bf16),
        grad_projected=pltpu.VMEM((M, 3 * D), bf16),
        gtok_stage=pltpu.VMEM((M, D), bf16),
        part=pltpu.VMEM((total_rows, D), bf16),
        total=pltpu.VMEM((total_rows, D), bf16),
        land_core=pltpu.VMEM((3, piece // 2, D), bf16),
        sum_core=pltpu.VMEM((3, piece // 2, D), bf16),
        land_plane=pltpu.VMEM((3, 3, piece // 8, D), bf16),
        sum_plane=pltpu.VMEM((3, piece // 8, D), bf16),
        land_z=pltpu.VMEM((3, 3, piece // 32, D), bf16),
        small=pltpu.VMEM((32, D), f32),
        small_a=pltpu.VMEM((16, D), f32),
        small_b=pltpu.VMEM((16, D), f32),
        small_sum=pltpu.VMEM((32, D), f32),
        land_small=pltpu.VMEM((7, 16, D), f32),
        send_sems=pltpu.SemaphoreType.DMA((80,)),
        recv_sems=pltpu.SemaphoreType.DMA((80,)),
        local_sems=pltpu.SemaphoreType.DMA((12,)),
    )
    mids = dict(
        out_o=jax.ShapeDtypeStruct((4, R, D), bf16),
        gtok_o=jax.ShapeDtypeStruct((4, R, D), bf16),
        grads_o=jax.ShapeDtypeStruct((total_rows, D), bf16),
        small_o=jax.ShapeDtypeStruct((32, D), f32),
    )
    names = tuple(arguments) + tuple(mids) + tuple(scratch)
    middle = pl.pallas_call(
        functools.partial(main_kernel, (R, D, FF), names),
        out_shape=tuple(mids.values()),
        in_specs=list(arguments.values()),
        out_specs=(anywhere,) * 4,
        scratch_shapes=list(scratch.values()),
        compiler_params=pltpu.CompilerParams(
            collective_id=0, has_side_effects=True, vmem_limit_bytes=60 << 20
        ),
        name="block_forward_backward",
    )(*args)
    outs = dict(
        out=((1, 4, R, D), anywhere),
        gtok=((1, 4, R, D), anywhere),
        table_o=((emb_table.shape[0], D), vmem),
        gada=((1, D, 6 * D), anywhere),
        gada_b=((1, 6 * D), vmem),
        gqkv=((1, D, 3 * D), anywhere),
        gout=((1, D, D), anywhere),
        out_b=((1, D), vmem),
        gup=((1, D, FF), anywhere),
        up_b=((1, FF), vmem),
        gdown=((1, FF, D), anywhere),
        down_b=((1, D), vmem),
    )
    ins = dict(
        out_i=anywhere,
        gtok_i=anywhere,
        grads_i=anywhere,
        small_i=anywhere,
        emb_table=vmem,
        ada_weight=anywhere,
    )
    scratch = dict(
        out_i_v=pltpu.VMEM((4, R, D), bf16),
        gtok_i_v=pltpu.VMEM((4, R, D), bf16),
        grads_v=pltpu.VMEM((total_rows, D), bf16),
        small_i_v=pltpu.VMEM((32, D), f32),
        ada_weight_v=pltpu.VMEM((1, D, 6 * D), bf16),
        out_v=pltpu.VMEM((4, R, D), f32),
        gtok_v=pltpu.VMEM((4, R, D), f32),
        gada_v=pltpu.VMEM((D, 6 * D), f32),
        gqkv_v=pltpu.VMEM((D, 3 * D), f32),
        gout_v=pltpu.VMEM((D, D), f32),
        gup_v=pltpu.VMEM((D, FF), f32),
        gdown_v=pltpu.VMEM((FF, D), f32),
        sems=pltpu.SemaphoreType.DMA((16,)),
    )
    names = tuple(ins) + tuple(outs) + tuple(scratch)
    return pl.pallas_call(
        functools.partial(last_kernel, (D, FF), names),
        out_shape=tuple(jax.ShapeDtypeStruct(size, f32) for size, _ in outs.values()),
        in_specs=list(ins.values()),
        out_specs=tuple(space for _, space in outs.values()),
        scratch_shapes=list(scratch.values()),
        compiler_params=pltpu.CompilerParams(vmem_limit_bytes=60 << 20),
        name="widen_and_embed",
    )(*middle, emb_table, ada_weight)


HEADS = 6
LAYERS = 1

epsilon = 1e-06
highest = lax.Precision.HIGHEST
root_half = 0.7071067811865476
inverse_root_two_pi = 0.3989422804014327


def layer_norm(values):
    average = jnp.mean(values, axis=-1, keepdims=True)
    centred = values - average
    variance = jnp.mean(centred * centred, axis=-1, keepdims=True)
    inverse = lax.rsqrt(variance + epsilon)
    return (centred * inverse, inverse)


def norm_back(grad_normed, normed, inverse):
    first = jnp.mean(grad_normed, axis=-1, keepdims=True)
    second = jnp.mean(grad_normed * normed, axis=-1, keepdims=True)
    return inverse * (grad_normed - first - normed * second)


def gelu_exact(values):
    return 0.5 * values * (1.0 + jax.scipy.special.erf(values * root_half))


def gelu_slope(values):
    return 0.5 * (
        1.0 + jax.scipy.special.erf(values * root_half)
    ) + values * inverse_root_two_pi * jnp.exp(-0.5 * values * values)


def split_heads(values):
    return values.reshape(values.shape[0], values.shape[1], HEADS, values.shape[2] // HEADS)


def modulation_parts(silu_rows, ada_w, ada_b):
    mods = jnp.dot(silu_rows, ada_w.astype(jnp.float32), precision=highest) + ada_b.astype(
        jnp.float32
    )
    mods = mods.reshape(mods.shape[0], 6, -1)
    return [mods[:, index][:, None, :] for index in range(6)]


def before_attention(hidden, parts, qkv_low):
    normed, inverse = layer_norm(hidden)
    modulated = (normed * (1.0 + parts[1]) + parts[0]).astype(jnp.bfloat16)
    projected = jnp.einsum(
        "spd,df->spf", modulated, qkv_low, preferred_element_type=jnp.float32
    ).astype(jnp.bfloat16)
    width = hidden.shape[2]
    return (
        normed,
        inverse,
        modulated,
        projected[..., :width],
        projected[..., width : 2 * width],
        projected[..., 2 * width :],
    )


def after_attention(hidden, attended, parts, later):
    out_w, out_b, up_w, up_b, down_w, down_b = later
    branch = jnp.einsum(
        "spd,de->spe", attended, out_w, preferred_element_type=jnp.float32
    ) + out_b.astype(jnp.float32)
    middle = hidden + parts[2] * branch
    normed, inverse = layer_norm(middle)
    modulated = (normed * (1.0 + parts[4]) + parts[3]).astype(jnp.bfloat16)
    upward = jnp.einsum(
        "spd,df->spf", modulated, up_w, preferred_element_type=jnp.float32
    ) + up_b.astype(jnp.float32)
    activated = gelu_exact(upward).astype(jnp.bfloat16)
    feed = jnp.einsum(
        "spf,fd->spd", activated, down_w, preferred_element_type=jnp.float32
    ) + down_b.astype(jnp.float32)
    return (
        middle + parts[5] * feed,
        (branch, middle, normed, inverse, modulated, upward, activated, feed),
    )


def attention_forward(queries, keys_here, values_here):
    slots, rows, width = queries.shape
    scale = HEAD_DIM ** (-0.5)
    query_heads = split_heads(queries)
    running_max = jnp.full((slots, rows, HEADS), -1e30, jnp.float32)
    key_heads = split_heads(lax.all_gather(keys_here, "wide", axis=1, tiled=True))
    value_heads = split_heads(lax.all_gather(values_here, "wide", axis=1, tiled=True))
    scores = (
        jnp.einsum("sphe,snhe->sphn", query_heads, key_heads, preferred_element_type=jnp.float32)
        * scale
    )
    new_max = jnp.maximum(running_max, jnp.max(scores, axis=-1))
    weights = jnp.exp(scores - new_max[..., None])
    new_sum = jnp.sum(weights, axis=-1)
    mixed = jnp.einsum(
        "sphn,snhe->sphe",
        weights.astype(jnp.bfloat16),
        value_heads,
        preferred_element_type=jnp.float32,
    )
    total = mixed
    running_max, running_sum, total = (new_max, new_sum, total.reshape(slots, rows, width))
    attended = (
        (split_heads(total) / running_sum[..., None])
        .reshape(slots, rows, width)
        .astype(jnp.bfloat16)
    )
    return (attended, running_max + jnp.log(running_sum), None)


def attention_backward(queries, keys_here, values_here, grad_attended, log_total, delta):
    slots, rows, width = queries.shape
    scale = HEAD_DIM ** (-0.5)
    query_heads = split_heads(queries)
    grad_heads = split_heads(grad_attended)
    piece = (
        lax.all_gather(keys_here, "wide", axis=1, tiled=True),
        lax.all_gather(values_here, "wide", axis=1, tiled=True),
    )
    toward_key_heads = split_heads(piece[0])
    toward_value_heads = split_heads(piece[1])
    scores = (
        jnp.einsum(
            "sphe,snhe->sphn", query_heads, toward_key_heads, preferred_element_type=jnp.float32
        )
        * scale
    )
    probs = jnp.exp(scores - log_total[..., None])
    slope = jnp.einsum(
        "sphe,snhe->sphn", grad_heads, toward_value_heads, preferred_element_type=jnp.float32
    )
    grad_scores = (probs * (slope - delta[..., None])).astype(jnp.bfloat16)
    grad_queries = (
        jnp.einsum(
            "sphn,snhe->sphe", grad_scores, toward_key_heads, preferred_element_type=jnp.float32
        )
        * scale
    ).reshape(slots, rows, width)
    stats = (
        lax.all_gather(log_total, "wide", axis=1, tiled=True),
        lax.all_gather(delta, "wide", axis=1, tiled=True),
    )
    key_heads = split_heads(keys_here)
    value_heads = split_heads(values_here)
    piece = (
        lax.all_gather(queries, "wide", axis=1, tiled=True),
        lax.all_gather(grad_attended, "wide", axis=1, tiled=True),
    )
    piece_queries = split_heads(piece[0])
    piece_grads = split_heads(piece[1])
    piece_total = stats[0]
    piece_delta = stats[1]
    scores = (
        jnp.einsum("snhe,sphe->snhp", piece_queries, key_heads, preferred_element_type=jnp.float32)
        * scale
    )
    probs = jnp.exp(scores - piece_total[..., None])
    slope = jnp.einsum(
        "snhe,sphe->snhp", piece_grads, value_heads, preferred_element_type=jnp.float32
    )
    grad_scores = (probs * (slope - piece_delta[..., None])).astype(jnp.bfloat16)
    keys_total = (
        jnp.einsum(
            "snhp,snhe->sphe", grad_scores, piece_queries, preferred_element_type=jnp.float32
        )
        * scale
    ).reshape(slots, rows, width)
    values_total = jnp.einsum(
        "snhp,snhe->sphe",
        probs.astype(jnp.bfloat16),
        piece_grads,
        preferred_element_type=jnp.float32,
    ).reshape(slots, rows, width)
    return (
        grad_queries.astype(jnp.bfloat16),
        keys_total.astype(jnp.bfloat16),
        values_total.astype(jnp.bfloat16),
    )


def body(
    tokens,
    cotangent,
    emb_table,
    ada_weight,
    ada_bias,
    qkv_weight,
    out_weight,
    out_bias,
    up_weight,
    up_bias,
    down_weight,
    down_bias,
    lead_class,
    group_count,
):
    group = lax.axis_index("narrow")
    slot_count = tokens.shape[1]
    width = tokens.shape[3]
    table = emb_table.astype(jnp.float32)
    class_range = jnp.arange(table.shape[0], dtype=jnp.int32)
    classes_here = lax.dynamic_index_in_dim(lead_class, group, 0, keepdims=False)
    count_here = lax.dynamic_index_in_dim(group_count, group, 0, keepdims=False)
    live = (jnp.arange(slot_count, dtype=jnp.int32) < count_here).astype(jnp.float32)[:, None, None]
    embed_here = jnp.dot(
        (classes_here[:, None] == class_range[None, :]).astype(jnp.float32),
        table,
        precision=highest,
    )
    silu_here = embed_here * jax.nn.sigmoid(embed_here)
    hidden = tokens[0].astype(jnp.float32)
    layer = 0
    parts = modulation_parts(silu_here, ada_weight[layer], ada_bias[layer])
    later = (
        out_weight[layer],
        out_bias[layer],
        up_weight[layer],
        up_bias[layer],
        down_weight[layer],
        down_bias[layer],
    )
    normed, inverse, modulated, queries, keys_here, values_here = before_attention(
        hidden, parts, qkv_weight[layer]
    )
    attended, log_total, whole_pair = attention_forward(queries, keys_here, values_here)
    kept = [(hidden, parts, attended, log_total, whole_pair)]
    hidden, unused = after_attention(hidden, attended, parts, later)
    output = hidden * live
    grad = cotangent[0].astype(jnp.float32) * live
    grad_mods = [None] * LAYERS
    weight_grads = [None] * LAYERS
    for layer in reversed(range(LAYERS)):
        layer_input, parts, attended, log_total, whole_pair = kept[layer]
        later = (
            out_weight[layer],
            out_bias[layer],
            up_weight[layer],
            up_bias[layer],
            down_weight[layer],
            down_bias[layer],
        )
        normed, inverse, modulated, queries, keys_here, values_here = before_attention(
            layer_input, parts, qkv_weight[layer]
        )
        unused, inner = after_attention(layer_input, attended, parts, later)
        branch, middle, normed_mlp, inverse_mlp, modulated_mlp, upward, activated, feed = inner
        grad_feed = (grad * parts[5]).astype(jnp.bfloat16)
        grad_gate_mlp = jnp.sum(grad * feed, axis=1)
        grad_down_w = jnp.einsum(
            "spf,spd->fd", activated, grad_feed, preferred_element_type=jnp.float32
        )
        grad_down_b = jnp.sum(grad_feed.astype(jnp.float32), axis=(0, 1))
        grad_upward = (
            jnp.einsum(
                "spd,fd->spf", grad_feed, down_weight[layer], preferred_element_type=jnp.float32
            )
            * gelu_slope(upward)
        ).astype(jnp.bfloat16)
        grad_up_w = jnp.einsum(
            "spd,spf->df", modulated_mlp, grad_upward, preferred_element_type=jnp.float32
        )
        grad_up_b = jnp.sum(grad_upward.astype(jnp.float32), axis=(0, 1))
        grad_mod_mlp = jnp.einsum(
            "spf,df->spd", grad_upward, up_weight[layer], preferred_element_type=jnp.float32
        )
        grad_shift_mlp = jnp.sum(grad_mod_mlp, axis=1)
        grad_scale_mlp = jnp.sum(grad_mod_mlp * normed_mlp, axis=1)
        grad_middle = grad + norm_back(grad_mod_mlp * (1.0 + parts[4]), normed_mlp, inverse_mlp)
        grad_gate_attn = jnp.sum(grad_middle * branch, axis=1)
        grad_branch = (grad_middle * parts[2]).astype(jnp.bfloat16)
        grad_out_w = jnp.einsum(
            "spd,spe->de", attended, grad_branch, preferred_element_type=jnp.float32
        )
        grad_out_b = jnp.sum(grad_branch.astype(jnp.float32), axis=(0, 1))
        grad_attended = jnp.einsum(
            "spe,de->spd", grad_branch, out_weight[layer], preferred_element_type=jnp.float32
        ).astype(jnp.bfloat16)
        delta = jnp.sum(
            split_heads(grad_attended.astype(jnp.float32) * attended.astype(jnp.float32)), axis=-1
        )
        grad_queries, grad_keys, grad_values = attention_backward(
            queries, keys_here, values_here, grad_attended, log_total, delta
        )
        grad_projected = jnp.concatenate([grad_queries, grad_keys, grad_values], axis=-1)
        grad_qkv_w = jnp.einsum(
            "spd,spf->df", modulated, grad_projected, preferred_element_type=jnp.float32
        )
        grad_mod_attn = jnp.einsum(
            "spf,df->spd", grad_projected, qkv_weight[layer], preferred_element_type=jnp.float32
        )
        grad_shift_attn = jnp.sum(grad_mod_attn, axis=1)
        grad_scale_attn = jnp.sum(grad_mod_attn * normed, axis=1)
        grad = grad_middle + norm_back(grad_mod_attn * (1.0 + parts[1]), normed, inverse)
        local_mods = jnp.stack(
            [
                grad_shift_attn,
                grad_scale_attn,
                grad_gate_attn,
                grad_shift_mlp,
                grad_scale_mlp,
                grad_gate_mlp,
            ],
            axis=1,
        ).reshape(slot_count, 6 * width)
        grad_mods[layer] = lax.psum(local_mods, "wide")
        weight_grads[layer] = lax.psum(
            (grad_qkv_w, grad_out_w, grad_out_b, grad_up_w, grad_up_b, grad_down_w, grad_down_b),
            ("narrow", "wide"),
        )
    all_mods = lax.all_gather(
        jnp.stack(grad_mods, axis=0).astype(jnp.bfloat16), "narrow", axis=1, tiled=True
    ).astype(jnp.float32)
    all_classes = lead_class.reshape(-1)
    onehot_all = (all_classes[:, None] == class_range[None, :]).astype(jnp.float32)
    embed_all = jnp.dot(onehot_all, table, precision=highest)
    sigmoid_all = jax.nn.sigmoid(embed_all)
    silu_all = embed_all * sigmoid_all
    grad_ada_w = jnp.einsum("id,lie->lde", silu_all, all_mods, precision=highest)
    grad_ada_b = jnp.sum(all_mods, axis=1)
    grad_silu = jnp.einsum(
        "lie,lde->id", all_mods, ada_weight.astype(jnp.float32), precision=highest
    )
    grad_embed = grad_silu * (sigmoid_all + embed_all * sigmoid_all * (1.0 - sigmoid_all))
    grad_table = jnp.dot(onehot_all.T, grad_embed, precision=highest)
    stacked = [jnp.stack([weight_grads[0][member]], axis=0) for member in range(7)]
    return (
        output[None],
        grad[None],
        grad_table,
        grad_ada_w,
        grad_ada_b,
        stacked[0],
        stacked[1],
        stacked[2],
        stacked[3],
        stacked[4],
        stacked[5],
        stacked[6],
    )


def solution(mesh):
    in_specs = (
        P("narrow", None, "wide", None),
        P("narrow", None, "wide", None),
        P(),
        P(),
        P(),
        P(),
        P(),
        P(),
        P(),
        P(),
        P(),
        P(),
        P(),
        P(),
    )
    out_specs = (
        P("narrow", None, "wide", None),
        P("narrow", None, "wide", None),
        P(),
        P(),
        P(),
        P(),
        P(),
        P(),
        P(),
        P(),
        P(),
        P(),
    )
    by_item = dict(mesh.shape) == {"narrow": 4, "wide": 8}
    return jax.shard_map(fast_body if by_item else body, mesh=mesh, in_specs=in_specs, out_specs=out_specs, check_vma=False)
```

```python
import functools
from types import SimpleNamespace

import jax
import jax.numpy as jnp
from jax import lax
from jax.experimental import pallas as pl
from jax.experimental.pallas import tpu as pltpu
from jax.sharding import PartitionSpec as P

MESH = pl.DeviceIdType.MESH
f32, bf16 = jnp.float32, jnp.bfloat16
EPS = 1e-06
ROOT_HALF = 0.7071067811865476
INV_ROOT_2PI = 0.3989422804014327
HEAD_DIM = 64
EARLY = 6
FORMS = (False, False, False, False, False, False, False, False, False)
PLAN = (
    (),
    (),
    (),
    (),
    (),
    (0, 1),
    (2, 3),
    (),
    (4,),
    (5,),
    (),
    (0,),
    (),
    (),
    (1,),
    (),
    (),
    (2, 0),
    (),
    (3, 6, 1),
    (),
    (4,),
    (),
    (2, 5),
    (0, 7, 3, 6, 1, 4, 8),
    (2,),
    (5, 9, 3, 0, 6, 0, 4, 7, 1, 1, 8, 2, 2, 5, 6, 7, 9, 8, 3, 3, 4, 7, 4, 5, 9, 5, 8, 9, 6, 6, 7, 7, 8, 8),
)


def dot_nn(a, b):
    return lax.dot_general(a, b, (((1,), (0,)), ((), ())), preferred_element_type=f32)


def dot_nt(a, b):
    return lax.dot_general(a, b, (((1,), (1,)), ((), ())), preferred_element_type=f32)


def dot_tn(a, b):
    return lax.dot_general(a, b, (((0,), (0,)), ((), ())), preferred_element_type=f32)


def norm_rows(x):
    centred = x - jnp.mean(x, axis=-1, keepdims=True)
    inverse = lax.rsqrt(jnp.mean(centred * centred, axis=-1, keepdims=True) + EPS)
    return centred * inverse, inverse


def norm_rows_back(x, n, inverse):
    first = jnp.mean(x, axis=-1, keepdims=True)
    second = jnp.mean(x * n, axis=-1, keepdims=True)
    return inverse * (x - first - n * second)


def col_sum(x):
    return jnp.sum(x, axis=0, keepdims=True)


class Place:
    def __init__(self):
        narrow, wide = lax.axis_index("narrow"), lax.axis_index("wide")
        self.y, self.c = narrow // 2, narrow % 2
        self.z, self.x = wide // 2, wide % 2
        self.wide = wide
        self.low = wide % 4
        self.half = wide // 4
        self.rows_half = 1 - self.c

    def low_xor(self, i):
        a = self.low
        if i & 1:
            a = a + 1 - 2 * (a % 2)
        if i & 2:
            a = a + 2 - 4 * (a // 2)
        return a

    def home(self, i):
        slot = self.low_xor(i)
        return slot, (2 * self.y + 1 - self.half, 4 * self.c + slot)

    def source(self, i):
        strip = self.low_xor(i)
        return strip, (2 * self.y + self.half, 4 * self.rows_half + strip)

    def core(self):
        return (2 * self.y + 1 - self.c, self.wide)

    def in_plane(self, k):
        x = 1 - self.x if k & 1 else self.x
        y = 1 - self.y if k & 2 else self.y
        return 2 * y + x, (2 * y + self.c, 2 * self.z + x)

    def along_z(self, k):
        z = self.z
        if k & 1:
            z = z + 1 - 2 * (z % 2)
        if k & 2:
            z = z + 2 - 4 * (z // 2)
        return z, (2 * self.y + self.c, 2 * z + self.x)


class Wire:
    def __init__(self, send_sems, recv_sems):
        self.send_sems, self.recv_sems = send_sems, recv_sems
        self.count = 0
        self.sent = []

    def copy(self, src, dst, device):
        index = self.count
        self.count += 1
        made = pltpu.make_async_remote_copy(
            src_ref=src,
            dst_ref=dst,
            send_sem=self.send_sems.at[index],
            recv_sem=self.recv_sems.at[index],
            device_id=device,
            device_id_type=MESH,
        )
        made.start()
        self.sent.append(made)
        return made

    def sent_out(self, made):
        made.wait_send()
        self.sent.remove(made)

    def finish(self):
        for made in self.sent:
            made.wait_send()


def main_kernel(sizes, names, *refs):
    r = SimpleNamespace(**dict(zip(names, refs, strict=True)))
    R, D, FF = sizes
    M, N = 4 * R, 8 * R
    MB = M // 2
    pairs = D // 128
    here = Place()
    wire = Wire(r.send_sems, r.recv_sems)
    local_sems = r.local_sems
    local_count = [0]

    def local(src, dst):
        made = pltpu.make_async_copy(src, dst, local_sems.at[local_count[0]])
        local_count[0] += 1
        made.start()
        return made

    load_ada = local(r.ada_weight.at[0], r.ada_weight_v)
    load_qkv = [
        local(
            r.qkv_weight.at[0, :, pl.ds(b * D + p * 128, 128)],
            r.qkv_weight_v.at[p, :, pl.ds(b * 128, 128)],
        )
        for p in range(pairs)
        for b in range(3)
    ]
    load_rest = [
        local(r.out_weight.at[0], r.out_weight_v),
        local(r.up_weight.at[0], r.up_weight_v),
        local(r.down_weight.at[0], r.down_weight_v),
    ]

    barrier = pltpu.get_barrier_semaphore()
    partners = [here.core()]
    partners += [here.home(i)[1] for i in range(4)] + [here.source(i)[1] for i in range(4)]
    partners += [here.in_plane(k)[1] for k in (1, 2, 3)] + [here.along_z(k)[1] for k in (1, 2, 3)]
    for device in partners:
        pl.semaphore_signal(barrier, inc=1, device_id=device, device_id_type=MESH)
    pl.semaphore_wait(barrier, len(partners))

    def send_home(whole, landing):
        place = pl.ds(pl.multiple_of(here.low * R, R), R)
        made = []
        for i in range(4):
            slot, device = here.home(i)
            made.append(wire.copy(whole.at[0, slot], landing.at[place, :], device))
        return made

    tokens_in = send_home(r.tokens, r.tokens_v)

    group, slot = 2 * here.y + here.half, here.low
    item_class = r.lead_class[group, slot]
    live = (slot < r.group_count[group]).astype(f32)
    table = r.emb_table[...].astype(f32)
    class_col = lax.broadcasted_iota(jnp.int32, (table.shape[0], 1), 0)
    onehot = (class_col == item_class).astype(f32)
    embed = jnp.sum(onehot * table, axis=0, keepdims=True)
    silu = embed * (1.0 / (1.0 + jnp.exp(-embed)))
    high = silu.astype(bf16).astype(f32)
    middle_part = (silu - high).astype(bf16).astype(f32)
    low_part = silu - high - middle_part
    row = lax.broadcasted_iota(jnp.int32, (16, D), 0)
    parts = jnp.where(row == 0, high, jnp.where(row == 1, middle_part, jnp.where(row == 2, low_part, 0.0)))
    load_ada.wait()
    mods = r.mods
    for k in range(6):
        cols = pl.ds(k * D, D)
        mods[k : k + 1, :] = col_sum(
            dot_nn(parts.astype(bf16), r.ada_weight_v[:, cols])
        ) + r.ada_bias[:, cols].astype(f32)

    def mod(k):
        return mods[k : k + 1, :]

    acc = r.acc
    acc[...] = jnp.zeros_like(acc)

    for made in load_qkv:
        made.wait()
    lane = lax.broadcasted_iota(jnp.int32, (R, 128), 1)
    left = lane < HEAD_DIM
    kv, qst = r.kv, r.qst
    kv_copies = []
    own = pl.multiple_of(here.rows_half * M, M)
    for i in range(4):
        strip, _ = here.source(i)
        tokens_in[i].wait_recv()
        at = pl.multiple_of(strip * R, R)
        rows = pl.ds(at, R)
        normed, inverse = norm_rows(r.tokens_v[rows, :].astype(f32))
        r.normed[rows, :] = normed
        r.inverse[rows, :] = inverse
        modulated = (normed * (1.0 + mod(1)) + mod(0)).astype(bf16)
        r.modulated[rows, :] = modulated
        kv_rows = pl.ds(pl.multiple_of(own + at, R), R)
        for p in range(pairs):
            projected = dot_nn(modulated, r.qkv_weight_v[p]).astype(bf16)
            kv[p, kv_rows, :] = projected[:, 128:]
            q = projected[:, :128] * HEAD_DIM ** (-0.5)
            zero = jnp.zeros_like(q)
            qst[p, pl.ds(at, R), :] = jnp.where(left, q, zero)
            qst[p, pl.ds(pl.multiple_of(M + at, R), R), :] = jnp.where(left, zero, q)
        kv_copies.append(wire.copy(kv.at[:, kv_rows, :], kv.at[:, kv_rows, :], here.core()))
    for made in tokens_in:
        wire.sent_out(made)
    cotangent_in = send_home(r.cotangent, r.cotangent_v)
    for made in kv_copies:
        made.wait_recv()

    kvt, es, ots = r.kvt, r.es, r.ots
    for p in range(pairs):
        kvt[p] = kv[p].T
    QB = M // 2
    CB = N // 4
    scores = (r.scores_a, r.scores_b)

    def score_rows(j, c):
        p, qb = j // 4, j % 4
        found = dot_nt(kv[p, c * CB : (c + 1) * CB, :128], qst[p, qb * QB : (qb + 1) * QB, :])
        scores[j % 2][c * CB : (c + 1) * CB, :] = found
        return jnp.max(found.reshape(CB // 8, 8, QB), axis=0)

    def mix(j):
        p, qb = j // 4, j % 4
        half = qb // 2 * HEAD_DIM
        mixed = dot_nn(kvt[p, 128 + half : 128 + half + HEAD_DIM, :], es[p, :, qb * QB : (qb + 1) * QB])
        head = slice(p * 128 + half, p * 128 + half + HEAD_DIM)
        ots[head, qb % 2 * QB : (qb % 2 + 1) * QB] = mixed * r.inv_sum[j]

    tops = [score_rows(0, c) for c in range(4)]
    for j in range(4 * pairs):
        p, qb = j // 4, j % 4
        top = jnp.maximum(jnp.maximum(tops[0], tops[1]), jnp.maximum(tops[2], tops[3]))
        top = jnp.max(top, axis=0, keepdims=True)
        tops, sums = [], []
        for c in range(4):
            keys = slice(c * CB, (c + 1) * CB)
            if j + 1 < 4 * pairs:
                tops.append(score_rows(j + 1, c))
            raised = jnp.exp(scores[j % 2][keys, :] - top)
            sums.append(jnp.sum(raised.reshape(CB // 8, 8, QB), axis=0))
            es[p, keys, qb * QB : (qb + 1) * QB] = raised.astype(bf16)
            if c == 0 and j > 0:
                mix(j - 1)
        r.inv_sum[j] = 1.0 / col_sum((sums[0] + sums[1]) + (sums[2] + sums[3]))
    mix(4 * pairs - 1)
    att = r.att
    for p in range(pairs):
        att[:, p * 128 : (p + 1) * 128] = ots[p * 128 : (p + 1) * 128, :].T.astype(bf16)

    for made in load_rest:
        made.wait()
    outw, upw, downw = r.out_weight_v, r.up_weight_v, r.down_weight_v
    chunks = FF // D

    def send_back(stage, landing):
        made = []
        for i in range(4):
            strip, device = here.source(i)
            rows = pl.ds(pl.multiple_of(strip * R, R), R)
            made.append(wire.copy(stage.at[rows, :], landing.at[here.low], device))
        return made

    def feed_rows(t):
        rows = slice(t * MB, (t + 1) * MB)
        branch = dot_nn(att[rows, :], outw[...]) + r.out_bias[...].astype(f32)
        middle = r.tokens_v[rows, :].astype(f32) + mod(2) * branch
        n, inverse = norm_rows(middle)
        modulated = (n * (1.0 + mod(4)) + mod(3)).astype(bf16)
        r.modulated_m[rows, :] = modulated
        yield
        for ck in range(chunks):
            cols = slice(ck * D, (ck + 1) * D)
            u = dot_nn(modulated, upw[:, cols]) + r.up_bias[:, cols].astype(f32)
            phi = 0.5 * (1.0 + lax.erf(u * ROOT_HALF))
            r.activated[rows, cols] = (u * phi).astype(bf16)
            r.slope[rows, cols] = phi + u * (INV_ROOT_2PI * jnp.exp(-0.5 * u * u))
            yield
        feed = dot_nn(r.activated[rows, :], downw[...]) + r.down_bias[...].astype(f32)
        r.out_stage[rows, :] = ((middle + mod(5) * feed) * live).astype(bf16)
        yield
        grad = r.cotangent_v[rows, :].astype(f32) * live
        grad_feed = (grad * mod(5)).astype(bf16)
        r.grad_feed[rows, :] = grad_feed
        acc[5:6, :] += col_sum(grad * feed)
        acc[8:9, :] += col_sum(grad_feed.astype(f32))
        yield
        for ck in range(chunks):
            cols = slice(ck * D, (ck + 1) * D)
            grad_up = (dot_nt(grad_feed, downw[cols, :]) * r.slope[rows, cols]).astype(bf16)
            r.grad_up[rows, cols] = grad_up
            acc[9 + ck : 10 + ck, :] += col_sum(grad_up.astype(f32))
            yield
        back = dot_nt(r.grad_up[rows, :], upw[...])
        acc[3:4, :] += col_sum(back)
        acc[4:5, :] += col_sum(back * n)
        grad_middle = grad + norm_rows_back(back * (1.0 + mod(4)), n, inverse)
        r.grad_middle[rows, :] = grad_middle
        acc[2:3, :] += col_sum(grad_middle * branch)
        grad_branch = (grad_middle * mod(2)).astype(bf16)
        r.grad_branch[rows, :] = grad_branch
        acc[13:14, :] += col_sum(grad_branch.astype(f32))
        yield
        r.grad_att[rows, :] = dot_nt(grad_branch, outw[...]).astype(bf16)

    blocks = [feed_rows(0), feed_rows(1)]
    for _ in range(chunks + 2):
        for block in blocks:
            next(block)
    out_copies = send_back(r.out_stage, r.out_o)
    for made in cotangent_in:
        made.wait_recv()
    for _ in range(chunks + 3):
        for block in blocks:
            next(block, None)

    part, total, arena = r.part, r.total, r.arena
    used = [0]
    stored = []

    def room(rows):
        start = used[0]
        used[0] += rows
        return start

    def span(start, index, rows):
        return pl.ds(pl.multiple_of(start + index * rows, 16), rows)

    def wide(ref, rows):
        return ref[rows, :].astype(f32)

    def receive(flight):
        for made in flight:
            made.wait_recv()

    def reduce_unit(base, rows, z_first):
        half = rows // 2
        land = room(half)
        block = room(half)
        flight = [
            wire.copy(
                part.at[span(base, 1 - here.c, half), :], arena.at[pl.ds(land, half), :], here.core()
            )
        ]
        yield
        receive(flight)
        count = half // 8

        def add(q, carry):
            arena[span(block, q, count), :] = (
                wide(part, span(base + half * here.c, q, count)) + wide(arena, span(land, q, count))
            ).astype(bf16)
            return carry

        lax.fori_loop(0, 8, add, 0)
        mine = base + half * here.c
        count = half
        axes = (here.along_z, here.in_plane) if z_first else (here.in_plane, here.along_z)
        for axis in axes:
            count = count // 4
            land = room(3 * count)
            flight = []
            for k in (3, 2, 1):
                q, device = axis(k)
                flight.append(
                    wire.copy(
                        arena.at[span(block, q, count), :],
                        arena.at[pl.ds(land + (k - 1) * count, count), :],
                        device,
                    )
                )
            yield
            receive(flight)
            me = axis(0)[0]
            summed = wide(arena, span(block, me, count)) + wide(arena, pl.ds(land, count))
            summed = summed + (
                wide(arena, pl.ds(land + count, count)) + wide(arena, pl.ds(land + 2 * count, count))
            )
            mine = mine + count * me
            if axis is axes[0]:
                block = room(count)
                arena[pl.ds(block, count), :] = summed.astype(bf16)
            else:
                total[span(mine, 0, count), :] = summed.astype(bf16)
        for axis in axes[::-1]:
            keep = span(mine, 0, count)
            flight = [
                wire.copy(total.at[keep, :], total.at[keep, :], axis(k)[1]) for k in (3, 2, 1)
            ]
            yield
            receive(flight)
            mine = mine - count * axis(0)[0]
            count = 4 * count
        keep = span(mine, 0, half)
        flight = [wire.copy(total.at[keep, :], total.at[keep, :], here.core())]
        yield
        receive(flight)
        keep = pl.ds(base, rows)
        stored.append(local(total.at[keep, :], r.grads_o.at[keep, :]))
        yield

    def reduce_small():
        small, small_a, small_b, land, small_sum = (
            r.small,
            r.small_a,
            r.small_b,
            r.land_small,
            r.small_sum,
        )
        here_rows = span(0, here.c, 16)
        flight = [wire.copy(small.at[span(0, 1 - here.c, 16), :], land.at[0], here.core())]
        yield
        receive(flight)
        small_a[...] = small[here_rows, :] + land[0]
        flight = [wire.copy(small_a, land.at[k], here.in_plane(k)[1]) for k in (3, 2, 1)]
        yield
        receive(flight)
        small_b[...] = (small_a[...] + land[1]) + (land[2] + land[3])
        flight = [wire.copy(small_b, land.at[3 + k], here.along_z(k)[1]) for k in (3, 2, 1)]
        yield
        receive(flight)
        small_sum[here_rows, :] = (small_b[...] + land[4]) + (land[5] + land[6])
        flight = [wire.copy(small_sum.at[here_rows, :], small_sum.at[here_rows, :], here.core())]
        yield
        receive(flight)
        stored.append(local(small_sum, r.small_o))
        yield

    third = 4 * D // 3
    early = 2 * FF // EARLY
    units = [reduce_unit(early * i, early, FORMS[i]) for i in range(EARLY)]
    units += [reduce_unit(2 * FF + third * i, third, FORMS[EARLY + i]) for i in range(3)]
    units.append(reduce_small())
    plan = iter(PLAN)

    def advance():
        for unit in next(plan):
            next(units[unit])

    started = 0
    for ck in range(2 * chunks):
        rows = slice(ck * D, (ck + 1) * D)
        cols = slice(ck % chunks * D, (ck % chunks + 1) * D)
        if ck < chunks:
            found = dot_tn(r.activated[:, cols], r.grad_feed[...])
        else:
            found = dot_tn(r.modulated_m[...], r.grad_up[:, cols])
        part[rows, :] = found.astype(bf16)
        while started < EARLY and (started + 1) * early <= (ck + 1) * D:
            next(units[started])
            started += 1
        advance()
    part[2 * FF : 2 * FF + D, :] = dot_tn(att[...], r.grad_branch[...]).astype(bf16)

    gat, qgt = r.gat, r.qgt
    for p in range(pairs):
        gat[p * 128 : (p + 1) * 128, :] = r.grad_att[:, p * 128 : (p + 1) * 128].T.astype(f32)
    zero_half = jnp.zeros((HEAD_DIM, QB), bf16)
    gst, gstt, deltas, dkv = r.gst, r.gstt, r.deltas, r.dkv
    dss = (r.dss_a, r.dss_b)
    for p in range(pairs):
        for qb in range(4):
            half = qb // 2
            head = slice(p * 128 + half * HEAD_DIM, p * 128 + (half + 1) * HEAD_DIM)
            queries = slice(qb % 2 * QB, (qb % 2 + 1) * QB)
            scaled = gat[head, queries] * r.inv_sum[4 * p + qb]
            deltas[4 * p + qb] = col_sum(scaled * ots[head, queries])
            scaled = scaled.astype(bf16)
            filled = [scaled, zero_half] if half == 0 else [zero_half, scaled]
            gstt[p, :, qb * QB : (qb + 1) * QB] = jnp.concatenate(filled, axis=0)
        gst[p] = gstt[p].T
    other = pl.multiple_of((1 - here.rows_half) * M, M)
    dkv_copies = []
    gp = r.grad_projected

    def finish_pair(p):
        gp[p, :, 0:128] = qgt[p * 128 : (p + 1) * 128, :].T.astype(bf16)
        dkv_copies[p].wait_recv()
        gp[p, :, 128:384] = (
            dkv[p, pl.ds(own, M), :].astype(f32) + r.land_dkv[p].astype(f32)
        ).astype(bf16)
        rows = slice(2 * FF + (p + 1) * D, 2 * FF + (p + 2) * D)
        part[rows, :] = dot_tn(r.modulated[...], gp[p]).astype(bf16)
        next(units[EARLY + p])
        advance()

    def grad_values(p, c):
        keys = slice(c * CB, (c + 1) * CB)
        dkv[p, keys, 128:256] = dot_nn(es[p, keys, :], gst[p]).astype(bf16)

    def grad_keys(p, c):
        keys = slice(c * CB, (c + 1) * CB)
        dkv[p, keys, 0:128] = dot_nn(dss[p % 2][keys, :], qst[p]).astype(bf16)
        if c == 3:
            dkv_copies.append(
                wire.copy(dkv.at[p, pl.ds(other, M), :], r.land_dkv.at[p], here.core())
            )

    def grad_queries(p, qb):
        half = qb // 2 * HEAD_DIM
        head = slice(p * 128 + half, p * 128 + half + HEAD_DIM)
        found = dot_nn(kvt[p, half : half + HEAD_DIM, :], dss[p % 2][:, qb * QB : (qb + 1) * QB])
        qgt[head, qb % 2 * QB : (qb % 2 + 1) * QB] = found * HEAD_DIM ** (-0.5)

    later = []
    advance()
    for p in range(pairs):
        for qb in range(4):
            queries = slice(qb * QB, (qb + 1) * QB)
            for c in range(4):
                keys = slice(c * CB, (c + 1) * CB)
                slope = dot_nn(kv[p, keys, 128:], gstt[p, :, queries])
                dss[p % 2][keys, queries] = (
                    es[p, keys, queries].astype(f32) * (slope - deltas[4 * p + qb])
                ).astype(bf16)
                if later:
                    later.pop(0)()
            later.append(functools.partial(grad_queries, p, qb))
            if qb == 0:
                later += [functools.partial(grad_values, p, k) for k in range(4)]
            if qb == 3:
                later += [functools.partial(grad_keys, p, k) for k in range(4)]
            advance()
            if p > 0 and qb == 3:
                finish_pair(p - 1)
    for made in later:
        made()
    advance()
    finish_pair(pairs - 1)

    for t in range(2):
        rows = slice(t * MB, (t + 1) * MB)
        back = dot_nt(gp[0, rows, :], r.qkv_weight_v[0])
        for p in range(1, pairs):
            back = back + dot_nt(gp[p, rows, :], r.qkv_weight_v[p])
        n = r.normed[rows, :]
        acc[0:1, :] += col_sum(back)
        acc[1:2, :] += col_sum(back * n)
        grad = r.grad_middle[rows, :] + norm_rows_back(
            back * (1.0 + mod(1)), n, r.inverse[rows, :]
        )
        r.gtok_stage[rows, :] = grad.astype(bf16)
        if t == 0:
            advance()
    gtok_copies = send_back(r.gtok_stage, r.gtok_o)

    small = r.small
    for k in range(6):
        small[4 * k : 4 * k + 4, :] = onehot * acc[k : k + 1, :]
    small[24:32, :] = acc[8:16, :]
    next(units[EARLY + 3])
    advance()
    for made in out_copies + gtok_copies:
        made.wait_recv()
    wire.finish()
    for made in stored:
        made.wait()


def last_kernel(sizes, names, *refs):
    r = SimpleNamespace(**dict(zip(names, refs, strict=True)))
    D, FF = sizes
    sems = r.sems
    count = [0]

    def local(src, dst):
        made = pltpu.make_async_copy(src, dst, sems.at[count[0]])
        count[0] += 1
        made.start()
        return made

    small_in = local(r.small_i, r.small_i_v)
    ada_in = local(r.ada_weight, r.ada_weight_v)
    out_in = local(r.out_i, r.out_i_v)
    gtok_in = local(r.gtok_i, r.gtok_i_v)
    grads_in = []
    for b in range(3):
        rows = pl.ds(b * 4 * D, 4 * D)
        grads_in.append(local(r.grads_i.at[rows, :], r.grads_v.at[rows, :]))
    outs = []
    small_in.wait()
    small = r.small_i_v
    table = r.emb_table[...].astype(f32)
    sigmoid = 1.0 / (1.0 + jnp.exp(-table))
    silu = table * sigmoid

    def split(v):
        high = v.astype(bf16).astype(f32)
        return high, v - high

    silu_high, silu_low = split(silu)
    zero = jnp.zeros_like(silu)
    left = jnp.concatenate([silu_high, silu_low, silu_high, zero], axis=0).astype(bf16)
    grad_silu = jnp.zeros_like(table)
    ada_in.wait()
    for k in range(6):
        cols = slice(k * D, (k + 1) * D)
        block = small[4 * k : 4 * k + 4, :]
        high, low = split(block)
        right = jnp.concatenate([high, high, low, zero], axis=0).astype(bf16)
        r.gada_v[:, cols] = dot_tn(left, right)
        r.gada_b[:, cols] = col_sum(block)
        both = jnp.concatenate([high, low, zero, zero], axis=0).astype(bf16)
        found = dot_nt(both, r.ada_weight_v[0, :, cols])
        grad_silu = grad_silu + found[0:4, :] + found[4:8, :]
    outs.append(local(r.gada_v, r.gada.at[0]))
    r.table_o[...] = grad_silu * (sigmoid + table * sigmoid * (1.0 - sigmoid))
    r.down_b[...] = small[24:25, :]
    for k in range(FF // D):
        r.up_b[:, k * D : (k + 1) * D] = small[25 + k : 26 + k, :]
    r.out_b[...] = small[29:30, :]
    for arrived, given, wide_v, result in (
        (out_in, r.out_i_v, r.out_v, r.out),
        (gtok_in, r.gtok_i_v, r.gtok_v, r.gtok),
    ):
        arrived.wait()
        for s in range(4):
            wide_v[s] = given[s].astype(f32)
        outs.append(local(wide_v, result.at[0]))
    grads = r.grads_v
    grads_in[0].wait()
    for k in range(FF // D):
        r.gdown_v[k * D : (k + 1) * D, :] = grads[k * D : (k + 1) * D, :].astype(f32)
    outs.append(local(r.gdown_v, r.gdown.at[0]))
    grads_in[1].wait()
    for k in range(FF // D):
        r.gup_v[:, k * D : (k + 1) * D] = grads[FF + k * D : FF + (k + 1) * D, :].astype(f32)
    outs.append(local(r.gup_v, r.gup.at[0]))
    grads_in[2].wait()
    r.gout_v[...] = grads[2 * FF : 2 * FF + D, :].astype(f32)
    outs.append(local(r.gout_v, r.gout.at[0]))
    for p in range(D // 128):
        for k in range(3):
            rows = slice(2 * FF + (p + 1) * D, 2 * FF + (p + 2) * D)
            cols = slice(k * D + p * 128, k * D + (p + 1) * 128)
            r.gqkv_v[:, cols] = grads[rows, k * 128 : (k + 1) * 128].astype(f32)
    outs.append(local(r.gqkv_v, r.gqkv.at[0]))
    for made in outs:
        made.wait()


def fast_body(*args):
    tokens, emb_table, ada_weight, up_weight = args[0], args[2], args[3], args[8]
    R, D = tokens.shape[2:]
    FF = up_weight.shape[2]
    M, N = 4 * R, 8 * R
    pairs = D // 128
    total_rows = 2 * FF + 4 * D
    vmem = pl.BlockSpec(memory_space=pltpu.VMEM)
    smem = pl.BlockSpec(memory_space=pltpu.SMEM)
    anywhere = pl.BlockSpec(memory_space=pl.ANY)
    arguments = dict(
        tokens=anywhere,
        cotangent=anywhere,
        emb_table=vmem,
        ada_weight=anywhere,
        ada_bias=vmem,
        qkv_weight=anywhere,
        out_weight=anywhere,
        out_bias=vmem,
        up_weight=anywhere,
        up_bias=vmem,
        down_weight=anywhere,
        down_bias=vmem,
        lead_class=smem,
        group_count=smem,
    )
    scratch = dict(
        ada_weight_v=pltpu.VMEM((D, 6 * D), bf16),
        qkv_weight_v=pltpu.VMEM((pairs, D, 384), bf16),
        out_weight_v=pltpu.VMEM((D, D), bf16),
        up_weight_v=pltpu.VMEM((D, FF), bf16),
        down_weight_v=pltpu.VMEM((FF, D), bf16),
        tokens_v=pltpu.VMEM((M, D), bf16),
        cotangent_v=pltpu.VMEM((M, D), bf16),
        mods=pltpu.VMEM((8, D), f32),
        acc=pltpu.VMEM((16, D), f32),
        normed=pltpu.VMEM((M, D), f32),
        inverse=pltpu.VMEM((M, 1), f32),
        modulated=pltpu.VMEM((M, D), bf16),
        kv=pltpu.VMEM((pairs, N, 256), bf16),
        kvt=pltpu.VMEM((pairs, 256, N), bf16),
        qst=pltpu.VMEM((pairs, 2 * M, 128), bf16),
        es=pltpu.VMEM((pairs, N, 2 * M), bf16),
        inv_sum=pltpu.VMEM((4 * pairs, 1, M // 2), f32),
        ots=pltpu.VMEM((D, M), f32),
        att=pltpu.VMEM((M, D), bf16),
        modulated_m=pltpu.VMEM((M, D), bf16),
        activated=pltpu.VMEM((M, FF), bf16),
        slope=pltpu.VMEM((M, FF), f32),
        out_stage=pltpu.VMEM((M, D), bf16),
        grad_feed=pltpu.VMEM((M, D), bf16),
        grad_up=pltpu.VMEM((M, FF), bf16),
        grad_middle=pltpu.VMEM((M, D), f32),
        grad_branch=pltpu.VMEM((M, D), bf16),
        grad_att=pltpu.VMEM((M, D), bf16),
        gat=pltpu.VMEM((D, M), f32),
        qgt=pltpu.VMEM((D, M), f32),
        gst=pltpu.VMEM((pairs, 2 * M, 128), bf16),
        gstt=pltpu.VMEM((pairs, 128, 2 * M), bf16),
        deltas=pltpu.VMEM((4 * pairs, 1, M // 2), f32),
        dss_a=pltpu.VMEM((N, 2 * M), bf16),
        dss_b=pltpu.VMEM((N, 2 * M), bf16),
        scores_a=pltpu.VMEM((N, M // 2), f32),
        scores_b=pltpu.VMEM((N, M // 2), f32),
        dkv=pltpu.VMEM((pairs, N, 256), bf16),
        land_dkv=pltpu.VMEM((pairs, M, 256), bf16),
        grad_projected=pltpu.VMEM((pairs, M, 384), bf16),
        gtok_stage=pltpu.VMEM((M, D), bf16),
        part=pltpu.VMEM((total_rows, D), bf16),
        total=pltpu.VMEM((total_rows, D), bf16),
        arena=pltpu.VMEM((2 * total_rows, D), bf16),
        small=pltpu.VMEM((32, D), f32),
        small_a=pltpu.VMEM((16, D), f32),
        small_b=pltpu.VMEM((16, D), f32),
        small_sum=pltpu.VMEM((32, D), f32),
        land_small=pltpu.VMEM((7, 16, D), f32),
        send_sems=pltpu.SemaphoreType.DMA((176,)),
        recv_sems=pltpu.SemaphoreType.DMA((176,)),
        local_sems=pltpu.SemaphoreType.DMA((24,)),
    )
    mids = dict(
        out_o=jax.ShapeDtypeStruct((4, R, D), bf16),
        gtok_o=jax.ShapeDtypeStruct((4, R, D), bf16),
        grads_o=jax.ShapeDtypeStruct((total_rows, D), bf16),
        small_o=jax.ShapeDtypeStruct((32, D), f32),
    )
    names = tuple(arguments) + tuple(mids) + tuple(scratch)
    middle = pl.pallas_call(
        functools.partial(main_kernel, (R, D, FF), names),
        out_shape=tuple(mids.values()),
        in_specs=list(arguments.values()),
        out_specs=(anywhere,) * 4,
        scratch_shapes=list(scratch.values()),
        compiler_params=pltpu.CompilerParams(
            collective_id=0, has_side_effects=True, vmem_limit_bytes=60 << 20
        ),
        name="block_forward_backward",
    )(*args)
    outs = dict(
        out=((1, 4, R, D), anywhere),
        gtok=((1, 4, R, D), anywhere),
        table_o=((emb_table.shape[0], D), vmem),
        gada=((1, D, 6 * D), anywhere),
        gada_b=((1, 6 * D), vmem),
        gqkv=((1, D, 3 * D), anywhere),
        gout=((1, D, D), anywhere),
        out_b=((1, D), vmem),
        gup=((1, D, FF), anywhere),
        up_b=((1, FF), vmem),
        gdown=((1, FF, D), anywhere),
        down_b=((1, D), vmem),
    )
    ins = dict(
        out_i=anywhere,
        gtok_i=anywhere,
        grads_i=anywhere,
        small_i=anywhere,
        emb_table=vmem,
        ada_weight=anywhere,
    )
    scratch = dict(
        out_i_v=pltpu.VMEM((4, R, D), bf16),
        gtok_i_v=pltpu.VMEM((4, R, D), bf16),
        grads_v=pltpu.VMEM((total_rows, D), bf16),
        small_i_v=pltpu.VMEM((32, D), f32),
        ada_weight_v=pltpu.VMEM((1, D, 6 * D), bf16),
        out_v=pltpu.VMEM((4, R, D), f32),
        gtok_v=pltpu.VMEM((4, R, D), f32),
        gada_v=pltpu.VMEM((D, 6 * D), f32),
        gqkv_v=pltpu.VMEM((D, 3 * D), f32),
        gout_v=pltpu.VMEM((D, D), f32),
        gup_v=pltpu.VMEM((D, FF), f32),
        gdown_v=pltpu.VMEM((FF, D), f32),
        sems=pltpu.SemaphoreType.DMA((16,)),
    )
    names = tuple(ins) + tuple(outs) + tuple(scratch)
    return pl.pallas_call(
        functools.partial(last_kernel, (D, FF), names),
        out_shape=tuple(jax.ShapeDtypeStruct(size, f32) for size, _ in outs.values()),
        in_specs=list(ins.values()),
        out_specs=tuple(space for _, space in outs.values()),
        scratch_shapes=list(scratch.values()),
        compiler_params=pltpu.CompilerParams(vmem_limit_bytes=60 << 20),
        name="widen_and_embed",
    )(*middle, emb_table, ada_weight)


HEADS = 6
LAYERS = 1

epsilon = 1e-06
highest = lax.Precision.HIGHEST
root_half = 0.7071067811865476
inverse_root_two_pi = 0.3989422804014327


def layer_norm(values):
    average = jnp.mean(values, axis=-1, keepdims=True)
    centred = values - average
    variance = jnp.mean(centred * centred, axis=-1, keepdims=True)
    inverse = lax.rsqrt(variance + epsilon)
    return (centred * inverse, inverse)


def norm_back(grad_normed, normed, inverse):
    first = jnp.mean(grad_normed, axis=-1, keepdims=True)
    second = jnp.mean(grad_normed * normed, axis=-1, keepdims=True)
    return inverse * (grad_normed - first - normed * second)


def gelu_exact(values):
    return 0.5 * values * (1.0 + jax.scipy.special.erf(values * root_half))


def gelu_slope(values):
    return 0.5 * (
        1.0 + jax.scipy.special.erf(values * root_half)
    ) + values * inverse_root_two_pi * jnp.exp(-0.5 * values * values)


def split_heads(values):
    return values.reshape(values.shape[0], values.shape[1], HEADS, values.shape[2] // HEADS)


def modulation_parts(silu_rows, ada_w, ada_b):
    mods = jnp.dot(silu_rows, ada_w.astype(jnp.float32), precision=highest) + ada_b.astype(
        jnp.float32
    )
    mods = mods.reshape(mods.shape[0], 6, -1)
    return [mods[:, index][:, None, :] for index in range(6)]


def before_attention(hidden, parts, qkv_low):
    normed, inverse = layer_norm(hidden)
    modulated = (normed * (1.0 + parts[1]) + parts[0]).astype(jnp.bfloat16)
    projected = jnp.einsum(
        "spd,df->spf", modulated, qkv_low, preferred_element_type=jnp.float32
    ).astype(jnp.bfloat16)
    width = hidden.shape[2]
    return (
        normed,
        inverse,
        modulated,
        projected[..., :width],
        projected[..., width : 2 * width],
        projected[..., 2 * width :],
    )


def after_attention(hidden, attended, parts, later):
    out_w, out_b, up_w, up_b, down_w, down_b = later
    branch = jnp.einsum(
        "spd,de->spe", attended, out_w, preferred_element_type=jnp.float32
    ) + out_b.astype(jnp.float32)
    middle = hidden + parts[2] * branch
    normed, inverse = layer_norm(middle)
    modulated = (normed * (1.0 + parts[4]) + parts[3]).astype(jnp.bfloat16)
    upward = jnp.einsum(
        "spd,df->spf", modulated, up_w, preferred_element_type=jnp.float32
    ) + up_b.astype(jnp.float32)
    activated = gelu_exact(upward).astype(jnp.bfloat16)
    feed = jnp.einsum(
        "spf,fd->spd", activated, down_w, preferred_element_type=jnp.float32
    ) + down_b.astype(jnp.float32)
    return (
        middle + parts[5] * feed,
        (branch, middle, normed, inverse, modulated, upward, activated, feed),
    )


def attention_forward(queries, keys_here, values_here):
    slots, rows, width = queries.shape
    scale = HEAD_DIM ** (-0.5)
    query_heads = split_heads(queries)
    running_max = jnp.full((slots, rows, HEADS), -1e30, jnp.float32)
    key_heads = split_heads(lax.all_gather(keys_here, "wide", axis=1, tiled=True))
    value_heads = split_heads(lax.all_gather(values_here, "wide", axis=1, tiled=True))
    scores = (
        jnp.einsum("sphe,snhe->sphn", query_heads, key_heads, preferred_element_type=jnp.float32)
        * scale
    )
    new_max = jnp.maximum(running_max, jnp.max(scores, axis=-1))
    weights = jnp.exp(scores - new_max[..., None])
    new_sum = jnp.sum(weights, axis=-1)
    mixed = jnp.einsum(
        "sphn,snhe->sphe",
        weights.astype(jnp.bfloat16),
        value_heads,
        preferred_element_type=jnp.float32,
    )
    total = mixed
    running_max, running_sum, total = (new_max, new_sum, total.reshape(slots, rows, width))
    attended = (
        (split_heads(total) / running_sum[..., None])
        .reshape(slots, rows, width)
        .astype(jnp.bfloat16)
    )
    return (attended, running_max + jnp.log(running_sum), None)


def attention_backward(queries, keys_here, values_here, grad_attended, log_total, delta):
    slots, rows, width = queries.shape
    scale = HEAD_DIM ** (-0.5)
    query_heads = split_heads(queries)
    grad_heads = split_heads(grad_attended)
    piece = (
        lax.all_gather(keys_here, "wide", axis=1, tiled=True),
        lax.all_gather(values_here, "wide", axis=1, tiled=True),
    )
    toward_key_heads = split_heads(piece[0])
    toward_value_heads = split_heads(piece[1])
    scores = (
        jnp.einsum(
            "sphe,snhe->sphn", query_heads, toward_key_heads, preferred_element_type=jnp.float32
        )
        * scale
    )
    probs = jnp.exp(scores - log_total[..., None])
    slope = jnp.einsum(
        "sphe,snhe->sphn", grad_heads, toward_value_heads, preferred_element_type=jnp.float32
    )
    grad_scores = (probs * (slope - delta[..., None])).astype(jnp.bfloat16)
    grad_queries = (
        jnp.einsum(
            "sphn,snhe->sphe", grad_scores, toward_key_heads, preferred_element_type=jnp.float32
        )
        * scale
    ).reshape(slots, rows, width)
    stats = (
        lax.all_gather(log_total, "wide", axis=1, tiled=True),
        lax.all_gather(delta, "wide", axis=1, tiled=True),
    )
    key_heads = split_heads(keys_here)
    value_heads = split_heads(values_here)
    piece = (
        lax.all_gather(queries, "wide", axis=1, tiled=True),
        lax.all_gather(grad_attended, "wide", axis=1, tiled=True),
    )
    piece_queries = split_heads(piece[0])
    piece_grads = split_heads(piece[1])
    piece_total = stats[0]
    piece_delta = stats[1]
    scores = (
        jnp.einsum("snhe,sphe->snhp", piece_queries, key_heads, preferred_element_type=jnp.float32)
        * scale
    )
    probs = jnp.exp(scores - piece_total[..., None])
    slope = jnp.einsum(
        "snhe,sphe->snhp", piece_grads, value_heads, preferred_element_type=jnp.float32
    )
    grad_scores = (probs * (slope - piece_delta[..., None])).astype(jnp.bfloat16)
    keys_total = (
        jnp.einsum(
            "snhp,snhe->sphe", grad_scores, piece_queries, preferred_element_type=jnp.float32
        )
        * scale
    ).reshape(slots, rows, width)
    values_total = jnp.einsum(
        "snhp,snhe->sphe",
        probs.astype(jnp.bfloat16),
        piece_grads,
        preferred_element_type=jnp.float32,
    ).reshape(slots, rows, width)
    return (
        grad_queries.astype(jnp.bfloat16),
        keys_total.astype(jnp.bfloat16),
        values_total.astype(jnp.bfloat16),
    )


def body(
    tokens,
    cotangent,
    emb_table,
    ada_weight,
    ada_bias,
    qkv_weight,
    out_weight,
    out_bias,
    up_weight,
    up_bias,
    down_weight,
    down_bias,
    lead_class,
    group_count,
):
    group = lax.axis_index("narrow")
    slot_count = tokens.shape[1]
    width = tokens.shape[3]
    table = emb_table.astype(jnp.float32)
    class_range = jnp.arange(table.shape[0], dtype=jnp.int32)
    classes_here = lax.dynamic_index_in_dim(lead_class, group, 0, keepdims=False)
    count_here = lax.dynamic_index_in_dim(group_count, group, 0, keepdims=False)
    live = (jnp.arange(slot_count, dtype=jnp.int32) < count_here).astype(jnp.float32)[:, None, None]
    embed_here = jnp.dot(
        (classes_here[:, None] == class_range[None, :]).astype(jnp.float32),
        table,
        precision=highest,
    )
    silu_here = embed_here * jax.nn.sigmoid(embed_here)
    hidden = tokens[0].astype(jnp.float32)
    layer = 0
    parts = modulation_parts(silu_here, ada_weight[layer], ada_bias[layer])
    later = (
        out_weight[layer],
        out_bias[layer],
        up_weight[layer],
        up_bias[layer],
        down_weight[layer],
        down_bias[layer],
    )
    normed, inverse, modulated, queries, keys_here, values_here = before_attention(
        hidden, parts, qkv_weight[layer]
    )
    attended, log_total, whole_pair = attention_forward(queries, keys_here, values_here)
    kept = [(hidden, parts, attended, log_total, whole_pair)]
    hidden, unused = after_attention(hidden, attended, parts, later)
    output = hidden * live
    grad = cotangent[0].astype(jnp.float32) * live
    grad_mods = [None] * LAYERS
    weight_grads = [None] * LAYERS
    for layer in reversed(range(LAYERS)):
        layer_input, parts, attended, log_total, whole_pair = kept[layer]
        later = (
            out_weight[layer],
            out_bias[layer],
            up_weight[layer],
            up_bias[layer],
            down_weight[layer],
            down_bias[layer],
        )
        normed, inverse, modulated, queries, keys_here, values_here = before_attention(
            layer_input, parts, qkv_weight[layer]
        )
        unused, inner = after_attention(layer_input, attended, parts, later)
        branch, middle, normed_mlp, inverse_mlp, modulated_mlp, upward, activated, feed = inner
        grad_feed = (grad * parts[5]).astype(jnp.bfloat16)
        grad_gate_mlp = jnp.sum(grad * feed, axis=1)
        grad_down_w = jnp.einsum(
            "spf,spd->fd", activated, grad_feed, preferred_element_type=jnp.float32
        )
        grad_down_b = jnp.sum(grad_feed.astype(jnp.float32), axis=(0, 1))
        grad_upward = (
            jnp.einsum(
                "spd,fd->spf", grad_feed, down_weight[layer], preferred_element_type=jnp.float32
            )
            * gelu_slope(upward)
        ).astype(jnp.bfloat16)
        grad_up_w = jnp.einsum(
            "spd,spf->df", modulated_mlp, grad_upward, preferred_element_type=jnp.float32
        )
        grad_up_b = jnp.sum(grad_upward.astype(jnp.float32), axis=(0, 1))
        grad_mod_mlp = jnp.einsum(
            "spf,df->spd", grad_upward, up_weight[layer], preferred_element_type=jnp.float32
        )
        grad_shift_mlp = jnp.sum(grad_mod_mlp, axis=1)
        grad_scale_mlp = jnp.sum(grad_mod_mlp * normed_mlp, axis=1)
        grad_middle = grad + norm_back(grad_mod_mlp * (1.0 + parts[4]), normed_mlp, inverse_mlp)
        grad_gate_attn = jnp.sum(grad_middle * branch, axis=1)
        grad_branch = (grad_middle * parts[2]).astype(jnp.bfloat16)
        grad_out_w = jnp.einsum(
            "spd,spe->de", attended, grad_branch, preferred_element_type=jnp.float32
        )
        grad_out_b = jnp.sum(grad_branch.astype(jnp.float32), axis=(0, 1))
        grad_attended = jnp.einsum(
            "spe,de->spd", grad_branch, out_weight[layer], preferred_element_type=jnp.float32
        ).astype(jnp.bfloat16)
        delta = jnp.sum(
            split_heads(grad_attended.astype(jnp.float32) * attended.astype(jnp.float32)), axis=-1
        )
        grad_queries, grad_keys, grad_values = attention_backward(
            queries, keys_here, values_here, grad_attended, log_total, delta
        )
        grad_projected = jnp.concatenate([grad_queries, grad_keys, grad_values], axis=-1)
        grad_qkv_w = jnp.einsum(
            "spd,spf->df", modulated, grad_projected, preferred_element_type=jnp.float32
        )
        grad_mod_attn = jnp.einsum(
            "spf,df->spd", grad_projected, qkv_weight[layer], preferred_element_type=jnp.float32
        )
        grad_shift_attn = jnp.sum(grad_mod_attn, axis=1)
        grad_scale_attn = jnp.sum(grad_mod_attn * normed, axis=1)
        grad = grad_middle + norm_back(grad_mod_attn * (1.0 + parts[1]), normed, inverse)
        local_mods = jnp.stack(
            [
                grad_shift_attn,
                grad_scale_attn,
                grad_gate_attn,
                grad_shift_mlp,
                grad_scale_mlp,
                grad_gate_mlp,
            ],
            axis=1,
        ).reshape(slot_count, 6 * width)
        grad_mods[layer] = lax.psum(local_mods, "wide")
        weight_grads[layer] = lax.psum(
            (grad_qkv_w, grad_out_w, grad_out_b, grad_up_w, grad_up_b, grad_down_w, grad_down_b),
            ("narrow", "wide"),
        )
    all_mods = lax.all_gather(
        jnp.stack(grad_mods, axis=0).astype(jnp.bfloat16), "narrow", axis=1, tiled=True
    ).astype(jnp.float32)
    all_classes = lead_class.reshape(-1)
    onehot_all = (all_classes[:, None] == class_range[None, :]).astype(jnp.float32)
    embed_all = jnp.dot(onehot_all, table, precision=highest)
    sigmoid_all = jax.nn.sigmoid(embed_all)
    silu_all = embed_all * sigmoid_all
    grad_ada_w = jnp.einsum("id,lie->lde", silu_all, all_mods, precision=highest)
    grad_ada_b = jnp.sum(all_mods, axis=1)
    grad_silu = jnp.einsum(
        "lie,lde->id", all_mods, ada_weight.astype(jnp.float32), precision=highest
    )
    grad_embed = grad_silu * (sigmoid_all + embed_all * sigmoid_all * (1.0 - sigmoid_all))
    grad_table = jnp.dot(onehot_all.T, grad_embed, precision=highest)
    stacked = [jnp.stack([weight_grads[0][member]], axis=0) for member in range(7)]
    return (
        output[None],
        grad[None],
        grad_table,
        grad_ada_w,
        grad_ada_b,
        stacked[0],
        stacked[1],
        stacked[2],
        stacked[3],
        stacked[4],
        stacked[5],
        stacked[6],
    )


def solution(mesh):
    in_specs = (
        P("narrow", None, "wide", None),
        P("narrow", None, "wide", None),
        P(),
        P(),
        P(),
        P(),
        P(),
        P(),
        P(),
        P(),
        P(),
        P(),
        P(),
        P(),
    )
    out_specs = (
        P("narrow", None, "wide", None),
        P("narrow", None, "wide", None),
        P(),
        P(),
        P(),
        P(),
        P(),
        P(),
        P(),
        P(),
        P(),
        P(),
    )
    by_item = dict(mesh.shape) == {"narrow": 4, "wide": 8}
    return jax.shard_map(fast_body if by_item else body, mesh=mesh, in_specs=in_specs, out_specs=out_specs, check_vma=False)
```

```python
import functools
from types import SimpleNamespace

import jax
import jax.numpy as jnp
from jax import lax
from jax.experimental import pallas as pl
from jax.experimental.pallas import tpu as pltpu
from jax.sharding import PartitionSpec as P

MESH = pl.DeviceIdType.MESH
f32, bf16 = jnp.float32, jnp.bfloat16
EPS = 1e-06
ROOT_HALF = 0.7071067811865476
INV_ROOT_2PI = 0.3989422804014327
HEAD_DIM = 64
EARLY_COTANGENT = 0
EARLY = 6
FORMS = (False, False, False, False, False, False, False, False, False)
PLAN = (
    (12, 13, 10, 11),
    (),
    (),
    (),
    (),
    (),
    (),
    (),
    (0,),
    (1, 2),
    (3, 4, 5),
    (),
    (),
    (),
    (),
    (),
    (),
    (0,),
    (),
    (1,),
    (),
    (),
    (6, 2),
    (),
    (0, 3),
    (7, 4, 1),
    (2,),
    (5, 15, 8, 0, 6, 9, 3, 4, 7, 1, 2, 5, 8, 6, 0, 3, 9, 0, 4, 7, 1, 5, 1, 8, 2, 14, 16, 6, 2, 3, 9, 3, 7, 9, 4, 8, 4, 17, 5, 5, 6, 6, 7, 7, 8, 8),
)


def dot_nn(a, b):
    return lax.dot_general(a, b, (((1,), (0,)), ((), ())), preferred_element_type=f32)


def dot_nt(a, b):
    return lax.dot_general(a, b, (((1,), (1,)), ((), ())), preferred_element_type=f32)


def dot_tn(a, b):
    return lax.dot_general(a, b, (((0,), (0,)), ((), ())), preferred_element_type=f32)


def norm_rows(x):
    centred = x - jnp.mean(x, axis=-1, keepdims=True)
    inverse = lax.rsqrt(jnp.mean(centred * centred, axis=-1, keepdims=True) + EPS)
    return centred * inverse, inverse


def norm_rows_back(x, n, inverse):
    first = jnp.mean(x, axis=-1, keepdims=True)
    second = jnp.mean(x * n, axis=-1, keepdims=True)
    return inverse * (x - first - n * second)


def col_sum(x):
    return jnp.sum(x, axis=0, keepdims=True)


class Place:
    def __init__(self):
        narrow, wide = lax.axis_index("narrow"), lax.axis_index("wide")
        self.y, self.c = narrow // 2, narrow % 2
        self.z, self.x = wide // 2, wide % 2
        self.wide = wide
        self.low = wide % 4
        self.half = wide // 4
        self.rows_half = 1 - self.c

    def low_xor(self, i):
        a = self.low
        if i & 1:
            a = a + 1 - 2 * (a % 2)
        if i & 2:
            a = a + 2 - 4 * (a // 2)
        return a

    def home(self, i):
        slot = self.low_xor(i)
        return slot, (2 * self.y + 1 - self.half, 4 * self.c + slot)

    def source(self, i):
        strip = self.low_xor(i)
        return strip, (2 * self.y + self.half, 4 * self.rows_half + strip)

    def core(self):
        return (2 * self.y + 1 - self.c, self.wide)

    def in_plane(self, k):
        x = 1 - self.x if k & 1 else self.x
        y = 1 - self.y if k & 2 else self.y
        return 2 * y + x, (2 * y + self.c, 2 * self.z + x)

    def along_z(self, k):
        z = self.z
        if k & 1:
            z = z + 1 - 2 * (z % 2)
        if k & 2:
            z = z + 2 - 4 * (z // 2)
        return z, (2 * self.y + self.c, 2 * z + self.x)


class Wire:
    def __init__(self, send_sems, recv_sems):
        self.send_sems, self.recv_sems = send_sems, recv_sems
        self.outs, self.ins = 0, 0

    def sender(self):
        self.outs += 1
        return self.send_sems.at[self.outs - 1]

    def receiver(self):
        self.ins += 1
        return self.recv_sems.at[self.ins - 1]

    def copy(self, src, dst, device, sender, receiver):
        pltpu.make_async_remote_copy(
            src_ref=src,
            dst_ref=dst,
            send_sem=sender,
            recv_sem=receiver,
            device_id=device,
            device_id_type=MESH,
        ).start()


def take(semaphore, like):
    pltpu.make_async_copy(like, like, semaphore).wait()


def main_kernel(sizes, names, *refs):
    r = SimpleNamespace(**dict(zip(names, refs, strict=True)))
    R, D, FF = sizes
    M, N = 4 * R, 8 * R
    MB = M // 2
    pairs = D // 128
    here = Place()
    wire = Wire(r.send_sems, r.recv_sems)
    local_sems = r.local_sems
    local_count = [0]

    def local(src, dst):
        made = pltpu.make_async_copy(src, dst, local_sems.at[local_count[0]])
        local_count[0] += 1
        made.start()
        return made

    small_loads = [
        local(r.emb_table, r.emb_table_v),
        local(r.ada_bias, r.ada_bias_v),
        local(r.out_bias, r.out_bias_v),
        local(r.up_bias, r.up_bias_v),
        local(r.down_bias, r.down_bias_v),
    ]
    load_ada = local(r.ada_weight.at[0], r.ada_weight_v)
    qkv_sem = local_sems.at[local_count[0]]
    local_count[0] += 1
    for p in range(pairs):
        for b in range(3):
            pltpu.make_async_copy(
                r.qkv_weight.at[0, :, pl.ds(b * D + p * 128, 128)],
                r.qkv_weight_v.at[p, :, pl.ds(b * 128, 128)],
                qkv_sem,
            ).start()
    load_rest = [
        local(r.out_weight.at[0], r.out_weight_v),
        local(r.up_weight.at[0], r.up_weight_v),
        local(r.down_weight.at[0], r.down_weight_v),
    ]

    barrier = pltpu.get_barrier_semaphore()
    partners = [here.core()]
    partners += [here.home(i)[1] for i in range(4)] + [here.source(i)[1] for i in range(4)]
    partners += [here.in_plane(k)[1] for k in (1, 2, 3)] + [here.along_z(k)[1] for k in (1, 2, 3)]
    for device in partners:
        pl.semaphore_signal(barrier, inc=1, device_id=device, device_id_type=MESH)
    pl.semaphore_wait(barrier, len(partners))

    def send_home(whole, landing, i, sender, receiver):
        place = pl.ds(pl.multiple_of(here.low * R, R), R)
        slot, device = here.home(i)
        wire.copy(whole.at[0, slot], landing.at[place, :], device, sender, receiver)

    tokens_out, tokens_in = wire.sender(), [wire.receiver() for _ in range(4)]
    cotangent_out, cotangent_in = wire.sender(), wire.receiver()
    for i in range(4):
        send_home(r.tokens, r.tokens_v, i, tokens_out, tokens_in[i])

    group, slot = 2 * here.y + here.half, here.low
    item_class = r.lead_class[group, slot]
    live = (slot < r.group_count[group]).astype(f32)
    for made in small_loads:
        made.wait()
    table = r.emb_table_v[...].astype(f32)
    class_col = lax.broadcasted_iota(jnp.int32, (table.shape[0], 1), 0)
    onehot = (class_col == item_class).astype(f32)
    embed = jnp.sum(onehot * table, axis=0, keepdims=True)
    silu = embed * (1.0 / (1.0 + jnp.exp(-embed)))
    high = silu.astype(bf16).astype(f32)
    middle_part = (silu - high).astype(bf16).astype(f32)
    low_part = silu - high - middle_part
    row = lax.broadcasted_iota(jnp.int32, (16, D), 0)
    parts = jnp.where(row == 0, high, jnp.where(row == 1, middle_part, jnp.where(row == 2, low_part, 0.0)))
    load_ada.wait()
    mods = r.mods
    for k in range(6):
        cols = pl.ds(k * D, D)
        mods[k : k + 1, :] = col_sum(
            dot_nn(parts.astype(bf16), r.ada_weight_v[:, cols])
        ) + r.ada_bias_v[:, cols].astype(f32)

    def mod(k):
        return mods[k : k + 1, :]

    acc = r.acc
    acc[...] = jnp.zeros_like(acc)

    take(qkv_sem, r.qkv_weight_v)
    lane = lax.broadcasted_iota(jnp.int32, (R, 128), 1)
    left = lane < HEAD_DIM
    kv, qst = r.kv, r.qst
    kv_out, kv_in = wire.sender(), wire.receiver()
    own = pl.multiple_of(here.rows_half * M, M)
    for i in range(4):
        strip, _ = here.source(i)
        take(tokens_in[i], r.tokens_v.at[pl.ds(0, R), :])
        at = pl.multiple_of(strip * R, R)
        rows = pl.ds(at, R)
        normed, inverse = norm_rows(r.tokens_v[rows, :].astype(f32))
        r.normed[rows, :] = normed
        r.inverse[rows, :] = inverse
        modulated = (normed * (1.0 + mod(1)) + mod(0)).astype(bf16)
        r.modulated[rows, :] = modulated
        kv_rows = pl.ds(pl.multiple_of(own + at, R), R)
        for p in range(pairs):
            projected = dot_nn(modulated, r.qkv_weight_v[p]).astype(bf16)
            kv[p, kv_rows, :] = projected[:, 128:]
            q = projected[:, :128] * HEAD_DIM ** (-0.5)
            zero = jnp.zeros_like(q)
            qst[p, pl.ds(at, R), :] = jnp.where(left, q, zero)
            qst[p, pl.ds(pl.multiple_of(M + at, R), R), :] = jnp.where(left, zero, q)
        wire.copy(kv.at[:, kv_rows, :], kv.at[:, kv_rows, :], here.core(), kv_out, kv_in)
        if i < EARLY_COTANGENT:
            send_home(r.cotangent, r.cotangent_v, i, cotangent_out, cotangent_in)
    take(tokens_out, r.tokens_v)
    for i in range(EARLY_COTANGENT, 4):
        send_home(r.cotangent, r.cotangent_v, i, cotangent_out, cotangent_in)
    take(kv_in, kv.at[:, pl.ds(0, M), :])

    kvt, es, ots = r.kvt, r.es, r.ots
    for p in range(pairs):
        kvt[p] = kv[p].T
    QB = M // 2
    CB = N // 4
    scores = (r.scores_a, r.scores_b)

    def score_rows(j, c):
        p, qb = j // 4, j % 4
        found = dot_nt(kv[p, c * CB : (c + 1) * CB, :128], qst[p, qb * QB : (qb + 1) * QB, :])
        scores[j % 2][c * CB : (c + 1) * CB, :] = found
        return jnp.max(found.reshape(CB // 8, 8, QB), axis=0)

    def mix(j):
        p, qb = j // 4, j % 4
        half = qb // 2 * HEAD_DIM
        mixed = dot_nn(kvt[p, 128 + half : 128 + half + HEAD_DIM, :], es[p, :, qb * QB : (qb + 1) * QB])
        head = slice(p * 128 + half, p * 128 + half + HEAD_DIM)
        ots[head, qb % 2 * QB : (qb % 2 + 1) * QB] = mixed * r.inv_sum[j]

    tops = [score_rows(0, c) for c in range(4)]
    for j in range(4 * pairs):
        p, qb = j // 4, j % 4
        top = jnp.maximum(jnp.maximum(tops[0], tops[1]), jnp.maximum(tops[2], tops[3]))
        top = jnp.max(top, axis=0, keepdims=True)
        tops, sums = [], []
        for c in range(4):
            keys = slice(c * CB, (c + 1) * CB)
            if j + 1 < 4 * pairs:
                tops.append(score_rows(j + 1, c))
            raised = jnp.exp(scores[j % 2][keys, :] - top)
            sums.append(jnp.sum(raised.reshape(CB // 8, 8, QB), axis=0))
            es[p, keys, qb * QB : (qb + 1) * QB] = raised.astype(bf16)
            if c == 0 and j > 0:
                mix(j - 1)
        r.inv_sum[j] = 1.0 / col_sum((sums[0] + sums[1]) + (sums[2] + sums[3]))
    mix(4 * pairs - 1)
    att = r.att
    for p in range(pairs):
        att[:, p * 128 : (p + 1) * 128] = ots[p * 128 : (p + 1) * 128, :].T.astype(bf16)

    part, total, arena = r.part, r.total, r.arena
    used = [0]
    stored = []

    def room(rows):
        start = used[0]
        used[0] += rows
        return start

    def span(start, index, rows):
        return pl.ds(pl.multiple_of(start + index * rows, 16), rows)

    def wide(ref, rows):
        return ref[rows, :].astype(f32)

    units_out = wire.sender()
    units_rows = [0]

    def reduce_unit(base, rows, z_first):
        half = rows // 2

        def move(src, dst, device, receiver):
            units_rows[0] += src.shape[0]
            wire.copy(src, dst, device, units_out, receiver)

        land = room(half)
        block = room(half)
        arrived = wire.receiver()
        move(
            part.at[span(base, 1 - here.c, half), :],
            arena.at[pl.ds(land, half), :],
            here.core(),
            arrived,
        )
        yield
        take(arrived, arena.at[pl.ds(land, half), :])
        arena[pl.ds(block, half), :] = (
            wide(part, span(base, here.c, half)) + wide(arena, pl.ds(land, half))
        ).astype(bf16)
        mine = base + half * here.c
        count = half
        axes = (here.along_z, here.in_plane) if z_first else (here.in_plane, here.along_z)
        for axis in axes:
            count = count // 4
            land = room(3 * count)
            arrived = wire.receiver()
            for k in (3, 2, 1):
                q, device = axis(k)
                move(
                    arena.at[span(block, q, count), :],
                    arena.at[pl.ds(land + (k - 1) * count, count), :],
                    device,
                    arrived,
                )
            yield
            take(arrived, arena.at[pl.ds(land, 3 * count), :])
            me = axis(0)[0]
            summed = wide(arena, span(block, me, count)) + wide(arena, pl.ds(land, count))
            summed = summed + (
                wide(arena, pl.ds(land + count, count)) + wide(arena, pl.ds(land + 2 * count, count))
            )
            mine = mine + count * me
            if axis is axes[0]:
                block = room(count)
                arena[pl.ds(block, count), :] = summed.astype(bf16)
            else:
                total[span(mine, 0, count), :] = summed.astype(bf16)
        for axis in axes[::-1]:
            keep = span(mine, 0, count)
            arrived = wire.receiver()
            for k in (3, 2, 1):
                move(total.at[keep, :], total.at[keep, :], axis(k)[1], arrived)
            yield
            take(arrived, total.at[pl.ds(0, 3 * count), :])
            mine = mine - count * axis(0)[0]
            count = 4 * count
        keep = span(mine, 0, half)
        arrived = wire.receiver()
        move(total.at[keep, :], total.at[keep, :], here.core(), arrived)
        yield
        take(arrived, total.at[pl.ds(0, half), :])
        keep = pl.ds(base, rows)
        stored.append(local(total.at[keep, :], r.grads_o.at[keep, :]))
        yield

    small_out = wire.sender()

    def reduce_small():
        small, small_a, small_b, land, small_sum = (
            r.small,
            r.small_a,
            r.small_b,
            r.land_small,
            r.small_sum,
        )
        here_rows = span(0, here.c, 16)
        arrived = wire.receiver()
        wire.copy(small.at[span(0, 1 - here.c, 16), :], land.at[0], here.core(), small_out, arrived)
        yield
        take(arrived, land.at[0])
        small_a[...] = small[here_rows, :] + land[0]
        arrived = wire.receiver()
        for k in (3, 2, 1):
            wire.copy(small_a, land.at[k], here.in_plane(k)[1], small_out, arrived)
        yield
        take(arrived, land.at[pl.ds(1, 3)])
        small_b[...] = (small_a[...] + land[1]) + (land[2] + land[3])
        arrived = wire.receiver()
        for k in (3, 2, 1):
            wire.copy(small_b, land.at[3 + k], here.along_z(k)[1], small_out, arrived)
        yield
        take(arrived, land.at[pl.ds(4, 3)])
        small_sum[here_rows, :] = (small_b[...] + land[4]) + (land[5] + land[6])
        arrived = wire.receiver()
        wire.copy(
            small_sum.at[here_rows, :], small_sum.at[here_rows, :], here.core(), small_out, arrived
        )
        yield
        take(arrived, small_sum.at[pl.ds(0, 16), :])
        stored.append(local(small_sum, r.small_o))
        yield

    def send_back(stage, landing, i, sender, receiver):
        strip, device = here.source(i)
        rows = pl.ds(pl.multiple_of(strip * R, R), R)
        wire.copy(stage.at[rows, :], landing.at[here.low], device, sender, receiver)
        yield

    out_out, out_in, gtok_out, gtok_in = (
        wire.sender(),
        wire.receiver(),
        wire.sender(),
        wire.receiver(),
    )

    third = 4 * D // 3
    early = 2 * FF // EARLY
    units = [reduce_unit(early * i, early, FORMS[i]) for i in range(EARLY)]
    units += [reduce_unit(2 * FF + third * i, third, FORMS[EARLY + i]) for i in range(3)]
    units.append(reduce_small())
    units += [send_back(r.out_stage, r.out_o, i, out_out, out_in) for i in range(4)]
    units += [send_back(r.gtok_stage, r.gtok_o, i, gtok_out, gtok_in) for i in range(4)]
    plan = iter(PLAN)

    def advance():
        for unit in next(plan):
            next(units[unit])

    for made in load_rest:
        made.wait()
    outw, upw, downw = r.out_weight_v, r.up_weight_v, r.down_weight_v
    chunks = FF // D

    def feed_rows(t):
        rows = slice(t * MB, (t + 1) * MB)
        branch = dot_nn(att[rows, :], outw[...]) + r.out_bias_v[...].astype(f32)
        middle = r.tokens_v[rows, :].astype(f32) + mod(2) * branch
        n, inverse = norm_rows(middle)
        modulated = (n * (1.0 + mod(4)) + mod(3)).astype(bf16)
        r.modulated_m[rows, :] = modulated
        yield
        for ck in range(chunks):
            cols = slice(ck * D, (ck + 1) * D)
            u = dot_nn(modulated, upw[:, cols]) + r.up_bias_v[:, cols].astype(f32)
            phi = 0.5 * (1.0 + lax.erf(u * ROOT_HALF))
            r.activated[rows, cols] = (u * phi).astype(bf16)
            r.slope[rows, cols] = phi + u * (INV_ROOT_2PI * jnp.exp(-0.5 * u * u))
            yield
        feed = dot_nn(r.activated[rows, :], downw[...]) + r.down_bias_v[...].astype(f32)
        r.out_stage[rows, :] = ((middle + mod(5) * feed) * live).astype(bf16)
        yield
        grad = r.cotangent_v[rows, :].astype(f32) * live
        grad_feed = (grad * mod(5)).astype(bf16)
        r.grad_feed[rows, :] = grad_feed
        acc[5:6, :] += col_sum(grad * feed)
        acc[8:9, :] += col_sum(grad_feed.astype(f32))
        yield
        for ck in range(chunks):
            cols = slice(ck * D, (ck + 1) * D)
            grad_up = (dot_nt(grad_feed, downw[cols, :]) * r.slope[rows, cols]).astype(bf16)
            r.grad_up[rows, cols] = grad_up
            acc[9 + ck : 10 + ck, :] += col_sum(grad_up.astype(f32))
            yield
        back = dot_nt(r.grad_up[rows, :], upw[...])
        acc[3:4, :] += col_sum(back)
        acc[4:5, :] += col_sum(back * n)
        grad_middle = grad + norm_rows_back(back * (1.0 + mod(4)), n, inverse)
        r.grad_middle[rows, :] = grad_middle
        acc[2:3, :] += col_sum(grad_middle * branch)
        grad_branch = (grad_middle * mod(2)).astype(bf16)
        r.grad_branch[rows, :] = grad_branch
        acc[13:14, :] += col_sum(grad_branch.astype(f32))
        yield
        r.grad_att[rows, :] = dot_nt(grad_branch, outw[...]).astype(bf16)

    blocks = [feed_rows(0), feed_rows(1)]
    for _ in range(chunks + 2):
        for block in blocks:
            next(block)
    advance()
    take(cotangent_in, r.cotangent_v)
    for _ in range(chunks + 3):
        for block in blocks:
            next(block, None)

    started = 0
    for ck in range(2 * chunks):
        rows = slice(ck * D, (ck + 1) * D)
        cols = slice(ck % chunks * D, (ck % chunks + 1) * D)
        if ck < chunks:
            found = dot_tn(r.activated[:, cols], r.grad_feed[...])
        else:
            found = dot_tn(r.modulated_m[...], r.grad_up[:, cols])
        part[rows, :] = found.astype(bf16)
        while started < EARLY and (started + 1) * early <= (ck + 1) * D:
            next(units[started])
            started += 1
        advance()
    part[2 * FF : 2 * FF + D, :] = dot_tn(att[...], r.grad_branch[...]).astype(bf16)

    gat, qgt = r.gat, r.qgt
    for p in range(pairs):
        gat[p * 128 : (p + 1) * 128, :] = r.grad_att[:, p * 128 : (p + 1) * 128].T.astype(f32)
    zero_half = jnp.zeros((HEAD_DIM, QB), bf16)
    gst, gstt, deltas, dkv = r.gst, r.gstt, r.deltas, r.dkv
    dss = (r.dss_a, r.dss_b)
    for p in range(pairs):
        for qb in range(4):
            half = qb // 2
            head = slice(p * 128 + half * HEAD_DIM, p * 128 + (half + 1) * HEAD_DIM)
            queries = slice(qb % 2 * QB, (qb % 2 + 1) * QB)
            scaled = gat[head, queries] * r.inv_sum[4 * p + qb]
            deltas[4 * p + qb] = col_sum(scaled * ots[head, queries])
            scaled = scaled.astype(bf16)
            filled = [scaled, zero_half] if half == 0 else [zero_half, scaled]
            gstt[p, :, qb * QB : (qb + 1) * QB] = jnp.concatenate(filled, axis=0)
        gst[p] = gstt[p].T
    other = pl.multiple_of((1 - here.rows_half) * M, M)
    dkv_out, dkv_in = wire.sender(), [wire.receiver() for _ in range(pairs)]
    gp = r.grad_projected

    def finish_pair(p):
        gp[p, :, 0:128] = qgt[p * 128 : (p + 1) * 128, :].T.astype(bf16)
        take(dkv_in[p], r.land_dkv.at[p])
        gp[p, :, 128:384] = (
            dkv[p, pl.ds(own, M), :].astype(f32) + r.land_dkv[p].astype(f32)
        ).astype(bf16)
        rows = slice(2 * FF + (p + 1) * D, 2 * FF + (p + 2) * D)
        part[rows, :] = dot_tn(r.modulated[...], gp[p]).astype(bf16)
        next(units[EARLY + p])
        advance()

    def grad_values(p, c):
        keys = slice(c * CB, (c + 1) * CB)
        dkv[p, keys, 128:256] = dot_nn(es[p, keys, :], gst[p]).astype(bf16)

    def grad_keys(p, c):
        keys = slice(c * CB, (c + 1) * CB)
        dkv[p, keys, 0:128] = dot_nn(dss[p % 2][keys, :], qst[p]).astype(bf16)
        if c == 3:
            wire.copy(
                dkv.at[p, pl.ds(other, M), :], r.land_dkv.at[p], here.core(), dkv_out, dkv_in[p]
            )

    def grad_queries(p, qb):
        half = qb // 2 * HEAD_DIM
        head = slice(p * 128 + half, p * 128 + half + HEAD_DIM)
        found = dot_nn(kvt[p, half : half + HEAD_DIM, :], dss[p % 2][:, qb * QB : (qb + 1) * QB])
        qgt[head, qb % 2 * QB : (qb % 2 + 1) * QB] = found * HEAD_DIM ** (-0.5)

    later = []
    advance()
    for p in range(pairs):
        for qb in range(4):
            queries = slice(qb * QB, (qb + 1) * QB)
            for c in range(4):
                keys = slice(c * CB, (c + 1) * CB)
                slope = dot_nn(kv[p, keys, 128:], gstt[p, :, queries])
                dss[p % 2][keys, queries] = (
                    es[p, keys, queries].astype(f32) * (slope - deltas[4 * p + qb])
                ).astype(bf16)
                if later:
                    later.pop(0)()
            later.append(functools.partial(grad_queries, p, qb))
            if qb == 0:
                later += [functools.partial(grad_values, p, k) for k in range(4)]
            if qb == 3:
                later += [functools.partial(grad_keys, p, k) for k in range(4)]
            advance()
            if p > 0 and qb == 3:
                finish_pair(p - 1)
    for made in later:
        made()
    advance()
    finish_pair(pairs - 1)

    for t in range(2):
        rows = slice(t * MB, (t + 1) * MB)
        back = dot_nt(gp[0, rows, :], r.qkv_weight_v[0])
        for p in range(1, pairs):
            back = back + dot_nt(gp[p, rows, :], r.qkv_weight_v[p])
        n = r.normed[rows, :]
        acc[0:1, :] += col_sum(back)
        acc[1:2, :] += col_sum(back * n)
        grad = r.grad_middle[rows, :] + norm_rows_back(
            back * (1.0 + mod(1)), n, r.inverse[rows, :]
        )
        r.gtok_stage[rows, :] = grad.astype(bf16)
        if t == 0:
            advance()

    small = r.small
    for k in range(6):
        small[4 * k : 4 * k + 4, :] = onehot * acc[k : k + 1, :]
    small[24:32, :] = acc[8:16, :]
    next(units[EARLY + 3])
    advance()
    take(out_in, r.out_stage)
    take(gtok_in, r.gtok_stage)
    take(cotangent_out, r.cotangent_v)
    take(kv_out, kv.at[:, pl.ds(0, M), :])
    take(dkv_out, r.land_dkv)
    take(out_out, r.out_stage)
    take(gtok_out, r.gtok_stage)
    take(small_out, r.land_small)
    take(units_out, arena.at[pl.ds(0, units_rows[0]), :])
    for made in stored:
        made.wait()


def last_kernel(sizes, names, *refs):
    r = SimpleNamespace(**dict(zip(names, refs, strict=True)))
    D, FF = sizes
    rows_total = 2 * FF + 4 * D
    sems = r.sems
    count = [0]

    def local(src, dst):
        made = pltpu.make_async_copy(src, dst, sems.at[count[0]])
        count[0] += 1
        made.start()
        return made

    grads_in = []
    for k in range(rows_total // D):
        rows = pl.ds(k * D, D)
        grads_in.append(local(r.grads_i.at[rows, :], r.grads_v.at[rows, :]))
        if k == 0:
            small_in = local(r.small_i, r.small_i_v)
            table_in = local(r.emb_table, r.emb_table_v)
    ada_in = local(r.ada_weight, r.ada_weight_v)
    out_in = local(r.out_i, r.out_i_v)
    gtok_in = local(r.gtok_i, r.gtok_i_v)
    outs = []
    grads = r.grads_v

    def widen(k, target):
        grads_in[k].wait()
        target[...] = grads[k * D : (k + 1) * D, :].astype(f32)

    for k in range(FF // D):
        rows = pl.ds(k * D, D)
        widen(k, r.gdown_v.at[rows, :])
        outs.append(local(r.gdown_v.at[rows, :], r.gdown.at[0, rows, :]))
    for k in range(FF // D):
        cols = pl.ds(k * D, D)
        widen(FF // D + k, r.gup_v.at[k])
        outs.append(local(r.gup_v.at[k], r.gup.at[0, :, cols]))
    first = 2 * FF // D
    widen(first, r.gout_v)
    outs.append(local(r.gout_v, r.gout.at[0]))
    for p in range(D // 128):
        grads_in[first + 1 + p].wait()
        rows = slice((first + 1 + p) * D, (first + 2 + p) * D)
        for k in range(3):
            cols = slice(k * D + p * 128, k * D + (p + 1) * 128)
            r.gqkv_v[:, cols] = grads[rows, k * 128 : (k + 1) * 128].astype(f32)
    outs.append(local(r.gqkv_v, r.gqkv.at[0]))
    for arrived, given, wide_v, result in (
        (out_in, r.out_i_v, r.out_v, r.out),
        (gtok_in, r.gtok_i_v, r.gtok_v, r.gtok),
    ):
        arrived.wait()
        for s in range(4):
            wide_v[s] = given[s].astype(f32)
        outs.append(local(wide_v, result.at[0]))
    small_in.wait()
    table_in.wait()
    small = r.small_i_v
    table = r.emb_table_v[...].astype(f32)
    sigmoid = 1.0 / (1.0 + jnp.exp(-table))
    silu = table * sigmoid

    def split(v):
        high = v.astype(bf16).astype(f32)
        return high, v - high

    silu_high, silu_low = split(silu)
    zero = jnp.zeros_like(silu)
    left = jnp.concatenate([silu_high, silu_low, silu_high, zero], axis=0).astype(bf16)
    grad_silu = jnp.zeros_like(table)
    ada_in.wait()
    for k in range(6):
        cols = slice(k * D, (k + 1) * D)
        block = small[4 * k : 4 * k + 4, :]
        high, low = split(block)
        right = jnp.concatenate([high, high, low, zero], axis=0).astype(bf16)
        r.gada_v[k] = dot_tn(left, right)
        outs.append(local(r.gada_v.at[k], r.gada.at[0, :, pl.ds(k * D, D)]))
        r.gada_b[:, cols] = col_sum(block)
        both = jnp.concatenate([high, low, zero, zero], axis=0).astype(bf16)
        found = dot_nt(both, r.ada_weight_v[0, :, cols])
        grad_silu = grad_silu + found[0:4, :] + found[4:8, :]
    r.table_o[...] = grad_silu * (sigmoid + table * sigmoid * (1.0 - sigmoid))
    r.down_b[...] = small[24:25, :]
    for k in range(FF // D):
        r.up_b[:, k * D : (k + 1) * D] = small[25 + k : 26 + k, :]
    r.out_b[...] = small[29:30, :]
    for made in outs:
        made.wait()


def fast_body(*args):
    tokens, emb_table, ada_weight, up_weight = args[0], args[2], args[3], args[8]
    R, D = tokens.shape[2:]
    FF = up_weight.shape[2]
    M, N = 4 * R, 8 * R
    pairs = D // 128
    total_rows = 2 * FF + 4 * D
    vmem = pl.BlockSpec(memory_space=pltpu.VMEM)
    smem = pl.BlockSpec(memory_space=pltpu.SMEM)
    anywhere = pl.BlockSpec(memory_space=pl.ANY)
    arguments = dict(
        tokens=anywhere,
        cotangent=anywhere,
        emb_table=anywhere,
        ada_weight=anywhere,
        ada_bias=anywhere,
        qkv_weight=anywhere,
        out_weight=anywhere,
        out_bias=anywhere,
        up_weight=anywhere,
        up_bias=anywhere,
        down_weight=anywhere,
        down_bias=anywhere,
        lead_class=smem,
        group_count=smem,
    )
    scratch = dict(
        emb_table_v=pltpu.VMEM(emb_table.shape, bf16),
        ada_bias_v=pltpu.VMEM((1, 6 * D), bf16),
        out_bias_v=pltpu.VMEM((1, D), bf16),
        up_bias_v=pltpu.VMEM((1, FF), bf16),
        down_bias_v=pltpu.VMEM((1, D), bf16),
        ada_weight_v=pltpu.VMEM((D, 6 * D), bf16),
        qkv_weight_v=pltpu.VMEM((pairs, D, 384), bf16),
        out_weight_v=pltpu.VMEM((D, D), bf16),
        up_weight_v=pltpu.VMEM((D, FF), bf16),
        down_weight_v=pltpu.VMEM((FF, D), bf16),
        tokens_v=pltpu.VMEM((M, D), bf16),
        cotangent_v=pltpu.VMEM((M, D), bf16),
        mods=pltpu.VMEM((8, D), f32),
        acc=pltpu.VMEM((16, D), f32),
        normed=pltpu.VMEM((M, D), f32),
        inverse=pltpu.VMEM((M, 1), f32),
        modulated=pltpu.VMEM((M, D), bf16),
        kv=pltpu.VMEM((pairs, N, 256), bf16),
        kvt=pltpu.VMEM((pairs, 256, N), bf16),
        qst=pltpu.VMEM((pairs, 2 * M, 128), bf16),
        es=pltpu.VMEM((pairs, N, 2 * M), bf16),
        inv_sum=pltpu.VMEM((4 * pairs, 1, M // 2), f32),
        ots=pltpu.VMEM((D, M), f32),
        att=pltpu.VMEM((M, D), bf16),
        modulated_m=pltpu.VMEM((M, D), bf16),
        activated=pltpu.VMEM((M, FF), bf16),
        slope=pltpu.VMEM((M, FF), f32),
        out_stage=pltpu.VMEM((M, D), bf16),
        grad_feed=pltpu.VMEM((M, D), bf16),
        grad_up=pltpu.VMEM((M, FF), bf16),
        grad_middle=pltpu.VMEM((M, D), f32),
        grad_branch=pltpu.VMEM((M, D), bf16),
        grad_att=pltpu.VMEM((M, D), bf16),
        gat=pltpu.VMEM((D, M), f32),
        qgt=pltpu.VMEM((D, M), f32),
        gst=pltpu.VMEM((pairs, 2 * M, 128), bf16),
        gstt=pltpu.VMEM((pairs, 128, 2 * M), bf16),
        deltas=pltpu.VMEM((4 * pairs, 1, M // 2), f32),
        dss_a=pltpu.VMEM((N, 2 * M), bf16),
        dss_b=pltpu.VMEM((N, 2 * M), bf16),
        scores_a=pltpu.VMEM((N, M // 2), f32),
        scores_b=pltpu.VMEM((N, M // 2), f32),
        dkv=pltpu.VMEM((pairs, N, 256), bf16),
        land_dkv=pltpu.VMEM((pairs, M, 256), bf16),
        grad_projected=pltpu.VMEM((pairs, M, 384), bf16),
        gtok_stage=pltpu.VMEM((M, D), bf16),
        part=pltpu.VMEM((total_rows, D), bf16),
        total=pltpu.VMEM((total_rows, D), bf16),
        arena=pltpu.VMEM((2 * total_rows, D), bf16),
        small=pltpu.VMEM((32, D), f32),
        small_a=pltpu.VMEM((16, D), f32),
        small_b=pltpu.VMEM((16, D), f32),
        small_sum=pltpu.VMEM((32, D), f32),
        land_small=pltpu.VMEM((8, 16, D), f32),
        send_sems=pltpu.SemaphoreType.DMA((8,)),
        recv_sems=pltpu.SemaphoreType.DMA((69,)),
        local_sems=pltpu.SemaphoreType.DMA((20,)),
    )
    mids = dict(
        out_o=jax.ShapeDtypeStruct((4, R, D), bf16),
        gtok_o=jax.ShapeDtypeStruct((4, R, D), bf16),
        grads_o=jax.ShapeDtypeStruct((total_rows, D), bf16),
        small_o=jax.ShapeDtypeStruct((32, D), f32),
    )
    names = tuple(arguments) + tuple(mids) + tuple(scratch)
    middle = pl.pallas_call(
        functools.partial(main_kernel, (R, D, FF), names),
        out_shape=tuple(mids.values()),
        in_specs=list(arguments.values()),
        out_specs=(anywhere,) * 4,
        scratch_shapes=list(scratch.values()),
        compiler_params=pltpu.CompilerParams(
            collective_id=0, has_side_effects=True, vmem_limit_bytes=60 << 20
        ),
        name="block_forward_backward",
    )(*args)
    outs = dict(
        out=((1, 4, R, D), anywhere),
        gtok=((1, 4, R, D), anywhere),
        table_o=((emb_table.shape[0], D), vmem),
        gada=((1, D, 6 * D), anywhere),
        gada_b=((1, 6 * D), vmem),
        gqkv=((1, D, 3 * D), anywhere),
        gout=((1, D, D), anywhere),
        out_b=((1, D), vmem),
        gup=((1, D, FF), anywhere),
        up_b=((1, FF), vmem),
        gdown=((1, FF, D), anywhere),
        down_b=((1, D), vmem),
    )
    ins = dict(
        out_i=anywhere,
        gtok_i=anywhere,
        grads_i=anywhere,
        small_i=anywhere,
        emb_table=anywhere,
        ada_weight=anywhere,
    )
    scratch = dict(
        out_i_v=pltpu.VMEM((4, R, D), bf16),
        gtok_i_v=pltpu.VMEM((4, R, D), bf16),
        grads_v=pltpu.VMEM((total_rows, D), bf16),
        emb_table_v=pltpu.VMEM(emb_table.shape, bf16),
        small_i_v=pltpu.VMEM((32, D), f32),
        ada_weight_v=pltpu.VMEM((1, D, 6 * D), bf16),
        out_v=pltpu.VMEM((4, R, D), f32),
        gtok_v=pltpu.VMEM((4, R, D), f32),
        gada_v=pltpu.VMEM((6, D, D), f32),
        gqkv_v=pltpu.VMEM((D, 3 * D), f32),
        gout_v=pltpu.VMEM((D, D), f32),
        gup_v=pltpu.VMEM((FF // D, D, D), f32),
        gdown_v=pltpu.VMEM((FF, D), f32),
        sems=pltpu.SemaphoreType.DMA((40,)),
    )
    names = tuple(ins) + tuple(outs) + tuple(scratch)
    return pl.pallas_call(
        functools.partial(last_kernel, (D, FF), names),
        out_shape=tuple(jax.ShapeDtypeStruct(size, f32) for size, _ in outs.values()),
        in_specs=list(ins.values()),
        out_specs=tuple(space for _, space in outs.values()),
        scratch_shapes=list(scratch.values()),
        compiler_params=pltpu.CompilerParams(vmem_limit_bytes=60 << 20),
        name="widen_and_embed",
    )(*middle, emb_table, ada_weight)


HEADS = 6
LAYERS = 1

epsilon = 1e-06
highest = lax.Precision.HIGHEST
root_half = 0.7071067811865476
inverse_root_two_pi = 0.3989422804014327


def layer_norm(values):
    average = jnp.mean(values, axis=-1, keepdims=True)
    centred = values - average
    variance = jnp.mean(centred * centred, axis=-1, keepdims=True)
    inverse = lax.rsqrt(variance + epsilon)
    return (centred * inverse, inverse)


def norm_back(grad_normed, normed, inverse):
    first = jnp.mean(grad_normed, axis=-1, keepdims=True)
    second = jnp.mean(grad_normed * normed, axis=-1, keepdims=True)
    return inverse * (grad_normed - first - normed * second)


def gelu_exact(values):
    return 0.5 * values * (1.0 + jax.scipy.special.erf(values * root_half))


def gelu_slope(values):
    return 0.5 * (
        1.0 + jax.scipy.special.erf(values * root_half)
    ) + values * inverse_root_two_pi * jnp.exp(-0.5 * values * values)


def split_heads(values):
    return values.reshape(values.shape[0], values.shape[1], HEADS, values.shape[2] // HEADS)


def modulation_parts(silu_rows, ada_w, ada_b):
    mods = jnp.dot(silu_rows, ada_w.astype(jnp.float32), precision=highest) + ada_b.astype(
        jnp.float32
    )
    mods = mods.reshape(mods.shape[0], 6, -1)
    return [mods[:, index][:, None, :] for index in range(6)]


def before_attention(hidden, parts, qkv_low):
    normed, inverse = layer_norm(hidden)
    modulated = (normed * (1.0 + parts[1]) + parts[0]).astype(jnp.bfloat16)
    projected = jnp.einsum(
        "spd,df->spf", modulated, qkv_low, preferred_element_type=jnp.float32
    ).astype(jnp.bfloat16)
    width = hidden.shape[2]
    return (
        normed,
        inverse,
        modulated,
        projected[..., :width],
        projected[..., width : 2 * width],
        projected[..., 2 * width :],
    )


def after_attention(hidden, attended, parts, later):
    out_w, out_b, up_w, up_b, down_w, down_b = later
    branch = jnp.einsum(
        "spd,de->spe", attended, out_w, preferred_element_type=jnp.float32
    ) + out_b.astype(jnp.float32)
    middle = hidden + parts[2] * branch
    normed, inverse = layer_norm(middle)
    modulated = (normed * (1.0 + parts[4]) + parts[3]).astype(jnp.bfloat16)
    upward = jnp.einsum(
        "spd,df->spf", modulated, up_w, preferred_element_type=jnp.float32
    ) + up_b.astype(jnp.float32)
    activated = gelu_exact(upward).astype(jnp.bfloat16)
    feed = jnp.einsum(
        "spf,fd->spd", activated, down_w, preferred_element_type=jnp.float32
    ) + down_b.astype(jnp.float32)
    return (
        middle + parts[5] * feed,
        (branch, middle, normed, inverse, modulated, upward, activated, feed),
    )


def attention_forward(queries, keys_here, values_here):
    slots, rows, width = queries.shape
    scale = HEAD_DIM ** (-0.5)
    query_heads = split_heads(queries)
    running_max = jnp.full((slots, rows, HEADS), -1e30, jnp.float32)
    key_heads = split_heads(lax.all_gather(keys_here, "wide", axis=1, tiled=True))
    value_heads = split_heads(lax.all_gather(values_here, "wide", axis=1, tiled=True))
    scores = (
        jnp.einsum("sphe,snhe->sphn", query_heads, key_heads, preferred_element_type=jnp.float32)
        * scale
    )
    new_max = jnp.maximum(running_max, jnp.max(scores, axis=-1))
    weights = jnp.exp(scores - new_max[..., None])
    new_sum = jnp.sum(weights, axis=-1)
    mixed = jnp.einsum(
        "sphn,snhe->sphe",
        weights.astype(jnp.bfloat16),
        value_heads,
        preferred_element_type=jnp.float32,
    )
    total = mixed
    running_max, running_sum, total = (new_max, new_sum, total.reshape(slots, rows, width))
    attended = (
        (split_heads(total) / running_sum[..., None])
        .reshape(slots, rows, width)
        .astype(jnp.bfloat16)
    )
    return (attended, running_max + jnp.log(running_sum), None)


def attention_backward(queries, keys_here, values_here, grad_attended, log_total, delta):
    slots, rows, width = queries.shape
    scale = HEAD_DIM ** (-0.5)
    query_heads = split_heads(queries)
    grad_heads = split_heads(grad_attended)
    piece = (
        lax.all_gather(keys_here, "wide", axis=1, tiled=True),
        lax.all_gather(values_here, "wide", axis=1, tiled=True),
    )
    toward_key_heads = split_heads(piece[0])
    toward_value_heads = split_heads(piece[1])
    scores = (
        jnp.einsum(
            "sphe,snhe->sphn", query_heads, toward_key_heads, preferred_element_type=jnp.float32
        )
        * scale
    )
    probs = jnp.exp(scores - log_total[..., None])
    slope = jnp.einsum(
        "sphe,snhe->sphn", grad_heads, toward_value_heads, preferred_element_type=jnp.float32
    )
    grad_scores = (probs * (slope - delta[..., None])).astype(jnp.bfloat16)
    grad_queries = (
        jnp.einsum(
            "sphn,snhe->sphe", grad_scores, toward_key_heads, preferred_element_type=jnp.float32
        )
        * scale
    ).reshape(slots, rows, width)
    stats = (
        lax.all_gather(log_total, "wide", axis=1, tiled=True),
        lax.all_gather(delta, "wide", axis=1, tiled=True),
    )
    key_heads = split_heads(keys_here)
    value_heads = split_heads(values_here)
    piece = (
        lax.all_gather(queries, "wide", axis=1, tiled=True),
        lax.all_gather(grad_attended, "wide", axis=1, tiled=True),
    )
    piece_queries = split_heads(piece[0])
    piece_grads = split_heads(piece[1])
    piece_total = stats[0]
    piece_delta = stats[1]
    scores = (
        jnp.einsum("snhe,sphe->snhp", piece_queries, key_heads, preferred_element_type=jnp.float32)
        * scale
    )
    probs = jnp.exp(scores - piece_total[..., None])
    slope = jnp.einsum(
        "snhe,sphe->snhp", piece_grads, value_heads, preferred_element_type=jnp.float32
    )
    grad_scores = (probs * (slope - piece_delta[..., None])).astype(jnp.bfloat16)
    keys_total = (
        jnp.einsum(
            "snhp,snhe->sphe", grad_scores, piece_queries, preferred_element_type=jnp.float32
        )
        * scale
    ).reshape(slots, rows, width)
    values_total = jnp.einsum(
        "snhp,snhe->sphe",
        probs.astype(jnp.bfloat16),
        piece_grads,
        preferred_element_type=jnp.float32,
    ).reshape(slots, rows, width)
    return (
        grad_queries.astype(jnp.bfloat16),
        keys_total.astype(jnp.bfloat16),
        values_total.astype(jnp.bfloat16),
    )


def body(
    tokens,
    cotangent,
    emb_table,
    ada_weight,
    ada_bias,
    qkv_weight,
    out_weight,
    out_bias,
    up_weight,
    up_bias,
    down_weight,
    down_bias,
    lead_class,
    group_count,
):
    group = lax.axis_index("narrow")
    slot_count = tokens.shape[1]
    width = tokens.shape[3]
    table = emb_table.astype(jnp.float32)
    class_range = jnp.arange(table.shape[0], dtype=jnp.int32)
    classes_here = lax.dynamic_index_in_dim(lead_class, group, 0, keepdims=False)
    count_here = lax.dynamic_index_in_dim(group_count, group, 0, keepdims=False)
    live = (jnp.arange(slot_count, dtype=jnp.int32) < count_here).astype(jnp.float32)[:, None, None]
    embed_here = jnp.dot(
        (classes_here[:, None] == class_range[None, :]).astype(jnp.float32),
        table,
        precision=highest,
    )
    silu_here = embed_here * jax.nn.sigmoid(embed_here)
    hidden = tokens[0].astype(jnp.float32)
    layer = 0
    parts = modulation_parts(silu_here, ada_weight[layer], ada_bias[layer])
    later = (
        out_weight[layer],
        out_bias[layer],
        up_weight[layer],
        up_bias[layer],
        down_weight[layer],
        down_bias[layer],
    )
    normed, inverse, modulated, queries, keys_here, values_here = before_attention(
        hidden, parts, qkv_weight[layer]
    )
    attended, log_total, whole_pair = attention_forward(queries, keys_here, values_here)
    kept = [(hidden, parts, attended, log_total, whole_pair)]
    hidden, unused = after_attention(hidden, attended, parts, later)
    output = hidden * live
    grad = cotangent[0].astype(jnp.float32) * live
    grad_mods = [None] * LAYERS
    weight_grads = [None] * LAYERS
    for layer in reversed(range(LAYERS)):
        layer_input, parts, attended, log_total, whole_pair = kept[layer]
        later = (
            out_weight[layer],
            out_bias[layer],
            up_weight[layer],
            up_bias[layer],
            down_weight[layer],
            down_bias[layer],
        )
        normed, inverse, modulated, queries, keys_here, values_here = before_attention(
            layer_input, parts, qkv_weight[layer]
        )
        unused, inner = after_attention(layer_input, attended, parts, later)
        branch, middle, normed_mlp, inverse_mlp, modulated_mlp, upward, activated, feed = inner
        grad_feed = (grad * parts[5]).astype(jnp.bfloat16)
        grad_gate_mlp = jnp.sum(grad * feed, axis=1)
        grad_down_w = jnp.einsum(
            "spf,spd->fd", activated, grad_feed, preferred_element_type=jnp.float32
        )
        grad_down_b = jnp.sum(grad_feed.astype(jnp.float32), axis=(0, 1))
        grad_upward = (
            jnp.einsum(
                "spd,fd->spf", grad_feed, down_weight[layer], preferred_element_type=jnp.float32
            )
            * gelu_slope(upward)
        ).astype(jnp.bfloat16)
        grad_up_w = jnp.einsum(
            "spd,spf->df", modulated_mlp, grad_upward, preferred_element_type=jnp.float32
        )
        grad_up_b = jnp.sum(grad_upward.astype(jnp.float32), axis=(0, 1))
        grad_mod_mlp = jnp.einsum(
            "spf,df->spd", grad_upward, up_weight[layer], preferred_element_type=jnp.float32
        )
        grad_shift_mlp = jnp.sum(grad_mod_mlp, axis=1)
        grad_scale_mlp = jnp.sum(grad_mod_mlp * normed_mlp, axis=1)
        grad_middle = grad + norm_back(grad_mod_mlp * (1.0 + parts[4]), normed_mlp, inverse_mlp)
        grad_gate_attn = jnp.sum(grad_middle * branch, axis=1)
        grad_branch = (grad_middle * parts[2]).astype(jnp.bfloat16)
        grad_out_w = jnp.einsum(
            "spd,spe->de", attended, grad_branch, preferred_element_type=jnp.float32
        )
        grad_out_b = jnp.sum(grad_branch.astype(jnp.float32), axis=(0, 1))
        grad_attended = jnp.einsum(
            "spe,de->spd", grad_branch, out_weight[layer], preferred_element_type=jnp.float32
        ).astype(jnp.bfloat16)
        delta = jnp.sum(
            split_heads(grad_attended.astype(jnp.float32) * attended.astype(jnp.float32)), axis=-1
        )
        grad_queries, grad_keys, grad_values = attention_backward(
            queries, keys_here, values_here, grad_attended, log_total, delta
        )
        grad_projected = jnp.concatenate([grad_queries, grad_keys, grad_values], axis=-1)
        grad_qkv_w = jnp.einsum(
            "spd,spf->df", modulated, grad_projected, preferred_element_type=jnp.float32
        )
        grad_mod_attn = jnp.einsum(
            "spf,df->spd", grad_projected, qkv_weight[layer], preferred_element_type=jnp.float32
        )
        grad_shift_attn = jnp.sum(grad_mod_attn, axis=1)
        grad_scale_attn = jnp.sum(grad_mod_attn * normed, axis=1)
        grad = grad_middle + norm_back(grad_mod_attn * (1.0 + parts[1]), normed, inverse)
        local_mods = jnp.stack(
            [
                grad_shift_attn,
                grad_scale_attn,
                grad_gate_attn,
                grad_shift_mlp,
                grad_scale_mlp,
                grad_gate_mlp,
            ],
            axis=1,
        ).reshape(slot_count, 6 * width)
        grad_mods[layer] = lax.psum(local_mods, "wide")
        weight_grads[layer] = lax.psum(
            (grad_qkv_w, grad_out_w, grad_out_b, grad_up_w, grad_up_b, grad_down_w, grad_down_b),
            ("narrow", "wide"),
        )
    all_mods = lax.all_gather(
        jnp.stack(grad_mods, axis=0).astype(jnp.bfloat16), "narrow", axis=1, tiled=True
    ).astype(jnp.float32)
    all_classes = lead_class.reshape(-1)
    onehot_all = (all_classes[:, None] == class_range[None, :]).astype(jnp.float32)
    embed_all = jnp.dot(onehot_all, table, precision=highest)
    sigmoid_all = jax.nn.sigmoid(embed_all)
    silu_all = embed_all * sigmoid_all
    grad_ada_w = jnp.einsum("id,lie->lde", silu_all, all_mods, precision=highest)
    grad_ada_b = jnp.sum(all_mods, axis=1)
    grad_silu = jnp.einsum(
        "lie,lde->id", all_mods, ada_weight.astype(jnp.float32), precision=highest
    )
    grad_embed = grad_silu * (sigmoid_all + embed_all * sigmoid_all * (1.0 - sigmoid_all))
    grad_table = jnp.dot(onehot_all.T, grad_embed, precision=highest)
    stacked = [jnp.stack([weight_grads[0][member]], axis=0) for member in range(7)]
    return (
        output[None],
        grad[None],
        grad_table,
        grad_ada_w,
        grad_ada_b,
        stacked[0],
        stacked[1],
        stacked[2],
        stacked[3],
        stacked[4],
        stacked[5],
        stacked[6],
    )


def solution(mesh):
    in_specs = (
        P("narrow", None, "wide", None),
        P("narrow", None, "wide", None),
        P(),
        P(),
        P(),
        P(),
        P(),
        P(),
        P(),
        P(),
        P(),
        P(),
        P(),
        P(),
    )
    out_specs = (
        P("narrow", None, "wide", None),
        P("narrow", None, "wide", None),
        P(),
        P(),
        P(),
        P(),
        P(),
        P(),
        P(),
        P(),
        P(),
        P(),
    )
    by_item = dict(mesh.shape) == {"narrow": 4, "wide": 8}
    return jax.shard_map(fast_body if by_item else body, mesh=mesh, in_specs=in_specs, out_specs=out_specs, check_vma=False)
```

```python
import functools
from types import SimpleNamespace

import jax
import jax.numpy as jnp
from jax import lax
from jax.experimental import pallas as pl
from jax.experimental.pallas import tpu as pltpu
from jax.sharding import PartitionSpec as P

MESH = pl.DeviceIdType.MESH
f32, bf16 = jnp.float32, jnp.bfloat16
EPS = 1e-06
ROOT_HALF = 0.7071067811865476
INV_ROOT_2PI = 0.3989422804014327
HEAD_DIM = 64
EARLY_COTANGENT = 0
EARLY = 6
FORMS = (False, False, False, False, False, False, False, False, False)
PLAN = (
    (12, 13, 11),
    (),
    (),
    (),
    (),
    (),
    (),
    (0,),
    (1, 2),
    (3, 4),
    (5,),
    (),
    (),
    (),
    (),
    (),
    (0,),
    (),
    (1,),
    (),
    (),
    (2, 6),
    (),
    (0, 3),
    (),
    (4, 7, 2, 5, 1),
    (),
    (8, 6, 0, 3, 9, 4, 7, 2, 5, 8, 1, 6, 0, 3, 9, 4, 0, 7, 2, 5, 8, 14, 17, 2, 1, 6, 1, 10, 3, 9, 7, 3, 9, 4, 8, 16, 4, 15, 5, 5, 6, 6, 7, 7, 8, 8),
)


def dot_nn(a, b):
    return lax.dot_general(a, b, (((1,), (0,)), ((), ())), preferred_element_type=f32)


def dot_nt(a, b):
    return lax.dot_general(a, b, (((1,), (1,)), ((), ())), preferred_element_type=f32)


def dot_tn(a, b):
    return lax.dot_general(a, b, (((0,), (0,)), ((), ())), preferred_element_type=f32)


def norm_rows(x):
    centred = x - jnp.mean(x, axis=-1, keepdims=True)
    inverse = lax.rsqrt(jnp.mean(centred * centred, axis=-1, keepdims=True) + EPS)
    return centred * inverse, inverse


def norm_rows_back(x, n, inverse):
    first = jnp.mean(x, axis=-1, keepdims=True)
    second = jnp.mean(x * n, axis=-1, keepdims=True)
    return inverse * (x - first - n * second)


def col_sum(x):
    return jnp.sum(x, axis=0, keepdims=True)


class Place:
    def __init__(self):
        narrow, wide = lax.axis_index("narrow"), lax.axis_index("wide")
        self.y, self.c = narrow // 2, narrow % 2
        self.z, self.x = wide // 2, wide % 2
        self.wide = wide
        self.low = wide % 4
        self.half = wide // 4
        self.rows_half = 1 - self.c

    def low_xor(self, i):
        a = self.low
        if i & 1:
            a = a + 1 - 2 * (a % 2)
        if i & 2:
            a = a + 2 - 4 * (a // 2)
        return a

    def home(self, i):
        slot = self.low_xor(i)
        return slot, (2 * self.y + 1 - self.half, 4 * self.c + slot)

    def source(self, i):
        strip = self.low_xor(i)
        return strip, (2 * self.y + self.half, 4 * self.rows_half + strip)

    def core(self):
        return (2 * self.y + 1 - self.c, self.wide)

    def in_plane(self, k):
        x = 1 - self.x if k & 1 else self.x
        y = 1 - self.y if k & 2 else self.y
        return 2 * y + x, (2 * y + self.c, 2 * self.z + x)

    def along_z(self, k):
        z = self.z
        if k & 1:
            z = z + 1 - 2 * (z % 2)
        if k & 2:
            z = z + 2 - 4 * (z // 2)
        return z, (2 * self.y + self.c, 2 * z + self.x)


class Wire:
    def __init__(self, send_sems, recv_sems):
        self.send_sems, self.recv_sems = send_sems, recv_sems
        self.outs, self.ins = 0, 0

    def sender(self):
        self.outs += 1
        return self.send_sems.at[self.outs - 1]

    def receiver(self):
        self.ins += 1
        return self.recv_sems.at[self.ins - 1]

    def copy(self, src, dst, device, sender, receiver):
        pltpu.make_async_remote_copy(
            src_ref=src,
            dst_ref=dst,
            send_sem=sender,
            recv_sem=receiver,
            device_id=device,
            device_id_type=MESH,
        ).start()


def take(semaphore, like):
    pltpu.make_async_copy(like, like, semaphore).wait()


def main_kernel(sizes, names, *refs):
    r = SimpleNamespace(**dict(zip(names, refs, strict=True)))
    R, D, FF = sizes
    M, N = 4 * R, 8 * R
    MB = M // 2
    pairs = D // 128
    here = Place()
    wire = Wire(r.send_sems, r.recv_sems)
    local_sems = r.local_sems
    local_count = [0]

    def local(src, dst):
        made = pltpu.make_async_copy(src, dst, local_sems.at[local_count[0]])
        local_count[0] += 1
        made.start()
        return made

    small_loads = [
        local(r.emb_table, r.emb_table_v),
        local(r.ada_bias, r.ada_bias_v),
        local(r.out_bias, r.out_bias_v),
        local(r.up_bias, r.up_bias_v),
        local(r.down_bias, r.down_bias_v),
    ]
    load_ada = local(r.ada_weight.at[0], r.ada_weight_v)
    qkv_sem = local_sems.at[local_count[0]]
    local_count[0] += 1
    for p in range(pairs):
        for b in range(3):
            pltpu.make_async_copy(
                r.qkv_weight.at[0, :, pl.ds(b * D + p * 128, 128)],
                r.qkv_weight_v.at[p, :, pl.ds(b * 128, 128)],
                qkv_sem,
            ).start()
    load_rest = [
        local(r.out_weight.at[0], r.out_weight_v),
        local(r.up_weight.at[0], r.up_weight_v),
        local(r.down_weight.at[0], r.down_weight_v),
    ]

    barrier = pltpu.get_barrier_semaphore()
    partners = [here.core()]
    partners += [here.home(i)[1] for i in range(4)] + [here.source(i)[1] for i in range(4)]
    partners += [here.in_plane(k)[1] for k in (1, 2, 3)] + [here.along_z(k)[1] for k in (1, 2, 3)]
    for device in partners:
        pl.semaphore_signal(barrier, inc=1, device_id=device, device_id_type=MESH)
    pl.semaphore_wait(barrier, len(partners))

    def send_home(whole, landing, i, sender, receiver):
        place = pl.ds(pl.multiple_of(here.low * R, R), R)
        slot, device = here.home(i)
        wire.copy(whole.at[0, slot], landing.at[place, :], device, sender, receiver)

    tokens_out, tokens_in = wire.sender(), [wire.receiver() for _ in range(4)]
    cotangent_out, cotangent_in = wire.sender(), wire.receiver()
    for i in range(4):
        send_home(r.tokens, r.tokens_v, i, tokens_out, tokens_in[i])

    group, slot = 2 * here.y + here.half, here.low
    item_class = r.lead_class[group, slot]
    live = (slot < r.group_count[group]).astype(f32)
    for made in small_loads:
        made.wait()
    table = r.emb_table_v[...].astype(f32)
    class_col = lax.broadcasted_iota(jnp.int32, (table.shape[0], 1), 0)
    onehot = (class_col == item_class).astype(f32)
    embed = jnp.sum(onehot * table, axis=0, keepdims=True)
    silu = embed * (1.0 / (1.0 + jnp.exp(-embed)))
    high = silu.astype(bf16).astype(f32)
    middle_part = (silu - high).astype(bf16).astype(f32)
    low_part = silu - high - middle_part
    row = lax.broadcasted_iota(jnp.int32, (16, D), 0)
    parts = jnp.where(row == 0, high, jnp.where(row == 1, middle_part, jnp.where(row == 2, low_part, 0.0)))
    load_ada.wait()
    mods = r.mods
    for k in range(6):
        cols = pl.ds(k * D, D)
        mods[k : k + 1, :] = col_sum(
            dot_nn(parts.astype(bf16), r.ada_weight_v[:, cols])
        ) + r.ada_bias_v[:, cols].astype(f32)

    def mod(k):
        return mods[k : k + 1, :]

    acc = r.acc
    acc[...] = jnp.zeros_like(acc)

    take(qkv_sem, r.qkv_weight_v)
    lane = lax.broadcasted_iota(jnp.int32, (R, 128), 1)
    left = lane < HEAD_DIM
    kv, qst = r.kv, r.qst
    kv_out, kv_in = wire.sender(), wire.receiver()
    own = pl.multiple_of(here.rows_half * M, M)
    for i in range(4):
        strip, _ = here.source(i)
        take(tokens_in[i], r.tokens_v.at[pl.ds(0, R), :])
        at = pl.multiple_of(strip * R, R)
        rows = pl.ds(at, R)
        normed, inverse = norm_rows(r.tokens_v[rows, :].astype(f32))
        r.normed[rows, :] = normed
        r.inverse[rows, :] = inverse
        modulated = (normed * (1.0 + mod(1)) + mod(0)).astype(bf16)
        r.modulated[rows, :] = modulated
        kv_rows = pl.ds(pl.multiple_of(own + at, R), R)
        for p in range(pairs):
            projected = dot_nn(modulated, r.qkv_weight_v[p]).astype(bf16)
            kv[p, kv_rows, :] = projected[:, 128:]
            q = projected[:, :128] * HEAD_DIM ** (-0.5)
            zero = jnp.zeros_like(q)
            qst[p, pl.ds(at, R), :] = jnp.where(left, q, zero)
            qst[p, pl.ds(pl.multiple_of(M + at, R), R), :] = jnp.where(left, zero, q)
        wire.copy(kv.at[:, kv_rows, :], kv.at[:, kv_rows, :], here.core(), kv_out, kv_in)
        if i < EARLY_COTANGENT:
            send_home(r.cotangent, r.cotangent_v, i, cotangent_out, cotangent_in)
    take(tokens_out, r.tokens_v)
    for i in range(EARLY_COTANGENT, 4):
        send_home(r.cotangent, r.cotangent_v, i, cotangent_out, cotangent_in)
    take(kv_in, kv.at[:, pl.ds(0, M), :])

    kvt, es, ots = r.kvt, r.es, r.ots
    for p in range(pairs):
        kvt[p] = kv[p].T
    QB = M // 2
    CB = N // 4
    scores = (r.scores_a, r.scores_b)

    def score_rows(j, c):
        p, qb = j // 4, j % 4
        found = dot_nt(kv[p, c * CB : (c + 1) * CB, :128], qst[p, qb * QB : (qb + 1) * QB, :])
        scores[j % 2][c * CB : (c + 1) * CB, :] = found
        return jnp.max(found.reshape(CB // 8, 8, QB), axis=0)

    def mix(j):
        p, qb = j // 4, j % 4
        half = qb // 2 * HEAD_DIM
        mixed = dot_nn(kvt[p, 128 + half : 128 + half + HEAD_DIM, :], es[p, :, qb * QB : (qb + 1) * QB])
        head = slice(p * 128 + half, p * 128 + half + HEAD_DIM)
        ots[head, qb % 2 * QB : (qb % 2 + 1) * QB] = mixed * r.inv_sum[j]

    tops = [score_rows(0, c) for c in range(4)]
    for j in range(4 * pairs):
        p, qb = j // 4, j % 4
        top = jnp.maximum(jnp.maximum(tops[0], tops[1]), jnp.maximum(tops[2], tops[3]))
        top = jnp.max(top, axis=0, keepdims=True)
        tops, sums = [], []
        for c in range(4):
            keys = slice(c * CB, (c + 1) * CB)
            if j + 1 < 4 * pairs:
                tops.append(score_rows(j + 1, c))
            raised = jnp.exp(scores[j % 2][keys, :] - top)
            sums.append(jnp.sum(raised.reshape(CB // 8, 8, QB), axis=0))
            es[p, keys, qb * QB : (qb + 1) * QB] = raised.astype(bf16)
            if c == 0 and j > 0:
                mix(j - 1)
        r.inv_sum[j] = 1.0 / col_sum((sums[0] + sums[1]) + (sums[2] + sums[3]))
    mix(4 * pairs - 1)
    att = r.att
    for p in range(pairs):
        att[:, p * 128 : (p + 1) * 128] = ots[p * 128 : (p + 1) * 128, :].T.astype(bf16)

    part, total, arena = r.part, r.grads_o, r.arena
    used = [0]

    def room(rows):
        start = used[0]
        used[0] += rows
        return start

    def span(start, index, rows):
        return pl.ds(pl.multiple_of(start + index * rows, 16), rows)

    def wide(ref, rows):
        return ref[rows, :].astype(f32)

    units_out = wire.sender()
    units_rows = [0]

    def reduce_unit(base, rows, z_first):
        half = rows // 2

        def move(src, dst, device, receiver):
            units_rows[0] += src.shape[0]
            wire.copy(src, dst, device, units_out, receiver)

        land = room(half)
        block = room(half)
        arrived = wire.receiver()
        move(
            part.at[span(base, 1 - here.c, half), :],
            arena.at[pl.ds(land, half), :],
            here.core(),
            arrived,
        )
        yield
        take(arrived, arena.at[pl.ds(land, half), :])
        arena[pl.ds(block, half), :] = (
            wide(part, span(base, here.c, half)) + wide(arena, pl.ds(land, half))
        ).astype(bf16)
        mine = base + half * here.c
        count = half
        axes = (here.along_z, here.in_plane) if z_first else (here.in_plane, here.along_z)
        for axis in axes:
            count = count // 4
            land = room(3 * count)
            arrived = wire.receiver()
            for k in (3, 2, 1):
                q, device = axis(k)
                move(
                    arena.at[span(block, q, count), :],
                    arena.at[pl.ds(land + (k - 1) * count, count), :],
                    device,
                    arrived,
                )
            yield
            take(arrived, arena.at[pl.ds(land, 3 * count), :])
            me = axis(0)[0]
            summed = wide(arena, span(block, me, count)) + wide(arena, pl.ds(land, count))
            summed = summed + (
                wide(arena, pl.ds(land + count, count)) + wide(arena, pl.ds(land + 2 * count, count))
            )
            mine = mine + count * me
            if axis is axes[0]:
                block = room(count)
                arena[pl.ds(block, count), :] = summed.astype(bf16)
            else:
                total[span(mine, 0, count), :] = summed.astype(bf16)
        for axis in axes[::-1]:
            keep = span(mine, 0, count)
            arrived = wire.receiver()
            for k in (3, 2, 1):
                move(total.at[keep, :], total.at[keep, :], axis(k)[1], arrived)
            yield
            take(arrived, total.at[pl.ds(0, 3 * count), :])
            mine = mine - count * axis(0)[0]
            count = 4 * count
        keep = span(mine, 0, half)
        arrived = wire.receiver()
        move(total.at[keep, :], total.at[keep, :], here.core(), arrived)
        yield
        take(arrived, total.at[pl.ds(0, half), :])
        yield

    small_out = wire.sender()

    def reduce_small():
        small, small_a, small_b, land, small_sum = (
            r.small,
            r.small_a,
            r.small_b,
            r.land_small,
            r.small_o,
        )
        here_rows = span(0, here.c, 16)
        arrived = wire.receiver()
        wire.copy(small.at[span(0, 1 - here.c, 16), :], land.at[0], here.core(), small_out, arrived)
        yield
        take(arrived, land.at[0])
        small_a[...] = small[here_rows, :] + land[0]
        arrived = wire.receiver()
        for k in (3, 2, 1):
            wire.copy(small_a, land.at[k], here.in_plane(k)[1], small_out, arrived)
        yield
        take(arrived, land.at[pl.ds(1, 3)])
        small_b[...] = (small_a[...] + land[1]) + (land[2] + land[3])
        arrived = wire.receiver()
        for k in (3, 2, 1):
            wire.copy(small_b, land.at[3 + k], here.along_z(k)[1], small_out, arrived)
        yield
        take(arrived, land.at[pl.ds(4, 3)])
        small_sum[here_rows, :] = (small_b[...] + land[4]) + (land[5] + land[6])
        arrived = wire.receiver()
        wire.copy(
            small_sum.at[here_rows, :], small_sum.at[here_rows, :], here.core(), small_out, arrived
        )
        yield
        take(arrived, small_sum.at[pl.ds(0, 16), :])
        yield

    def send_back(stage, landing, i, sender, receiver):
        strip, device = here.source(i)
        rows = pl.ds(pl.multiple_of(strip * R, R), R)
        wire.copy(stage.at[rows, :], landing.at[here.low], device, sender, receiver)
        yield

    out_out, out_in, gtok_out, gtok_in = (
        wire.sender(),
        wire.receiver(),
        wire.sender(),
        wire.receiver(),
    )

    third = 4 * D // 3
    early = 2 * FF // EARLY
    units = [reduce_unit(early * i, early, FORMS[i]) for i in range(EARLY)]
    units += [reduce_unit(2 * FF + third * i, third, FORMS[EARLY + i]) for i in range(3)]
    units.append(reduce_small())
    units += [send_back(r.out_stage, r.out_o, i, out_out, out_in) for i in range(4)]
    units += [send_back(r.gtok_stage, r.gtok_o, i, gtok_out, gtok_in) for i in range(4)]
    plan = iter(PLAN)

    def advance():
        for unit in next(plan):
            next(units[unit])

    for made in load_rest:
        made.wait()
    outw, upw, downw = r.out_weight_v, r.up_weight_v, r.down_weight_v
    chunks = FF // D

    def feed_rows(t):
        rows = slice(t * MB, (t + 1) * MB)
        branch = dot_nn(att[rows, :], outw[...]) + r.out_bias_v[...].astype(f32)
        middle = r.tokens_v[rows, :].astype(f32) + mod(2) * branch
        n, inverse = norm_rows(middle)
        modulated = (n * (1.0 + mod(4)) + mod(3)).astype(bf16)
        r.modulated_m[rows, :] = modulated
        yield
        for ck in range(chunks):
            cols = slice(ck * D, (ck + 1) * D)
            u = dot_nn(modulated, upw[:, cols]) + r.up_bias_v[:, cols].astype(f32)
            phi = 0.5 * (1.0 + lax.erf(u * ROOT_HALF))
            r.activated[rows, cols] = (u * phi).astype(bf16)
            r.slope[rows, cols] = phi + u * (INV_ROOT_2PI * jnp.exp(-0.5 * u * u))
            yield
        feed = dot_nn(r.activated[rows, :], downw[...]) + r.down_bias_v[...].astype(f32)
        r.out_stage[rows, :] = ((middle + mod(5) * feed) * live).astype(bf16)
        yield
        grad = r.cotangent_v[rows, :].astype(f32) * live
        grad_feed = (grad * mod(5)).astype(bf16)
        r.grad_feed[rows, :] = grad_feed
        acc[5:6, :] += col_sum(grad * feed)
        acc[8:9, :] += col_sum(grad_feed.astype(f32))
        yield
        for ck in range(chunks):
            cols = slice(ck * D, (ck + 1) * D)
            grad_up = (dot_nt(grad_feed, downw[cols, :]) * r.slope[rows, cols]).astype(bf16)
            r.grad_up[rows, cols] = grad_up
            acc[9 + ck : 10 + ck, :] += col_sum(grad_up.astype(f32))
            yield
        back = dot_nt(r.grad_up[rows, :], upw[...])
        acc[3:4, :] += col_sum(back)
        acc[4:5, :] += col_sum(back * n)
        grad_middle = grad + norm_rows_back(back * (1.0 + mod(4)), n, inverse)
        r.grad_middle[rows, :] = grad_middle
        acc[2:3, :] += col_sum(grad_middle * branch)
        grad_branch = (grad_middle * mod(2)).astype(bf16)
        r.grad_branch[rows, :] = grad_branch
        acc[13:14, :] += col_sum(grad_branch.astype(f32))
        yield
        r.grad_att[rows, :] = dot_nt(grad_branch, outw[...]).astype(bf16)

    blocks = [feed_rows(0), feed_rows(1)]
    for _ in range(chunks + 2):
        for block in blocks:
            next(block)
    take(cotangent_in, r.cotangent_v)
    advance()
    for _ in range(chunks + 3):
        for block in blocks:
            next(block, None)

    started = 0
    for ck in range(2 * chunks):
        rows = slice(ck * D, (ck + 1) * D)
        cols = slice(ck % chunks * D, (ck % chunks + 1) * D)
        if ck < chunks:
            found = dot_tn(r.activated[:, cols], r.grad_feed[...])
        else:
            found = dot_tn(r.modulated_m[...], r.grad_up[:, cols])
        part[rows, :] = found.astype(bf16)
        while started < EARLY and (started + 1) * early <= (ck + 1) * D:
            next(units[started])
            started += 1
        advance()
    part[2 * FF : 2 * FF + D, :] = dot_tn(att[...], r.grad_branch[...]).astype(bf16)

    gat, qgt = r.gat, r.qgt
    for p in range(pairs):
        gat[p * 128 : (p + 1) * 128, :] = r.grad_att[:, p * 128 : (p + 1) * 128].T.astype(f32)
    zero_half = jnp.zeros((HEAD_DIM, QB), bf16)
    gst, gstt, deltas, dkv = r.gst, r.gstt, r.deltas, r.dkv
    dss = (r.dss_a, r.dss_b)
    for p in range(pairs):
        for qb in range(4):
            half = qb // 2
            head = slice(p * 128 + half * HEAD_DIM, p * 128 + (half + 1) * HEAD_DIM)
            queries = slice(qb % 2 * QB, (qb % 2 + 1) * QB)
            scaled = gat[head, queries] * r.inv_sum[4 * p + qb]
            deltas[4 * p + qb] = col_sum(scaled * ots[head, queries])
            scaled = scaled.astype(bf16)
            filled = [scaled, zero_half] if half == 0 else [zero_half, scaled]
            gstt[p, :, qb * QB : (qb + 1) * QB] = jnp.concatenate(filled, axis=0)
        gst[p] = gstt[p].T
    other = pl.multiple_of((1 - here.rows_half) * M, M)
    dkv_out, dkv_in = wire.sender(), [wire.receiver() for _ in range(pairs)]
    gp = r.grad_projected

    def finish_pair(p):
        gp[p, :, 0:128] = qgt[p * 128 : (p + 1) * 128, :].T.astype(bf16)
        take(dkv_in[p], r.land_dkv.at[p])
        gp[p, :, 128:384] = (
            dkv[p, pl.ds(own, M), :].astype(f32) + r.land_dkv[p].astype(f32)
        ).astype(bf16)
        rows = slice(2 * FF + (p + 1) * D, 2 * FF + (p + 2) * D)
        part[rows, :] = dot_tn(r.modulated[...], gp[p]).astype(bf16)
        next(units[EARLY + p])
        advance()

    def grad_values(p, c):
        keys = slice(c * CB, (c + 1) * CB)
        dkv[p, keys, 128:256] = dot_nn(es[p, keys, :], gst[p]).astype(bf16)

    def grad_keys(p, c):
        keys = slice(c * CB, (c + 1) * CB)
        dkv[p, keys, 0:128] = dot_nn(dss[p % 2][keys, :], qst[p]).astype(bf16)
        if c == 3:
            wire.copy(
                dkv.at[p, pl.ds(other, M), :], r.land_dkv.at[p], here.core(), dkv_out, dkv_in[p]
            )

    def grad_queries(p, qb):
        half = qb // 2 * HEAD_DIM
        head = slice(p * 128 + half, p * 128 + half + HEAD_DIM)
        found = dot_nn(kvt[p, half : half + HEAD_DIM, :], dss[p % 2][:, qb * QB : (qb + 1) * QB])
        qgt[head, qb % 2 * QB : (qb % 2 + 1) * QB] = found * HEAD_DIM ** (-0.5)

    later = []
    advance()
    for p in range(pairs):
        for qb in range(4):
            queries = slice(qb * QB, (qb + 1) * QB)
            for c in range(4):
                keys = slice(c * CB, (c + 1) * CB)
                slope = dot_nn(kv[p, keys, 128:], gstt[p, :, queries])
                dss[p % 2][keys, queries] = (
                    es[p, keys, queries].astype(f32) * (slope - deltas[4 * p + qb])
                ).astype(bf16)
                if later:
                    later.pop(0)()
            later.append(functools.partial(grad_queries, p, qb))
            if qb == 0:
                later += [functools.partial(grad_values, p, k) for k in range(4)]
            if qb == 3:
                later += [functools.partial(grad_keys, p, k) for k in range(4)]
            advance()
            if p > 0 and qb == 3:
                finish_pair(p - 1)
    for made in later:
        made()
    advance()
    finish_pair(pairs - 1)

    for t in range(2):
        rows = slice(t * MB, (t + 1) * MB)
        back = dot_nt(gp[0, rows, :], r.qkv_weight_v[0])
        for p in range(1, pairs):
            back = back + dot_nt(gp[p, rows, :], r.qkv_weight_v[p])
        n = r.normed[rows, :]
        acc[0:1, :] += col_sum(back)
        acc[1:2, :] += col_sum(back * n)
        grad = r.grad_middle[rows, :] + norm_rows_back(
            back * (1.0 + mod(1)), n, r.inverse[rows, :]
        )
        r.gtok_stage[rows, :] = grad.astype(bf16)
        if t == 0:
            advance()

    small = r.small
    for k in range(6):
        small[4 * k : 4 * k + 4, :] = onehot * acc[k : k + 1, :]
    small[24:32, :] = acc[8:16, :]
    next(units[EARLY + 3])
    advance()
    take(out_in, r.out_o)
    take(gtok_in, r.gtok_o)
    take(cotangent_out, r.cotangent_v)
    take(kv_out, kv.at[:, pl.ds(0, M), :])
    take(dkv_out, r.land_dkv)
    take(out_out, r.out_stage)
    take(gtok_out, r.gtok_stage)
    take(small_out, r.land_small)
    take(units_out, arena.at[pl.ds(0, units_rows[0]), :])


def last_kernel(sizes, names, *refs):
    r = SimpleNamespace(**dict(zip(names, refs, strict=True)))
    D, FF = sizes
    sems = r.sems
    count = [0]

    def local(src, dst):
        made = pltpu.make_async_copy(src, dst, sems.at[count[0]])
        count[0] += 1
        made.start()
        return made

    table_in = local(r.emb_table, r.emb_table_v)
    ada_in = local(r.ada_weight, r.ada_weight_v)
    outs = []
    grads = r.grads_i

    def widen(k, target):
        target[...] = grads[k * D : (k + 1) * D, :].astype(f32)

    for k in range(FF // D):
        rows = pl.ds(k * D, D)
        widen(k, r.gdown_v.at[rows, :])
        outs.append(local(r.gdown_v.at[rows, :], r.gdown.at[0, rows, :]))
    for k in range(FF // D):
        cols = pl.ds(k * D, D)
        widen(FF // D + k, r.gup_v.at[k])
        outs.append(local(r.gup_v.at[k], r.gup.at[0, :, cols]))
    first = 2 * FF // D
    widen(first, r.gout_v)
    outs.append(local(r.gout_v, r.gout.at[0]))
    for p in range(D // 128):
        rows = slice((first + 1 + p) * D, (first + 2 + p) * D)
        for k in range(3):
            cols = slice(k * D + p * 128, k * D + (p + 1) * 128)
            r.gqkv_v[:, cols] = grads[rows, k * 128 : (k + 1) * 128].astype(f32)
    outs.append(local(r.gqkv_v, r.gqkv.at[0]))
    for given, wide_v, result in ((r.out_i, r.out_v, r.out), (r.gtok_i, r.gtok_v, r.gtok)):
        for s in range(4):
            wide_v[s] = given[s].astype(f32)
        outs.append(local(wide_v, result.at[0]))
    table_in.wait()
    small = r.small_i
    table = r.emb_table_v[...].astype(f32)
    sigmoid = 1.0 / (1.0 + jnp.exp(-table))
    silu = table * sigmoid

    def split(v):
        high = v.astype(bf16).astype(f32)
        return high, v - high

    silu_high, silu_low = split(silu)
    zero = jnp.zeros_like(silu)
    left = jnp.concatenate([silu_high, silu_low, silu_high, zero], axis=0).astype(bf16)
    grad_silu = jnp.zeros_like(table)
    ada_in.wait()
    for k in range(6):
        cols = slice(k * D, (k + 1) * D)
        block = small[4 * k : 4 * k + 4, :]
        high, low = split(block)
        right = jnp.concatenate([high, high, low, zero], axis=0).astype(bf16)
        r.gada_v[k] = dot_tn(left, right)
        outs.append(local(r.gada_v.at[k], r.gada.at[0, :, pl.ds(k * D, D)]))
        r.gada_b[:, cols] = col_sum(block)
        both = jnp.concatenate([high, low, zero, zero], axis=0).astype(bf16)
        found = dot_nt(both, r.ada_weight_v[0, :, cols])
        grad_silu = grad_silu + found[0:4, :] + found[4:8, :]
    r.table_o[...] = grad_silu * (sigmoid + table * sigmoid * (1.0 - sigmoid))
    r.down_b[...] = small[24:25, :]
    for k in range(FF // D):
        r.up_b[:, k * D : (k + 1) * D] = small[25 + k : 26 + k, :]
    r.out_b[...] = small[29:30, :]
    for made in outs:
        made.wait()


def fast_body(*args):
    tokens, emb_table, ada_weight, up_weight = args[0], args[2], args[3], args[8]
    R, D = tokens.shape[2:]
    FF = up_weight.shape[2]
    M, N = 4 * R, 8 * R
    pairs = D // 128
    total_rows = 2 * FF + 4 * D
    vmem = pl.BlockSpec(memory_space=pltpu.VMEM)
    smem = pl.BlockSpec(memory_space=pltpu.SMEM)
    anywhere = pl.BlockSpec(memory_space=pl.ANY)
    arguments = dict(
        tokens=anywhere,
        cotangent=anywhere,
        emb_table=anywhere,
        ada_weight=anywhere,
        ada_bias=anywhere,
        qkv_weight=anywhere,
        out_weight=anywhere,
        out_bias=anywhere,
        up_weight=anywhere,
        up_bias=anywhere,
        down_weight=anywhere,
        down_bias=anywhere,
        lead_class=smem,
        group_count=smem,
    )
    scratch = dict(
        emb_table_v=pltpu.VMEM(emb_table.shape, bf16),
        ada_bias_v=pltpu.VMEM((1, 6 * D), bf16),
        out_bias_v=pltpu.VMEM((1, D), bf16),
        up_bias_v=pltpu.VMEM((1, FF), bf16),
        down_bias_v=pltpu.VMEM((1, D), bf16),
        ada_weight_v=pltpu.VMEM((D, 6 * D), bf16),
        qkv_weight_v=pltpu.VMEM((pairs, D, 384), bf16),
        out_weight_v=pltpu.VMEM((D, D), bf16),
        up_weight_v=pltpu.VMEM((D, FF), bf16),
        down_weight_v=pltpu.VMEM((FF, D), bf16),
        tokens_v=pltpu.VMEM((M, D), bf16),
        cotangent_v=pltpu.VMEM((M, D), bf16),
        mods=pltpu.VMEM((8, D), f32),
        acc=pltpu.VMEM((16, D), f32),
        normed=pltpu.VMEM((M, D), f32),
        inverse=pltpu.VMEM((M, 1), f32),
        modulated=pltpu.VMEM((M, D), bf16),
        kv=pltpu.VMEM((pairs, N, 256), bf16),
        kvt=pltpu.VMEM((pairs, 256, N), bf16),
        qst=pltpu.VMEM((pairs, 2 * M, 128), bf16),
        es=pltpu.VMEM((pairs, N, 2 * M), bf16),
        inv_sum=pltpu.VMEM((4 * pairs, 1, M // 2), f32),
        ots=pltpu.VMEM((D, M), f32),
        att=pltpu.VMEM((M, D), bf16),
        modulated_m=pltpu.VMEM((M, D), bf16),
        activated=pltpu.VMEM((M, FF), bf16),
        slope=pltpu.VMEM((M, FF), f32),
        out_stage=pltpu.VMEM((M, D), bf16),
        grad_feed=pltpu.VMEM((M, D), bf16),
        grad_up=pltpu.VMEM((M, FF), bf16),
        grad_middle=pltpu.VMEM((M, D), f32),
        grad_branch=pltpu.VMEM((M, D), bf16),
        grad_att=pltpu.VMEM((M, D), bf16),
        gat=pltpu.VMEM((D, M), f32),
        qgt=pltpu.VMEM((D, M), f32),
        gst=pltpu.VMEM((pairs, 2 * M, 128), bf16),
        gstt=pltpu.VMEM((pairs, 128, 2 * M), bf16),
        deltas=pltpu.VMEM((4 * pairs, 1, M // 2), f32),
        dss_a=pltpu.VMEM((N, 2 * M), bf16),
        dss_b=pltpu.VMEM((N, 2 * M), bf16),
        scores_a=pltpu.VMEM((N, M // 2), f32),
        scores_b=pltpu.VMEM((N, M // 2), f32),
        dkv=pltpu.VMEM((pairs, N, 256), bf16),
        land_dkv=pltpu.VMEM((pairs, M, 256), bf16),
        grad_projected=pltpu.VMEM((pairs, M, 384), bf16),
        gtok_stage=pltpu.VMEM((M, D), bf16),
        part=pltpu.VMEM((total_rows, D), bf16),
        arena=pltpu.VMEM((2 * total_rows, D), bf16),
        small=pltpu.VMEM((32, D), f32),
        small_a=pltpu.VMEM((16, D), f32),
        small_b=pltpu.VMEM((16, D), f32),
        land_small=pltpu.VMEM((8, 16, D), f32),
        send_sems=pltpu.SemaphoreType.DMA((8,)),
        recv_sems=pltpu.SemaphoreType.DMA((69,)),
        local_sems=pltpu.SemaphoreType.DMA((20,)),
    )
    mids = dict(
        out_o=pltpu.VMEM((4, R, D), bf16),
        gtok_o=pltpu.VMEM((4, R, D), bf16),
        grads_o=pltpu.VMEM((total_rows, D), bf16),
        small_o=pltpu.VMEM((32, D), f32),
    )
    names = tuple(arguments) + tuple(mids) + tuple(scratch)
    middle = pl.pallas_call(
        functools.partial(main_kernel, (R, D, FF), names),
        out_shape=tuple(mids.values()),
        in_specs=list(arguments.values()),
        out_specs=(vmem,) * 4,
        scratch_shapes=list(scratch.values()),
        compiler_params=pltpu.CompilerParams(
            collective_id=0, has_side_effects=True, vmem_limit_bytes=58 << 20
        ),
        name="block_forward_backward",
    )(*args)
    outs = dict(
        out=((1, 4, R, D), anywhere),
        gtok=((1, 4, R, D), anywhere),
        table_o=((emb_table.shape[0], D), vmem),
        gada=((1, D, 6 * D), anywhere),
        gada_b=((1, 6 * D), vmem),
        gqkv=((1, D, 3 * D), anywhere),
        gout=((1, D, D), anywhere),
        out_b=((1, D), vmem),
        gup=((1, D, FF), anywhere),
        up_b=((1, FF), vmem),
        gdown=((1, FF, D), anywhere),
        down_b=((1, D), vmem),
    )
    ins = dict(
        out_i=vmem,
        gtok_i=vmem,
        grads_i=vmem,
        small_i=vmem,
        emb_table=anywhere,
        ada_weight=anywhere,
    )
    scratch = dict(
        emb_table_v=pltpu.VMEM(emb_table.shape, bf16),
        ada_weight_v=pltpu.VMEM((1, D, 6 * D), bf16),
        out_v=pltpu.VMEM((4, R, D), f32),
        gtok_v=pltpu.VMEM((4, R, D), f32),
        gada_v=pltpu.VMEM((6, D, D), f32),
        gqkv_v=pltpu.VMEM((D, 3 * D), f32),
        gout_v=pltpu.VMEM((D, D), f32),
        gup_v=pltpu.VMEM((FF // D, D, D), f32),
        gdown_v=pltpu.VMEM((FF, D), f32),
        sems=pltpu.SemaphoreType.DMA((40,)),
    )
    names = tuple(ins) + tuple(outs) + tuple(scratch)
    return pl.pallas_call(
        functools.partial(last_kernel, (D, FF), names),
        out_shape=tuple(jax.ShapeDtypeStruct(size, f32) for size, _ in outs.values()),
        in_specs=list(ins.values()),
        out_specs=tuple(space for _, space in outs.values()),
        scratch_shapes=list(scratch.values()),
        compiler_params=pltpu.CompilerParams(vmem_limit_bytes=40 << 20),
        name="widen_and_embed",
    )(*middle, emb_table, ada_weight)


HEADS = 6
LAYERS = 1

epsilon = 1e-06
highest = lax.Precision.HIGHEST
root_half = 0.7071067811865476
inverse_root_two_pi = 0.3989422804014327


def layer_norm(values):
    average = jnp.mean(values, axis=-1, keepdims=True)
    centred = values - average
    variance = jnp.mean(centred * centred, axis=-1, keepdims=True)
    inverse = lax.rsqrt(variance + epsilon)
    return (centred * inverse, inverse)


def norm_back(grad_normed, normed, inverse):
    first = jnp.mean(grad_normed, axis=-1, keepdims=True)
    second = jnp.mean(grad_normed * normed, axis=-1, keepdims=True)
    return inverse * (grad_normed - first - normed * second)


def gelu_exact(values):
    return 0.5 * values * (1.0 + jax.scipy.special.erf(values * root_half))


def gelu_slope(values):
    return 0.5 * (
        1.0 + jax.scipy.special.erf(values * root_half)
    ) + values * inverse_root_two_pi * jnp.exp(-0.5 * values * values)


def split_heads(values):
    return values.reshape(values.shape[0], values.shape[1], HEADS, values.shape[2] // HEADS)


def modulation_parts(silu_rows, ada_w, ada_b):
    mods = jnp.dot(silu_rows, ada_w.astype(jnp.float32), precision=highest) + ada_b.astype(
        jnp.float32
    )
    mods = mods.reshape(mods.shape[0], 6, -1)
    return [mods[:, index][:, None, :] for index in range(6)]


def before_attention(hidden, parts, qkv_low):
    normed, inverse = layer_norm(hidden)
    modulated = (normed * (1.0 + parts[1]) + parts[0]).astype(jnp.bfloat16)
    projected = jnp.einsum(
        "spd,df->spf", modulated, qkv_low, preferred_element_type=jnp.float32
    ).astype(jnp.bfloat16)
    width = hidden.shape[2]
    return (
        normed,
        inverse,
        modulated,
        projected[..., :width],
        projected[..., width : 2 * width],
        projected[..., 2 * width :],
    )


def after_attention(hidden, attended, parts, later):
    out_w, out_b, up_w, up_b, down_w, down_b = later
    branch = jnp.einsum(
        "spd,de->spe", attended, out_w, preferred_element_type=jnp.float32
    ) + out_b.astype(jnp.float32)
    middle = hidden + parts[2] * branch
    normed, inverse = layer_norm(middle)
    modulated = (normed * (1.0 + parts[4]) + parts[3]).astype(jnp.bfloat16)
    upward = jnp.einsum(
        "spd,df->spf", modulated, up_w, preferred_element_type=jnp.float32
    ) + up_b.astype(jnp.float32)
    activated = gelu_exact(upward).astype(jnp.bfloat16)
    feed = jnp.einsum(
        "spf,fd->spd", activated, down_w, preferred_element_type=jnp.float32
    ) + down_b.astype(jnp.float32)
    return (
        middle + parts[5] * feed,
        (branch, middle, normed, inverse, modulated, upward, activated, feed),
    )


def attention_forward(queries, keys_here, values_here):
    slots, rows, width = queries.shape
    scale = HEAD_DIM ** (-0.5)
    query_heads = split_heads(queries)
    running_max = jnp.full((slots, rows, HEADS), -1e30, jnp.float32)
    key_heads = split_heads(lax.all_gather(keys_here, "wide", axis=1, tiled=True))
    value_heads = split_heads(lax.all_gather(values_here, "wide", axis=1, tiled=True))
    scores = (
        jnp.einsum("sphe,snhe->sphn", query_heads, key_heads, preferred_element_type=jnp.float32)
        * scale
    )
    new_max = jnp.maximum(running_max, jnp.max(scores, axis=-1))
    weights = jnp.exp(scores - new_max[..., None])
    new_sum = jnp.sum(weights, axis=-1)
    mixed = jnp.einsum(
        "sphn,snhe->sphe",
        weights.astype(jnp.bfloat16),
        value_heads,
        preferred_element_type=jnp.float32,
    )
    total = mixed
    running_max, running_sum, total = (new_max, new_sum, total.reshape(slots, rows, width))
    attended = (
        (split_heads(total) / running_sum[..., None])
        .reshape(slots, rows, width)
        .astype(jnp.bfloat16)
    )
    return (attended, running_max + jnp.log(running_sum), None)


def attention_backward(queries, keys_here, values_here, grad_attended, log_total, delta):
    slots, rows, width = queries.shape
    scale = HEAD_DIM ** (-0.5)
    query_heads = split_heads(queries)
    grad_heads = split_heads(grad_attended)
    piece = (
        lax.all_gather(keys_here, "wide", axis=1, tiled=True),
        lax.all_gather(values_here, "wide", axis=1, tiled=True),
    )
    toward_key_heads = split_heads(piece[0])
    toward_value_heads = split_heads(piece[1])
    scores = (
        jnp.einsum(
            "sphe,snhe->sphn", query_heads, toward_key_heads, preferred_element_type=jnp.float32
        )
        * scale
    )
    probs = jnp.exp(scores - log_total[..., None])
    slope = jnp.einsum(
        "sphe,snhe->sphn", grad_heads, toward_value_heads, preferred_element_type=jnp.float32
    )
    grad_scores = (probs * (slope - delta[..., None])).astype(jnp.bfloat16)
    grad_queries = (
        jnp.einsum(
            "sphn,snhe->sphe", grad_scores, toward_key_heads, preferred_element_type=jnp.float32
        )
        * scale
    ).reshape(slots, rows, width)
    stats = (
        lax.all_gather(log_total, "wide", axis=1, tiled=True),
        lax.all_gather(delta, "wide", axis=1, tiled=True),
    )
    key_heads = split_heads(keys_here)
    value_heads = split_heads(values_here)
    piece = (
        lax.all_gather(queries, "wide", axis=1, tiled=True),
        lax.all_gather(grad_attended, "wide", axis=1, tiled=True),
    )
    piece_queries = split_heads(piece[0])
    piece_grads = split_heads(piece[1])
    piece_total = stats[0]
    piece_delta = stats[1]
    scores = (
        jnp.einsum("snhe,sphe->snhp", piece_queries, key_heads, preferred_element_type=jnp.float32)
        * scale
    )
    probs = jnp.exp(scores - piece_total[..., None])
    slope = jnp.einsum(
        "snhe,sphe->snhp", piece_grads, value_heads, preferred_element_type=jnp.float32
    )
    grad_scores = (probs * (slope - piece_delta[..., None])).astype(jnp.bfloat16)
    keys_total = (
        jnp.einsum(
            "snhp,snhe->sphe", grad_scores, piece_queries, preferred_element_type=jnp.float32
        )
        * scale
    ).reshape(slots, rows, width)
    values_total = jnp.einsum(
        "snhp,snhe->sphe",
        probs.astype(jnp.bfloat16),
        piece_grads,
        preferred_element_type=jnp.float32,
    ).reshape(slots, rows, width)
    return (
        grad_queries.astype(jnp.bfloat16),
        keys_total.astype(jnp.bfloat16),
        values_total.astype(jnp.bfloat16),
    )


def body(
    tokens,
    cotangent,
    emb_table,
    ada_weight,
    ada_bias,
    qkv_weight,
    out_weight,
    out_bias,
    up_weight,
    up_bias,
    down_weight,
    down_bias,
    lead_class,
    group_count,
):
    group = lax.axis_index("narrow")
    slot_count = tokens.shape[1]
    width = tokens.shape[3]
    table = emb_table.astype(jnp.float32)
    class_range = jnp.arange(table.shape[0], dtype=jnp.int32)
    classes_here = lax.dynamic_index_in_dim(lead_class, group, 0, keepdims=False)
    count_here = lax.dynamic_index_in_dim(group_count, group, 0, keepdims=False)
    live = (jnp.arange(slot_count, dtype=jnp.int32) < count_here).astype(jnp.float32)[:, None, None]
    embed_here = jnp.dot(
        (classes_here[:, None] == class_range[None, :]).astype(jnp.float32),
        table,
        precision=highest,
    )
    silu_here = embed_here * jax.nn.sigmoid(embed_here)
    hidden = tokens[0].astype(jnp.float32)
    layer = 0
    parts = modulation_parts(silu_here, ada_weight[layer], ada_bias[layer])
    later = (
        out_weight[layer],
        out_bias[layer],
        up_weight[layer],
        up_bias[layer],
        down_weight[layer],
        down_bias[layer],
    )
    normed, inverse, modulated, queries, keys_here, values_here = before_attention(
        hidden, parts, qkv_weight[layer]
    )
    attended, log_total, whole_pair = attention_forward(queries, keys_here, values_here)
    kept = [(hidden, parts, attended, log_total, whole_pair)]
    hidden, unused = after_attention(hidden, attended, parts, later)
    output = hidden * live
    grad = cotangent[0].astype(jnp.float32) * live
    grad_mods = [None] * LAYERS
    weight_grads = [None] * LAYERS
    for layer in reversed(range(LAYERS)):
        layer_input, parts, attended, log_total, whole_pair = kept[layer]
        later = (
            out_weight[layer],
            out_bias[layer],
            up_weight[layer],
            up_bias[layer],
            down_weight[layer],
            down_bias[layer],
        )
        normed, inverse, modulated, queries, keys_here, values_here = before_attention(
            layer_input, parts, qkv_weight[layer]
        )
        unused, inner = after_attention(layer_input, attended, parts, later)
        branch, middle, normed_mlp, inverse_mlp, modulated_mlp, upward, activated, feed = inner
        grad_feed = (grad * parts[5]).astype(jnp.bfloat16)
        grad_gate_mlp = jnp.sum(grad * feed, axis=1)
        grad_down_w = jnp.einsum(
            "spf,spd->fd", activated, grad_feed, preferred_element_type=jnp.float32
        )
        grad_down_b = jnp.sum(grad_feed.astype(jnp.float32), axis=(0, 1))
        grad_upward = (
            jnp.einsum(
                "spd,fd->spf", grad_feed, down_weight[layer], preferred_element_type=jnp.float32
            )
            * gelu_slope(upward)
        ).astype(jnp.bfloat16)
        grad_up_w = jnp.einsum(
            "spd,spf->df", modulated_mlp, grad_upward, preferred_element_type=jnp.float32
        )
        grad_up_b = jnp.sum(grad_upward.astype(jnp.float32), axis=(0, 1))
        grad_mod_mlp = jnp.einsum(
            "spf,df->spd", grad_upward, up_weight[layer], preferred_element_type=jnp.float32
        )
        grad_shift_mlp = jnp.sum(grad_mod_mlp, axis=1)
        grad_scale_mlp = jnp.sum(grad_mod_mlp * normed_mlp, axis=1)
        grad_middle = grad + norm_back(grad_mod_mlp * (1.0 + parts[4]), normed_mlp, inverse_mlp)
        grad_gate_attn = jnp.sum(grad_middle * branch, axis=1)
        grad_branch = (grad_middle * parts[2]).astype(jnp.bfloat16)
        grad_out_w = jnp.einsum(
            "spd,spe->de", attended, grad_branch, preferred_element_type=jnp.float32
        )
        grad_out_b = jnp.sum(grad_branch.astype(jnp.float32), axis=(0, 1))
        grad_attended = jnp.einsum(
            "spe,de->spd", grad_branch, out_weight[layer], preferred_element_type=jnp.float32
        ).astype(jnp.bfloat16)
        delta = jnp.sum(
            split_heads(grad_attended.astype(jnp.float32) * attended.astype(jnp.float32)), axis=-1
        )
        grad_queries, grad_keys, grad_values = attention_backward(
            queries, keys_here, values_here, grad_attended, log_total, delta
        )
        grad_projected = jnp.concatenate([grad_queries, grad_keys, grad_values], axis=-1)
        grad_qkv_w = jnp.einsum(
            "spd,spf->df", modulated, grad_projected, preferred_element_type=jnp.float32
        )
        grad_mod_attn = jnp.einsum(
            "spf,df->spd", grad_projected, qkv_weight[layer], preferred_element_type=jnp.float32
        )
        grad_shift_attn = jnp.sum(grad_mod_attn, axis=1)
        grad_scale_attn = jnp.sum(grad_mod_attn * normed, axis=1)
        grad = grad_middle + norm_back(grad_mod_attn * (1.0 + parts[1]), normed, inverse)
        local_mods = jnp.stack(
            [
                grad_shift_attn,
                grad_scale_attn,
                grad_gate_attn,
                grad_shift_mlp,
                grad_scale_mlp,
                grad_gate_mlp,
            ],
            axis=1,
        ).reshape(slot_count, 6 * width)
        grad_mods[layer] = lax.psum(local_mods, "wide")
        weight_grads[layer] = lax.psum(
            (grad_qkv_w, grad_out_w, grad_out_b, grad_up_w, grad_up_b, grad_down_w, grad_down_b),
            ("narrow", "wide"),
        )
    all_mods = lax.all_gather(
        jnp.stack(grad_mods, axis=0).astype(jnp.bfloat16), "narrow", axis=1, tiled=True
    ).astype(jnp.float32)
    all_classes = lead_class.reshape(-1)
    onehot_all = (all_classes[:, None] == class_range[None, :]).astype(jnp.float32)
    embed_all = jnp.dot(onehot_all, table, precision=highest)
    sigmoid_all = jax.nn.sigmoid(embed_all)
    silu_all = embed_all * sigmoid_all
    grad_ada_w = jnp.einsum("id,lie->lde", silu_all, all_mods, precision=highest)
    grad_ada_b = jnp.sum(all_mods, axis=1)
    grad_silu = jnp.einsum(
        "lie,lde->id", all_mods, ada_weight.astype(jnp.float32), precision=highest
    )
    grad_embed = grad_silu * (sigmoid_all + embed_all * sigmoid_all * (1.0 - sigmoid_all))
    grad_table = jnp.dot(onehot_all.T, grad_embed, precision=highest)
    stacked = [jnp.stack([weight_grads[0][member]], axis=0) for member in range(7)]
    return (
        output[None],
        grad[None],
        grad_table,
        grad_ada_w,
        grad_ada_b,
        stacked[0],
        stacked[1],
        stacked[2],
        stacked[3],
        stacked[4],
        stacked[5],
        stacked[6],
    )


def solution(mesh):
    in_specs = (
        P("narrow", None, "wide", None),
        P("narrow", None, "wide", None),
        P(),
        P(),
        P(),
        P(),
        P(),
        P(),
        P(),
        P(),
        P(),
        P(),
        P(),
        P(),
    )
    out_specs = (
        P("narrow", None, "wide", None),
        P("narrow", None, "wide", None),
        P(),
        P(),
        P(),
        P(),
        P(),
        P(),
        P(),
        P(),
        P(),
        P(),
    )
    by_item = dict(mesh.shape) == {"narrow": 4, "wide": 8}
    return jax.shard_map(fast_body if by_item else body, mesh=mesh, in_specs=in_specs, out_specs=out_specs, check_vma=False)
```

```python
import functools
from types import SimpleNamespace

import jax
import jax.numpy as jnp
from jax import lax
from jax.experimental import pallas as pl
from jax.experimental.pallas import tpu as pltpu
from jax.sharding import PartitionSpec as P

MESH = pl.DeviceIdType.MESH
f32, bf16 = jnp.float32, jnp.bfloat16
EPS = 1e-06
ROOT_HALF = 0.7071067811865476
INV_ROOT_2PI = 0.3989422804014327
HEAD_DIM = 64
EARLY_COTANGENT = 0
EARLY = 6
FORMS = (False, False, False, False, False, False, False, False, False)
PLAN = (
    (10, 11, 13),
    (),
    (),
    (),
    (),
    (),
    (),
    (0,),
    (1, 2),
    (3, 4),
    (5,),
    (),
    (),
    (),
    (),
    (),
    (),
    (0,),
    (1,),
    (),
    (),
    (),
    (2, 6),
    (3, 0),
    (),
    (7, 1, 4, 2, 5),
    (),
    (8, 6, 3, 0, 9, 1, 7, 4, 2, 8, 5, 6, 0, 3, 9, 0, 7, 17, 4, 1, 8, 2, 1, 5, 16, 6, 2, 3, 9, 3, 7, 12, 9, 4, 8, 14, 4, 5, 15, 6, 5, 6, 7, 8, 7, 8),
)


def dot_nn(a, b):
    return lax.dot_general(a, b, (((1,), (0,)), ((), ())), preferred_element_type=f32)


def dot_nt(a, b):
    return lax.dot_general(a, b, (((1,), (1,)), ((), ())), preferred_element_type=f32)


def dot_tn(a, b):
    return lax.dot_general(a, b, (((0,), (0,)), ((), ())), preferred_element_type=f32)


def norm_rows(x):
    centred = x - jnp.mean(x, axis=-1, keepdims=True)
    inverse = lax.rsqrt(jnp.mean(centred * centred, axis=-1, keepdims=True) + EPS)
    return centred * inverse, inverse


def norm_rows_back(x, n, inverse):
    first = jnp.mean(x, axis=-1, keepdims=True)
    second = jnp.mean(x * n, axis=-1, keepdims=True)
    return inverse * (x - first - n * second)


def col_sum(x):
    return jnp.sum(x, axis=0, keepdims=True)


class Place:
    def __init__(self):
        narrow, wide = lax.axis_index("narrow"), lax.axis_index("wide")
        self.y, self.c = narrow // 2, narrow % 2
        self.z, self.x = wide // 2, wide % 2
        self.wide = wide
        self.low = wide % 4
        self.half = wide // 4
        self.rows_half = 1 - self.c

    def low_xor(self, i):
        a = self.low
        if i & 1:
            a = a + 1 - 2 * (a % 2)
        if i & 2:
            a = a + 2 - 4 * (a // 2)
        return a

    def home(self, i):
        slot = self.low_xor(i)
        return slot, (2 * self.y + 1 - self.half, 4 * self.c + slot)

    def source(self, i):
        strip = self.low_xor(i)
        return strip, (2 * self.y + self.half, 4 * self.rows_half + strip)

    def core(self):
        return (2 * self.y + 1 - self.c, self.wide)

    def in_plane(self, k):
        x = 1 - self.x if k & 1 else self.x
        y = 1 - self.y if k & 2 else self.y
        return 2 * y + x, (2 * y + self.c, 2 * self.z + x)

    def along_z(self, k):
        z = self.z
        if k & 1:
            z = z + 1 - 2 * (z % 2)
        if k & 2:
            z = z + 2 - 4 * (z // 2)
        return z, (2 * self.y + self.c, 2 * z + self.x)


class Wire:
    def __init__(self, send_sems, recv_sems):
        self.send_sems, self.recv_sems = send_sems, recv_sems
        self.outs, self.ins = 0, 0

    def sender(self):
        self.outs += 1
        return self.send_sems.at[self.outs - 1]

    def receiver(self):
        self.ins += 1
        return self.recv_sems.at[self.ins - 1]

    def copy(self, src, dst, device, sender, receiver):
        pltpu.make_async_remote_copy(
            src_ref=src,
            dst_ref=dst,
            send_sem=sender,
            recv_sem=receiver,
            device_id=device,
            device_id_type=MESH,
        ).start()


def take(semaphore, like):
    pltpu.make_async_copy(like, like, semaphore).wait()


def main_kernel(sizes, names, *refs):
    r = SimpleNamespace(**dict(zip(names, refs, strict=True)))
    R, D, FF = sizes
    M, N = 4 * R, 8 * R
    MB = M // 2
    pairs = D // 128
    here = Place()
    wire = Wire(r.send_sems, r.recv_sems)
    local_sems = r.local_sems
    local_count = [0]

    def local(src, dst):
        made = pltpu.make_async_copy(src, dst, local_sems.at[local_count[0]])
        local_count[0] += 1
        made.start()
        return made

    small_loads = [
        local(r.emb_table, r.emb_table_v),
        local(r.ada_bias, r.ada_bias_v),
        local(r.out_bias, r.out_bias_v),
        local(r.up_bias, r.up_bias_v),
        local(r.down_bias, r.down_bias_v),
    ]
    load_ada = local(r.ada_weight.at[0], r.ada_weight_v)
    qkv_sem = local_sems.at[local_count[0]]
    local_count[0] += 1
    for p in range(pairs):
        for b in range(3):
            pltpu.make_async_copy(
                r.qkv_weight.at[0, :, pl.ds(b * D + p * 128, 128)],
                r.qkv_weight_v.at[p, :, pl.ds(b * 128, 128)],
                qkv_sem,
            ).start()
    load_rest = [
        local(r.out_weight.at[0], r.out_weight_v),
        local(r.up_weight.at[0], r.up_weight_v),
        local(r.down_weight.at[0], r.down_weight_v),
    ]

    barrier = pltpu.get_barrier_semaphore()
    partners = [here.core()]
    partners += [here.home(i)[1] for i in range(4)] + [here.source(i)[1] for i in range(4)]
    partners += [here.in_plane(k)[1] for k in (1, 2, 3)] + [here.along_z(k)[1] for k in (1, 2, 3)]
    for device in partners:
        pl.semaphore_signal(barrier, inc=1, device_id=device, device_id_type=MESH)
    pl.semaphore_wait(barrier, len(partners))

    def send_home(whole, landing, i, sender, receiver):
        place = pl.ds(pl.multiple_of(here.low * R, R), R)
        slot, device = here.home(i)
        wire.copy(whole.at[0, slot], landing.at[place, :], device, sender, receiver)

    tokens_out, tokens_in = wire.sender(), [wire.receiver() for _ in range(4)]
    cotangent_out, cotangent_in = wire.sender(), wire.receiver()
    for i in range(4):
        send_home(r.tokens, r.tokens_v, i, tokens_out, tokens_in[i])

    group, slot = 2 * here.y + here.half, here.low
    item_class = r.lead_class[group, slot]
    live = (slot < r.group_count[group]).astype(f32)
    for made in small_loads:
        made.wait()
    table = r.emb_table_v[...].astype(f32)
    class_col = lax.broadcasted_iota(jnp.int32, (table.shape[0], 1), 0)
    onehot = (class_col == item_class).astype(f32)
    embed = jnp.sum(onehot * table, axis=0, keepdims=True)
    silu = embed * (1.0 / (1.0 + jnp.exp(-embed)))
    high = silu.astype(bf16).astype(f32)
    middle_part = (silu - high).astype(bf16).astype(f32)
    low_part = silu - high - middle_part
    row = lax.broadcasted_iota(jnp.int32, (16, D), 0)
    parts = jnp.where(row == 0, high, jnp.where(row == 1, middle_part, jnp.where(row == 2, low_part, 0.0)))
    load_ada.wait()
    mods = r.mods
    for k in range(6):
        cols = pl.ds(k * D, D)
        mods[k : k + 1, :] = col_sum(
            dot_nn(parts.astype(bf16), r.ada_weight_v[:, cols])
        ) + r.ada_bias_v[:, cols].astype(f32)

    def mod(k):
        return mods[k : k + 1, :]

    acc = r.acc
    acc[...] = jnp.zeros_like(acc)

    take(qkv_sem, r.qkv_weight_v)
    lane = lax.broadcasted_iota(jnp.int32, (R, 128), 1)
    left = lane < HEAD_DIM
    kv, qst = r.kv, r.qst
    kv_out, kv_in = wire.sender(), wire.receiver()
    own = pl.multiple_of(here.rows_half * M, M)
    for i in range(4):
        strip, _ = here.source(i)
        take(tokens_in[i], r.tokens_v.at[pl.ds(0, R), :])
        at = pl.multiple_of(strip * R, R)
        rows = pl.ds(at, R)
        normed, inverse = norm_rows(r.tokens_v[rows, :].astype(f32))
        r.normed[rows, :] = normed
        r.inverse[rows, :] = inverse
        modulated = (normed * (1.0 + mod(1)) + mod(0)).astype(bf16)
        r.modulated[rows, :] = modulated
        kv_rows = pl.ds(pl.multiple_of(own + at, R), R)
        for p in range(pairs):
            projected = dot_nn(modulated, r.qkv_weight_v[p]).astype(bf16)
            kv[p, kv_rows, :] = projected[:, 128:]
            q = projected[:, :128] * HEAD_DIM ** (-0.5)
            zero = jnp.zeros_like(q)
            qst[p, pl.ds(at, R), :] = jnp.where(left, q, zero)
            qst[p, pl.ds(pl.multiple_of(M + at, R), R), :] = jnp.where(left, zero, q)
        wire.copy(kv.at[:, kv_rows, :], kv.at[:, kv_rows, :], here.core(), kv_out, kv_in)
        if i < EARLY_COTANGENT:
            send_home(r.cotangent, r.cotangent_v, i, cotangent_out, cotangent_in)
    take(tokens_out, r.tokens_v)
    for i in range(EARLY_COTANGENT, 4):
        send_home(r.cotangent, r.cotangent_v, i, cotangent_out, cotangent_in)
    take(kv_in, kv.at[:, pl.ds(0, M), :])

    kvt, es, ots = r.kvt, r.es, r.ots
    for p in range(pairs):
        kvt[p] = kv[p].T
    QB = M // 2
    CB = N // 4
    scores = (r.scores_a, r.scores_b)

    def score_rows(j, c):
        p, qb = j // 4, j % 4
        found = dot_nt(kv[p, c * CB : (c + 1) * CB, :128], qst[p, qb * QB : (qb + 1) * QB, :])
        scores[j % 2][c * CB : (c + 1) * CB, :] = found
        return jnp.max(found.reshape(CB // 8, 8, QB), axis=0)

    def mix(j):
        p, qb = j // 4, j % 4
        half = qb // 2 * HEAD_DIM
        mixed = dot_nn(kvt[p, 128 + half : 128 + half + HEAD_DIM, :], es[p, :, qb * QB : (qb + 1) * QB])
        head = slice(p * 128 + half, p * 128 + half + HEAD_DIM)
        ots[head, qb % 2 * QB : (qb % 2 + 1) * QB] = mixed * r.inv_sum[j]

    tops = [score_rows(0, c) for c in range(4)]
    for j in range(4 * pairs):
        p, qb = j // 4, j % 4
        top = jnp.maximum(jnp.maximum(tops[0], tops[1]), jnp.maximum(tops[2], tops[3]))
        top = jnp.max(top, axis=0, keepdims=True)
        tops, sums = [], []
        for c in range(4):
            keys = slice(c * CB, (c + 1) * CB)
            if j + 1 < 4 * pairs:
                tops.append(score_rows(j + 1, c))
            raised = jnp.exp(scores[j % 2][keys, :] - top)
            sums.append(jnp.sum(raised.reshape(CB // 8, 8, QB), axis=0))
            es[p, keys, qb * QB : (qb + 1) * QB] = raised.astype(bf16)
            if c == 0 and j > 0:
                mix(j - 1)
        r.inv_sum[j] = 1.0 / col_sum((sums[0] + sums[1]) + (sums[2] + sums[3]))
    mix(4 * pairs - 1)
    att = r.att
    for p in range(pairs):
        att[:, p * 128 : (p + 1) * 128] = ots[p * 128 : (p + 1) * 128, :].T.astype(bf16)

    part, total, arena = r.part, r.grads_o, r.arena
    used = [0]

    def room(rows):
        start = used[0]
        used[0] += rows
        return start

    def span(start, index, rows):
        return pl.ds(pl.multiple_of(start + index * rows, 16), rows)

    def wide(ref, rows):
        return ref[rows, :].astype(f32)

    units_out = wire.sender()
    units_rows = [0]

    def reduce_unit(base, rows, z_first):
        half = rows // 2

        def move(src, dst, device, receiver):
            units_rows[0] += src.shape[0]
            wire.copy(src, dst, device, units_out, receiver)

        land = room(half)
        block = room(half)
        arrived = wire.receiver()
        move(
            part.at[span(base, 1 - here.c, half), :],
            arena.at[pl.ds(land, half), :],
            here.core(),
            arrived,
        )
        yield
        take(arrived, arena.at[pl.ds(land, half), :])
        arena[pl.ds(block, half), :] = (
            wide(part, span(base, here.c, half)) + wide(arena, pl.ds(land, half))
        ).astype(bf16)
        mine = base + half * here.c
        count = half
        axes = (here.along_z, here.in_plane) if z_first else (here.in_plane, here.along_z)
        for axis in axes:
            count = count // 4
            land = room(3 * count)
            arrived = wire.receiver()
            for k in (3, 2, 1):
                q, device = axis(k)
                move(
                    arena.at[span(block, q, count), :],
                    arena.at[pl.ds(land + (k - 1) * count, count), :],
                    device,
                    arrived,
                )
            yield
            take(arrived, arena.at[pl.ds(land, 3 * count), :])
            me = axis(0)[0]
            summed = wide(arena, span(block, me, count)) + wide(arena, pl.ds(land, count))
            summed = summed + (
                wide(arena, pl.ds(land + count, count)) + wide(arena, pl.ds(land + 2 * count, count))
            )
            mine = mine + count * me
            if axis is axes[0]:
                block = room(count)
                arena[pl.ds(block, count), :] = summed.astype(bf16)
            else:
                total[span(mine, 0, count), :] = summed.astype(bf16)
        for axis in axes[::-1]:
            keep = span(mine, 0, count)
            arrived = wire.receiver()
            for k in (3, 2, 1):
                move(total.at[keep, :], total.at[keep, :], axis(k)[1], arrived)
            yield
            take(arrived, total.at[pl.ds(0, 3 * count), :])
            mine = mine - count * axis(0)[0]
            count = 4 * count
        keep = span(mine, 0, half)
        arrived = wire.receiver()
        move(total.at[keep, :], total.at[keep, :], here.core(), arrived)
        yield
        take(arrived, total.at[pl.ds(0, half), :])
        yield

    small_out = wire.sender()

    def reduce_small():
        small, small_a, small_b, land, small_sum = (
            r.small,
            r.small_a,
            r.small_b,
            r.land_small,
            r.small_o,
        )
        here_rows = span(0, here.c, 16)
        arrived = wire.receiver()
        wire.copy(small.at[span(0, 1 - here.c, 16), :], land.at[0], here.core(), small_out, arrived)
        yield
        take(arrived, land.at[0])
        small_a[...] = small[here_rows, :] + land[0]
        arrived = wire.receiver()
        for k in (3, 2, 1):
            wire.copy(small_a, land.at[k], here.in_plane(k)[1], small_out, arrived)
        yield
        take(arrived, land.at[pl.ds(1, 3)])
        small_b[...] = (small_a[...] + land[1]) + (land[2] + land[3])
        arrived = wire.receiver()
        for k in (3, 2, 1):
            wire.copy(small_b, land.at[3 + k], here.along_z(k)[1], small_out, arrived)
        yield
        take(arrived, land.at[pl.ds(4, 3)])
        small_sum[here_rows, :] = (small_b[...] + land[4]) + (land[5] + land[6])
        arrived = wire.receiver()
        wire.copy(
            small_sum.at[here_rows, :], small_sum.at[here_rows, :], here.core(), small_out, arrived
        )
        yield
        take(arrived, small_sum.at[pl.ds(0, 16), :])
        yield

    def send_back(stage, landing, i, sender, receiver):
        strip, device = here.source(i)
        rows = pl.ds(pl.multiple_of(strip * R, R), R)
        wire.copy(stage.at[rows, :], landing.at[here.low], device, sender, receiver)
        yield

    out_out, out_in, gtok_out, gtok_in = (
        wire.sender(),
        wire.receiver(),
        wire.sender(),
        wire.receiver(),
    )

    third = 4 * D // 3
    early = 2 * FF // EARLY
    units = [reduce_unit(early * i, early, FORMS[i]) for i in range(EARLY)]
    units += [reduce_unit(2 * FF + third * i, third, FORMS[EARLY + i]) for i in range(3)]
    units.append(reduce_small())
    units += [send_back(r.out_stage, r.out_o, i, out_out, out_in) for i in range(4)]
    units += [send_back(r.gtok_stage, r.gtok_o, i, gtok_out, gtok_in) for i in range(4)]
    plan = iter(PLAN)

    def advance():
        for unit in next(plan):
            next(units[unit])

    for made in load_rest:
        made.wait()
    outw, upw, downw = r.out_weight_v, r.up_weight_v, r.down_weight_v
    chunks = FF // D

    def feed_rows(t):
        rows = slice(t * MB, (t + 1) * MB)
        branch = dot_nn(att[rows, :], outw[...]) + r.out_bias_v[...].astype(f32)
        middle = r.tokens_v[rows, :].astype(f32) + mod(2) * branch
        n, inverse = norm_rows(middle)
        modulated = (n * (1.0 + mod(4)) + mod(3)).astype(bf16)
        r.modulated_m[rows, :] = modulated
        yield
        for ck in range(chunks):
            cols = slice(ck * D, (ck + 1) * D)
            u = dot_nn(modulated, upw[:, cols]) + r.up_bias_v[:, cols].astype(f32)
            phi = 0.5 * (1.0 + lax.erf(u * ROOT_HALF))
            r.activated[rows, cols] = (u * phi).astype(bf16)
            r.slope[rows, cols] = phi + u * (INV_ROOT_2PI * jnp.exp(-0.5 * u * u))
            yield
        feed = dot_nn(r.activated[rows, :], downw[...]) + r.down_bias_v[...].astype(f32)
        r.out_stage[rows, :] = ((middle + mod(5) * feed) * live).astype(bf16)
        yield
        grad = r.cotangent_v[rows, :].astype(f32) * live
        grad_feed = (grad * mod(5)).astype(bf16)
        r.grad_feed[rows, :] = grad_feed
        acc[5:6, :] += col_sum(grad * feed)
        acc[8:9, :] += col_sum(grad_feed.astype(f32))
        yield
        for ck in range(chunks):
            cols = slice(ck * D, (ck + 1) * D)
            grad_up = (dot_nt(grad_feed, downw[cols, :]) * r.slope[rows, cols]).astype(bf16)
            r.grad_up[rows, cols] = grad_up
            acc[9 + ck : 10 + ck, :] += col_sum(grad_up.astype(f32))
            yield
        back = dot_nt(r.grad_up[rows, :], upw[...])
        acc[3:4, :] += col_sum(back)
        acc[4:5, :] += col_sum(back * n)
        grad_middle = grad + norm_rows_back(back * (1.0 + mod(4)), n, inverse)
        r.grad_middle[rows, :] = grad_middle
        acc[2:3, :] += col_sum(grad_middle * branch)
        grad_branch = (grad_middle * mod(2)).astype(bf16)
        r.grad_branch[rows, :] = grad_branch
        acc[13:14, :] += col_sum(grad_branch.astype(f32))
        yield
        r.grad_att[rows, :] = dot_nt(grad_branch, outw[...]).astype(bf16)

    blocks = [feed_rows(0), feed_rows(1)]
    for _ in range(chunks + 2):
        for block in blocks:
            next(block)
    take(cotangent_in, r.cotangent_v)
    advance()
    for _ in range(chunks + 3):
        for block in blocks:
            next(block, None)

    started = 0
    for ck in range(2 * chunks):
        rows = slice(ck * D, (ck + 1) * D)
        cols = slice(ck % chunks * D, (ck % chunks + 1) * D)
        if ck < chunks:
            found = dot_tn(r.activated[:, cols], r.grad_feed[...])
        else:
            found = dot_tn(r.modulated_m[...], r.grad_up[:, cols])
        part[rows, :] = found.astype(bf16)
        while started < EARLY and (started + 1) * early <= (ck + 1) * D:
            next(units[started])
            started += 1
        advance()
    part[2 * FF : 2 * FF + D, :] = dot_tn(att[...], r.grad_branch[...]).astype(bf16)

    gat, qgt = r.gat, r.qgt
    for p in range(pairs):
        gat[p * 128 : (p + 1) * 128, :] = r.grad_att[:, p * 128 : (p + 1) * 128].T.astype(f32)
    zero_half = jnp.zeros((HEAD_DIM, QB), bf16)
    gst, gstt, deltas, dkv = r.gst, r.gstt, r.deltas, r.dkv
    dss = (r.dss_a, r.dss_b)
    for p in range(pairs):
        for qb in range(4):
            half = qb // 2
            head = slice(p * 128 + half * HEAD_DIM, p * 128 + (half + 1) * HEAD_DIM)
            queries = slice(qb % 2 * QB, (qb % 2 + 1) * QB)
            scaled = gat[head, queries] * r.inv_sum[4 * p + qb]
            deltas[4 * p + qb] = col_sum(scaled * ots[head, queries])
            scaled = scaled.astype(bf16)
            filled = [scaled, zero_half] if half == 0 else [zero_half, scaled]
            gstt[p, :, qb * QB : (qb + 1) * QB] = jnp.concatenate(filled, axis=0)
        gst[p] = gstt[p].T
    other = pl.multiple_of((1 - here.rows_half) * M, M)
    dkv_out, dkv_in = wire.sender(), [wire.receiver() for _ in range(pairs)]
    gp = r.grad_projected

    def finish_pair(p):
        gp[p, :, 0:128] = qgt[p * 128 : (p + 1) * 128, :].T.astype(bf16)
        take(dkv_in[p], r.land_dkv.at[p])
        gp[p, :, 128:384] = (
            dkv[p, pl.ds(own, M), :].astype(f32) + r.land_dkv[p].astype(f32)
        ).astype(bf16)
        rows = slice(2 * FF + (p + 1) * D, 2 * FF + (p + 2) * D)
        part[rows, :] = dot_tn(r.modulated[...], gp[p]).astype(bf16)
        next(units[EARLY + p])
        advance()

    def grad_values(p, c):
        keys = slice(c * CB, (c + 1) * CB)
        dkv[p, keys, 128:256] = dot_nn(es[p, keys, :], gst[p]).astype(bf16)

    def grad_keys(p, c):
        keys = slice(c * CB, (c + 1) * CB)
        dkv[p, keys, 0:128] = dot_nn(dss[p % 2][keys, :], qst[p]).astype(bf16)
        if c == 3:
            wire.copy(
                dkv.at[p, pl.ds(other, M), :], r.land_dkv.at[p], here.core(), dkv_out, dkv_in[p]
            )

    def grad_queries(p, qb):
        half = qb // 2 * HEAD_DIM
        head = slice(p * 128 + half, p * 128 + half + HEAD_DIM)
        found = dot_nn(kvt[p, half : half + HEAD_DIM, :], dss[p % 2][:, qb * QB : (qb + 1) * QB])
        qgt[head, qb % 2 * QB : (qb % 2 + 1) * QB] = found * HEAD_DIM ** (-0.5)

    later = []
    advance()
    for p in range(pairs):
        for qb in range(4):
            queries = slice(qb * QB, (qb + 1) * QB)
            for c in range(4):
                keys = slice(c * CB, (c + 1) * CB)
                slope = dot_nn(kv[p, keys, 128:], gstt[p, :, queries])
                dss[p % 2][keys, queries] = (
                    es[p, keys, queries].astype(f32) * (slope - deltas[4 * p + qb])
                ).astype(bf16)
                if later:
                    later.pop(0)()
            later.append(functools.partial(grad_queries, p, qb))
            if qb == 0:
                later += [functools.partial(grad_values, p, k) for k in range(4)]
            if qb == 3:
                later += [functools.partial(grad_keys, p, k) for k in range(4)]
            advance()
            if p > 0 and qb == 3:
                finish_pair(p - 1)
    for made in later:
        made()
    advance()
    finish_pair(pairs - 1)

    for t in range(2):
        rows = slice(t * MB, (t + 1) * MB)
        back = dot_nt(gp[0, rows, :], r.qkv_weight_v[0])
        for p in range(1, pairs):
            back = back + dot_nt(gp[p, rows, :], r.qkv_weight_v[p])
        n = r.normed[rows, :]
        acc[0:1, :] += col_sum(back)
        acc[1:2, :] += col_sum(back * n)
        grad = r.grad_middle[rows, :] + norm_rows_back(
            back * (1.0 + mod(1)), n, r.inverse[rows, :]
        )
        r.gtok_stage[rows, :] = grad.astype(bf16)
        if t == 0:
            advance()

    small = r.small
    for k in range(6):
        small[4 * k : 4 * k + 4, :] = onehot * acc[k : k + 1, :]
    small[24:32, :] = acc[8:16, :]
    next(units[EARLY + 3])
    advance()
    take(out_in, r.out_o)
    take(gtok_in, r.gtok_o)
    take(cotangent_out, r.cotangent_v)
    take(kv_out, kv.at[:, pl.ds(0, M), :])
    take(dkv_out, r.land_dkv)
    take(out_out, r.out_stage)
    take(gtok_out, r.gtok_stage)
    take(small_out, r.land_small)
    take(units_out, arena.at[pl.ds(0, units_rows[0]), :])


def last_kernel(sizes, names, *refs):
    r = SimpleNamespace(**dict(zip(names, refs, strict=True)))
    D, FF = sizes
    sems = r.sems
    count = [0]

    def local(src, dst):
        made = pltpu.make_async_copy(src, dst, sems.at[count[0]])
        count[0] += 1
        made.start()
        return made

    table_in = local(r.emb_table, r.emb_table_v)
    ada_in = local(r.ada_weight, r.ada_weight_v)
    outs = []
    grads = r.grads_i

    def widen(k, target):
        target[...] = grads[k * D : (k + 1) * D, :].astype(f32)

    for k in range(FF // D):
        rows = pl.ds(k * D, D)
        widen(k, r.gdown_v.at[rows, :])
        outs.append(local(r.gdown_v.at[rows, :], r.gdown.at[0, rows, :]))
    for k in range(FF // D):
        cols = pl.ds(k * D, D)
        widen(FF // D + k, r.gup_v.at[k])
        outs.append(local(r.gup_v.at[k], r.gup.at[0, :, cols]))
    first = 2 * FF // D
    widen(first, r.gout_v)
    outs.append(local(r.gout_v, r.gout.at[0]))
    for p in range(D // 128):
        rows = slice((first + 1 + p) * D, (first + 2 + p) * D)
        for k in range(3):
            cols = slice(k * D + p * 128, k * D + (p + 1) * 128)
            r.gqkv_v[:, cols] = grads[rows, k * 128 : (k + 1) * 128].astype(f32)
    outs.append(local(r.gqkv_v, r.gqkv.at[0]))
    for given, wide_v, result in ((r.out_i, r.out_v, r.out), (r.gtok_i, r.gtok_v, r.gtok)):
        for s in range(4):
            wide_v[s] = given[s].astype(f32)
        outs.append(local(wide_v, result.at[0]))
    table_in.wait()
    small = r.small_i
    table = r.emb_table_v[...].astype(f32)
    sigmoid = 1.0 / (1.0 + jnp.exp(-table))
    silu = table * sigmoid

    def split(v):
        high = v.astype(bf16).astype(f32)
        return high, v - high

    silu_high, silu_low = split(silu)
    zero = jnp.zeros_like(silu)
    left = jnp.concatenate([silu_high, silu_low, silu_high, zero], axis=0).astype(bf16)
    grad_silu = jnp.zeros_like(table)
    ada_in.wait()
    for k in range(6):
        cols = slice(k * D, (k + 1) * D)
        block = small[4 * k : 4 * k + 4, :]
        high, low = split(block)
        right = jnp.concatenate([high, high, low, zero], axis=0).astype(bf16)
        r.gada_v[k] = dot_tn(left, right)
        outs.append(local(r.gada_v.at[k], r.gada.at[0, :, pl.ds(k * D, D)]))
        r.gada_b[:, cols] = col_sum(block)
        both = jnp.concatenate([high, low, zero, zero], axis=0).astype(bf16)
        found = dot_nt(both, r.ada_weight_v[0, :, cols])
        grad_silu = grad_silu + found[0:4, :] + found[4:8, :]
    r.table_o[...] = grad_silu * (sigmoid + table * sigmoid * (1.0 - sigmoid))
    r.down_b[...] = small[24:25, :]
    for k in range(FF // D):
        r.up_b[:, k * D : (k + 1) * D] = small[25 + k : 26 + k, :]
    r.out_b[...] = small[29:30, :]
    for made in outs:
        made.wait()


def fast_body(*args):
    tokens, emb_table, ada_weight, up_weight = args[0], args[2], args[3], args[8]
    R, D = tokens.shape[2:]
    FF = up_weight.shape[2]
    M, N = 4 * R, 8 * R
    pairs = D // 128
    total_rows = 2 * FF + 4 * D
    vmem = pl.BlockSpec(memory_space=pltpu.VMEM)
    smem = pl.BlockSpec(memory_space=pltpu.SMEM)
    anywhere = pl.BlockSpec(memory_space=pl.ANY)
    arguments = dict(
        tokens=anywhere,
        cotangent=anywhere,
        emb_table=anywhere,
        ada_weight=anywhere,
        ada_bias=anywhere,
        qkv_weight=anywhere,
        out_weight=anywhere,
        out_bias=anywhere,
        up_weight=anywhere,
        up_bias=anywhere,
        down_weight=anywhere,
        down_bias=anywhere,
        lead_class=smem,
        group_count=smem,
    )
    scratch = dict(
        emb_table_v=pltpu.VMEM(emb_table.shape, bf16),
        ada_bias_v=pltpu.VMEM((1, 6 * D), bf16),
        out_bias_v=pltpu.VMEM((1, D), bf16),
        up_bias_v=pltpu.VMEM((1, FF), bf16),
        down_bias_v=pltpu.VMEM((1, D), bf16),
        ada_weight_v=pltpu.VMEM((D, 6 * D), bf16),
        qkv_weight_v=pltpu.VMEM((pairs, D, 384), bf16),
        out_weight_v=pltpu.VMEM((D, D), bf16),
        up_weight_v=pltpu.VMEM((D, FF), bf16),
        down_weight_v=pltpu.VMEM((FF, D), bf16),
        tokens_v=pltpu.VMEM((M, D), bf16),
        cotangent_v=pltpu.VMEM((M, D), bf16),
        mods=pltpu.VMEM((8, D), f32),
        acc=pltpu.VMEM((16, D), f32),
        normed=pltpu.VMEM((M, D), f32),
        inverse=pltpu.VMEM((M, 1), f32),
        modulated=pltpu.VMEM((M, D), bf16),
        kv=pltpu.VMEM((pairs, N, 256), bf16),
        kvt=pltpu.VMEM((pairs, 256, N), bf16),
        qst=pltpu.VMEM((pairs, 2 * M, 128), bf16),
        es=pltpu.VMEM((pairs, N, 2 * M), bf16),
        inv_sum=pltpu.VMEM((4 * pairs, 1, M // 2), f32),
        ots=pltpu.VMEM((D, M), f32),
        att=pltpu.VMEM((M, D), bf16),
        modulated_m=pltpu.VMEM((M, D), bf16),
        activated=pltpu.VMEM((M, FF), bf16),
        slope=pltpu.VMEM((M, FF), f32),
        out_stage=pltpu.VMEM((M, D), bf16),
        grad_feed=pltpu.VMEM((M, D), bf16),
        grad_up=pltpu.VMEM((M, FF), bf16),
        grad_middle=pltpu.VMEM((M, D), f32),
        grad_branch=pltpu.VMEM((M, D), bf16),
        grad_att=pltpu.VMEM((M, D), bf16),
        gat=pltpu.VMEM((D, M), f32),
        qgt=pltpu.VMEM((D, M), f32),
        gst=pltpu.VMEM((pairs, 2 * M, 128), bf16),
        gstt=pltpu.VMEM((pairs, 128, 2 * M), bf16),
        deltas=pltpu.VMEM((4 * pairs, 1, M // 2), f32),
        dss_a=pltpu.VMEM((N, 2 * M), bf16),
        dss_b=pltpu.VMEM((N, 2 * M), bf16),
        scores_a=pltpu.VMEM((N, M // 2), f32),
        scores_b=pltpu.VMEM((N, M // 2), f32),
        dkv=pltpu.VMEM((pairs, N, 256), bf16),
        land_dkv=pltpu.VMEM((pairs, M, 256), bf16),
        grad_projected=pltpu.VMEM((pairs, M, 384), bf16),
        gtok_stage=pltpu.VMEM((M, D), bf16),
        part=pltpu.VMEM((total_rows, D), bf16),
        arena=pltpu.VMEM((2 * total_rows, D), bf16),
        small=pltpu.VMEM((32, D), f32),
        small_a=pltpu.VMEM((16, D), f32),
        small_b=pltpu.VMEM((16, D), f32),
        land_small=pltpu.VMEM((8, 16, D), f32),
        send_sems=pltpu.SemaphoreType.DMA((8,)),
        recv_sems=pltpu.SemaphoreType.DMA((69,)),
        local_sems=pltpu.SemaphoreType.DMA((10,)),
    )
    mids = dict(
        out_o=pltpu.VMEM((4, R, D), bf16),
        gtok_o=pltpu.VMEM((4, R, D), bf16),
        grads_o=pltpu.VMEM((total_rows, D), bf16),
        small_o=pltpu.VMEM((32, D), f32),
    )
    names = tuple(arguments) + tuple(mids) + tuple(scratch)
    middle = pl.pallas_call(
        functools.partial(main_kernel, (R, D, FF), names),
        out_shape=tuple(mids.values()),
        in_specs=list(arguments.values()),
        out_specs=(vmem,) * 4,
        scratch_shapes=list(scratch.values()),
        compiler_params=pltpu.CompilerParams(
            collective_id=0, has_side_effects=True, vmem_limit_bytes=58 << 20
        ),
        name="block_forward_backward",
    )(*args)
    outs = dict(
        out=((1, 4, R, D), anywhere),
        gtok=((1, 4, R, D), anywhere),
        table_o=((emb_table.shape[0], D), vmem),
        gada=((1, D, 6 * D), anywhere),
        gada_b=((1, 6 * D), vmem),
        gqkv=((1, D, 3 * D), anywhere),
        gout=((1, D, D), anywhere),
        out_b=((1, D), vmem),
        gup=((1, D, FF), anywhere),
        up_b=((1, FF), vmem),
        gdown=((1, FF, D), anywhere),
        down_b=((1, D), vmem),
    )
    ins = dict(
        out_i=vmem,
        gtok_i=vmem,
        grads_i=vmem,
        small_i=vmem,
        emb_table=anywhere,
        ada_weight=anywhere,
    )
    scratch = dict(
        emb_table_v=pltpu.VMEM(emb_table.shape, bf16),
        ada_weight_v=pltpu.VMEM((1, D, 6 * D), bf16),
        out_v=pltpu.VMEM((4, R, D), f32),
        gtok_v=pltpu.VMEM((4, R, D), f32),
        gada_v=pltpu.VMEM((6, D, D), f32),
        gqkv_v=pltpu.VMEM((D, 3 * D), f32),
        gout_v=pltpu.VMEM((D, D), f32),
        gup_v=pltpu.VMEM((FF // D, D, D), f32),
        gdown_v=pltpu.VMEM((FF, D), f32),
        sems=pltpu.SemaphoreType.DMA((20,)),
    )
    names = tuple(ins) + tuple(outs) + tuple(scratch)
    return pl.pallas_call(
        functools.partial(last_kernel, (D, FF), names),
        out_shape=tuple(jax.ShapeDtypeStruct(size, f32) for size, _ in outs.values()),
        in_specs=list(ins.values()),
        out_specs=tuple(space for _, space in outs.values()),
        scratch_shapes=list(scratch.values()),
        compiler_params=pltpu.CompilerParams(vmem_limit_bytes=40 << 20),
        name="widen_and_embed",
    )(*middle, emb_table, ada_weight)


HEADS = 6
LAYERS = 1

epsilon = 1e-06
highest = lax.Precision.HIGHEST
root_half = 0.7071067811865476
inverse_root_two_pi = 0.3989422804014327


def layer_norm(values):
    average = jnp.mean(values, axis=-1, keepdims=True)
    centred = values - average
    variance = jnp.mean(centred * centred, axis=-1, keepdims=True)
    inverse = lax.rsqrt(variance + epsilon)
    return (centred * inverse, inverse)


def norm_back(grad_normed, normed, inverse):
    first = jnp.mean(grad_normed, axis=-1, keepdims=True)
    second = jnp.mean(grad_normed * normed, axis=-1, keepdims=True)
    return inverse * (grad_normed - first - normed * second)


def gelu_exact(values):
    return 0.5 * values * (1.0 + jax.scipy.special.erf(values * root_half))


def gelu_slope(values):
    return 0.5 * (
        1.0 + jax.scipy.special.erf(values * root_half)
    ) + values * inverse_root_two_pi * jnp.exp(-0.5 * values * values)


def split_heads(values):
    return values.reshape(values.shape[0], values.shape[1], HEADS, values.shape[2] // HEADS)


def modulation_parts(silu_rows, ada_w, ada_b):
    mods = jnp.dot(silu_rows, ada_w.astype(jnp.float32), precision=highest) + ada_b.astype(
        jnp.float32
    )
    mods = mods.reshape(mods.shape[0], 6, -1)
    return [mods[:, index][:, None, :] for index in range(6)]


def before_attention(hidden, parts, qkv_low):
    normed, inverse = layer_norm(hidden)
    modulated = (normed * (1.0 + parts[1]) + parts[0]).astype(jnp.bfloat16)
    projected = jnp.einsum(
        "spd,df->spf", modulated, qkv_low, preferred_element_type=jnp.float32
    ).astype(jnp.bfloat16)
    width = hidden.shape[2]
    return (
        normed,
        inverse,
        modulated,
        projected[..., :width],
        projected[..., width : 2 * width],
        projected[..., 2 * width :],
    )


def after_attention(hidden, attended, parts, later):
    out_w, out_b, up_w, up_b, down_w, down_b = later
    branch = jnp.einsum(
        "spd,de->spe", attended, out_w, preferred_element_type=jnp.float32
    ) + out_b.astype(jnp.float32)
    middle = hidden + parts[2] * branch
    normed, inverse = layer_norm(middle)
    modulated = (normed * (1.0 + parts[4]) + parts[3]).astype(jnp.bfloat16)
    upward = jnp.einsum(
        "spd,df->spf", modulated, up_w, preferred_element_type=jnp.float32
    ) + up_b.astype(jnp.float32)
    activated = gelu_exact(upward).astype(jnp.bfloat16)
    feed = jnp.einsum(
        "spf,fd->spd", activated, down_w, preferred_element_type=jnp.float32
    ) + down_b.astype(jnp.float32)
    return (
        middle + parts[5] * feed,
        (branch, middle, normed, inverse, modulated, upward, activated, feed),
    )


def attention_forward(queries, keys_here, values_here):
    slots, rows, width = queries.shape
    scale = HEAD_DIM ** (-0.5)
    query_heads = split_heads(queries)
    running_max = jnp.full((slots, rows, HEADS), -1e30, jnp.float32)
    key_heads = split_heads(lax.all_gather(keys_here, "wide", axis=1, tiled=True))
    value_heads = split_heads(lax.all_gather(values_here, "wide", axis=1, tiled=True))
    scores = (
        jnp.einsum("sphe,snhe->sphn", query_heads, key_heads, preferred_element_type=jnp.float32)
        * scale
    )
    new_max = jnp.maximum(running_max, jnp.max(scores, axis=-1))
    weights = jnp.exp(scores - new_max[..., None])
    new_sum = jnp.sum(weights, axis=-1)
    mixed = jnp.einsum(
        "sphn,snhe->sphe",
        weights.astype(jnp.bfloat16),
        value_heads,
        preferred_element_type=jnp.float32,
    )
    total = mixed
    running_max, running_sum, total = (new_max, new_sum, total.reshape(slots, rows, width))
    attended = (
        (split_heads(total) / running_sum[..., None])
        .reshape(slots, rows, width)
        .astype(jnp.bfloat16)
    )
    return (attended, running_max + jnp.log(running_sum), None)


def attention_backward(queries, keys_here, values_here, grad_attended, log_total, delta):
    slots, rows, width = queries.shape
    scale = HEAD_DIM ** (-0.5)
    query_heads = split_heads(queries)
    grad_heads = split_heads(grad_attended)
    piece = (
        lax.all_gather(keys_here, "wide", axis=1, tiled=True),
        lax.all_gather(values_here, "wide", axis=1, tiled=True),
    )
    toward_key_heads = split_heads(piece[0])
    toward_value_heads = split_heads(piece[1])
    scores = (
        jnp.einsum(
            "sphe,snhe->sphn", query_heads, toward_key_heads, preferred_element_type=jnp.float32
        )
        * scale
    )
    probs = jnp.exp(scores - log_total[..., None])
    slope = jnp.einsum(
        "sphe,snhe->sphn", grad_heads, toward_value_heads, preferred_element_type=jnp.float32
    )
    grad_scores = (probs * (slope - delta[..., None])).astype(jnp.bfloat16)
    grad_queries = (
        jnp.einsum(
            "sphn,snhe->sphe", grad_scores, toward_key_heads, preferred_element_type=jnp.float32
        )
        * scale
    ).reshape(slots, rows, width)
    stats = (
        lax.all_gather(log_total, "wide", axis=1, tiled=True),
        lax.all_gather(delta, "wide", axis=1, tiled=True),
    )
    key_heads = split_heads(keys_here)
    value_heads = split_heads(values_here)
    piece = (
        lax.all_gather(queries, "wide", axis=1, tiled=True),
        lax.all_gather(grad_attended, "wide", axis=1, tiled=True),
    )
    piece_queries = split_heads(piece[0])
    piece_grads = split_heads(piece[1])
    piece_total = stats[0]
    piece_delta = stats[1]
    scores = (
        jnp.einsum("snhe,sphe->snhp", piece_queries, key_heads, preferred_element_type=jnp.float32)
        * scale
    )
    probs = jnp.exp(scores - piece_total[..., None])
    slope = jnp.einsum(
        "snhe,sphe->snhp", piece_grads, value_heads, preferred_element_type=jnp.float32
    )
    grad_scores = (probs * (slope - piece_delta[..., None])).astype(jnp.bfloat16)
    keys_total = (
        jnp.einsum(
            "snhp,snhe->sphe", grad_scores, piece_queries, preferred_element_type=jnp.float32
        )
        * scale
    ).reshape(slots, rows, width)
    values_total = jnp.einsum(
        "snhp,snhe->sphe",
        probs.astype(jnp.bfloat16),
        piece_grads,
        preferred_element_type=jnp.float32,
    ).reshape(slots, rows, width)
    return (
        grad_queries.astype(jnp.bfloat16),
        keys_total.astype(jnp.bfloat16),
        values_total.astype(jnp.bfloat16),
    )


def body(
    tokens,
    cotangent,
    emb_table,
    ada_weight,
    ada_bias,
    qkv_weight,
    out_weight,
    out_bias,
    up_weight,
    up_bias,
    down_weight,
    down_bias,
    lead_class,
    group_count,
):
    group = lax.axis_index("narrow")
    slot_count = tokens.shape[1]
    width = tokens.shape[3]
    table = emb_table.astype(jnp.float32)
    class_range = jnp.arange(table.shape[0], dtype=jnp.int32)
    classes_here = lax.dynamic_index_in_dim(lead_class, group, 0, keepdims=False)
    count_here = lax.dynamic_index_in_dim(group_count, group, 0, keepdims=False)
    live = (jnp.arange(slot_count, dtype=jnp.int32) < count_here).astype(jnp.float32)[:, None, None]
    embed_here = jnp.dot(
        (classes_here[:, None] == class_range[None, :]).astype(jnp.float32),
        table,
        precision=highest,
    )
    silu_here = embed_here * jax.nn.sigmoid(embed_here)
    hidden = tokens[0].astype(jnp.float32)
    layer = 0
    parts = modulation_parts(silu_here, ada_weight[layer], ada_bias[layer])
    later = (
        out_weight[layer],
        out_bias[layer],
        up_weight[layer],
        up_bias[layer],
        down_weight[layer],
        down_bias[layer],
    )
    normed, inverse, modulated, queries, keys_here, values_here = before_attention(
        hidden, parts, qkv_weight[layer]
    )
    attended, log_total, whole_pair = attention_forward(queries, keys_here, values_here)
    kept = [(hidden, parts, attended, log_total, whole_pair)]
    hidden, unused = after_attention(hidden, attended, parts, later)
    output = hidden * live
    grad = cotangent[0].astype(jnp.float32) * live
    grad_mods = [None] * LAYERS
    weight_grads = [None] * LAYERS
    for layer in reversed(range(LAYERS)):
        layer_input, parts, attended, log_total, whole_pair = kept[layer]
        later = (
            out_weight[layer],
            out_bias[layer],
            up_weight[layer],
            up_bias[layer],
            down_weight[layer],
            down_bias[layer],
        )
        normed, inverse, modulated, queries, keys_here, values_here = before_attention(
            layer_input, parts, qkv_weight[layer]
        )
        unused, inner = after_attention(layer_input, attended, parts, later)
        branch, middle, normed_mlp, inverse_mlp, modulated_mlp, upward, activated, feed = inner
        grad_feed = (grad * parts[5]).astype(jnp.bfloat16)
        grad_gate_mlp = jnp.sum(grad * feed, axis=1)
        grad_down_w = jnp.einsum(
            "spf,spd->fd", activated, grad_feed, preferred_element_type=jnp.float32
        )
        grad_down_b = jnp.sum(grad_feed.astype(jnp.float32), axis=(0, 1))
        grad_upward = (
            jnp.einsum(
                "spd,fd->spf", grad_feed, down_weight[layer], preferred_element_type=jnp.float32
            )
            * gelu_slope(upward)
        ).astype(jnp.bfloat16)
        grad_up_w = jnp.einsum(
            "spd,spf->df", modulated_mlp, grad_upward, preferred_element_type=jnp.float32
        )
        grad_up_b = jnp.sum(grad_upward.astype(jnp.float32), axis=(0, 1))
        grad_mod_mlp = jnp.einsum(
            "spf,df->spd", grad_upward, up_weight[layer], preferred_element_type=jnp.float32
        )
        grad_shift_mlp = jnp.sum(grad_mod_mlp, axis=1)
        grad_scale_mlp = jnp.sum(grad_mod_mlp * normed_mlp, axis=1)
        grad_middle = grad + norm_back(grad_mod_mlp * (1.0 + parts[4]), normed_mlp, inverse_mlp)
        grad_gate_attn = jnp.sum(grad_middle * branch, axis=1)
        grad_branch = (grad_middle * parts[2]).astype(jnp.bfloat16)
        grad_out_w = jnp.einsum(
            "spd,spe->de", attended, grad_branch, preferred_element_type=jnp.float32
        )
        grad_out_b = jnp.sum(grad_branch.astype(jnp.float32), axis=(0, 1))
        grad_attended = jnp.einsum(
            "spe,de->spd", grad_branch, out_weight[layer], preferred_element_type=jnp.float32
        ).astype(jnp.bfloat16)
        delta = jnp.sum(
            split_heads(grad_attended.astype(jnp.float32) * attended.astype(jnp.float32)), axis=-1
        )
        grad_queries, grad_keys, grad_values = attention_backward(
            queries, keys_here, values_here, grad_attended, log_total, delta
        )
        grad_projected = jnp.concatenate([grad_queries, grad_keys, grad_values], axis=-1)
        grad_qkv_w = jnp.einsum(
            "spd,spf->df", modulated, grad_projected, preferred_element_type=jnp.float32
        )
        grad_mod_attn = jnp.einsum(
            "spf,df->spd", grad_projected, qkv_weight[layer], preferred_element_type=jnp.float32
        )
        grad_shift_attn = jnp.sum(grad_mod_attn, axis=1)
        grad_scale_attn = jnp.sum(grad_mod_attn * normed, axis=1)
        grad = grad_middle + norm_back(grad_mod_attn * (1.0 + parts[1]), normed, inverse)
        local_mods = jnp.stack(
            [
                grad_shift_attn,
                grad_scale_attn,
                grad_gate_attn,
                grad_shift_mlp,
                grad_scale_mlp,
                grad_gate_mlp,
            ],
            axis=1,
        ).reshape(slot_count, 6 * width)
        grad_mods[layer] = lax.psum(local_mods, "wide")
        weight_grads[layer] = lax.psum(
            (grad_qkv_w, grad_out_w, grad_out_b, grad_up_w, grad_up_b, grad_down_w, grad_down_b),
            ("narrow", "wide"),
        )
    all_mods = lax.all_gather(
        jnp.stack(grad_mods, axis=0).astype(jnp.bfloat16), "narrow", axis=1, tiled=True
    ).astype(jnp.float32)
    all_classes = lead_class.reshape(-1)
    onehot_all = (all_classes[:, None] == class_range[None, :]).astype(jnp.float32)
    embed_all = jnp.dot(onehot_all, table, precision=highest)
    sigmoid_all = jax.nn.sigmoid(embed_all)
    silu_all = embed_all * sigmoid_all
    grad_ada_w = jnp.einsum("id,lie->lde", silu_all, all_mods, precision=highest)
    grad_ada_b = jnp.sum(all_mods, axis=1)
    grad_silu = jnp.einsum(
        "lie,lde->id", all_mods, ada_weight.astype(jnp.float32), precision=highest
    )
    grad_embed = grad_silu * (sigmoid_all + embed_all * sigmoid_all * (1.0 - sigmoid_all))
    grad_table = jnp.dot(onehot_all.T, grad_embed, precision=highest)
    stacked = [jnp.stack([weight_grads[0][member]], axis=0) for member in range(7)]
    return (
        output[None],
        grad[None],
        grad_table,
        grad_ada_w,
        grad_ada_b,
        stacked[0],
        stacked[1],
        stacked[2],
        stacked[3],
        stacked[4],
        stacked[5],
        stacked[6],
    )


def solution(mesh):
    in_specs = (
        P("narrow", None, "wide", None),
        P("narrow", None, "wide", None),
        P(),
        P(),
        P(),
        P(),
        P(),
        P(),
        P(),
        P(),
        P(),
        P(),
        P(),
        P(),
    )
    out_specs = (
        P("narrow", None, "wide", None),
        P("narrow", None, "wide", None),
        P(),
        P(),
        P(),
        P(),
        P(),
        P(),
        P(),
        P(),
        P(),
        P(),
    )
    by_item = dict(mesh.shape) == {"narrow": 4, "wide": 8}
    return jax.shard_map(fast_body if by_item else body, mesh=mesh, in_specs=in_specs, out_specs=out_specs, check_vma=False)
```
